32 devices in a mesh: seq: 8 (over z, core), fsdp: 4 (over y, x).
Axes of the slice: x: 2, y: 2, z: 4, core: 2. Of those that a mesh axis runs over, the one named last changes fastest.
Arguments:
- layer_input: bfloat16 [8, 512, 1152], P('fsdp', 'seq'), may hold values from -6 to 6
- document_numbers: int32 [8, 512], P('fsdp', 'seq'), may hold values from 0 to 14, as said below
- cotangent: bfloat16 [8, 512, 1152], P('fsdp', 'seq'), may hold values from -6 to 6
- shared_qkv_weight: bfloat16 [1152, 1536], P(('seq', 'fsdp')), may hold values from -0.1875 to 0.1875
- qkv_adapter_a: bfloat16 [1152, 768], P(('seq', 'fsdp')), may hold values from -0.1875 to 0.1875
- query_adapter_b: bfloat16 [256, 1024], P(('seq', 'fsdp')), may hold values from -0.375 to 0.375
- keyvalue_adapter_b: bfloat16 [2, 256, 256], P(None, ('seq', 'fsdp')), may hold values from -0.375 to 0.375
- shared_outproj_weight: bfloat16 [1024, 1152], P(('seq', 'fsdp')), may hold values from -0.75 to 0.75
- outproj_adapter_a: bfloat16 [1024, 256], P(('seq', 'fsdp')), may hold values from -0.75 to 0.75
- outproj_adapter_b: bfloat16 [256, 1152], P(('seq', 'fsdp')), may hold values from -0.375 to 0.375
- shared_gateup_weight: bfloat16 [1152, 13824], P(('seq', 'fsdp')), may hold values from -0.1875 to 0.1875
- gateup_adapter_a: bfloat16 [1152, 512], P(('seq', 'fsdp')), may hold values from -0.1875 to 0.1875
- gateup_adapter_b: bfloat16 [2, 256, 6912], P(None, ('seq', 'fsdp')), may hold values from -0.375 to 0.375
- shared_down_weight: bfloat16 [6912, 1152], P(('seq', 'fsdp')), may hold values from -0.078125 to 0.078125
- down_adapter_a: bfloat16 [6912, 256], P(('seq', 'fsdp')), may hold values from -0.078125 to 0.078125
- down_adapter_b: bfloat16 [256, 1152], P(('seq', 'fsdp')), may hold values from -0.375 to 0.375
- attention_norm_gain: bfloat16 [1152], P(('seq', 'fsdp')), may hold values from 0.099609375 to 1.8984375
- feedforward_norm_gain: bfloat16 [1152], P(('seq', 'fsdp')), may hold values from 0.099609375 to 1.8984375
Outputs:
- activations: bfloat16 [8, 512, 1152], P('fsdp', 'seq')
- grad_input: float32 [8, 512, 1152], P('fsdp', 'seq')
- grad_w_qkv: float32 [1152, 1536], P(('seq', 'fsdp'))
- qkv_adapter_a_gradient: float32 [1152, 768], P(('seq', 'fsdp'))
- query_adapter_b_gradient: float32 [256, 1024], P(('seq', 'fsdp'))
- keyvalue_adapter_b_gradient: float32 [2, 256, 256], P(None, ('seq', 'fsdp'))
- grad_w_out: float32 [1024, 1152], P(('seq', 'fsdp'))
- outproj_adapter_a_gradient: float32 [1024, 256], P(('seq', 'fsdp'))
- outproj_adapter_b_gradient: float32 [256, 1152], P(('seq', 'fsdp'))
- grad_w_gate_up: float32 [1152, 13824], P(('seq', 'fsdp'))
- gateup_adapter_a_gradient: float32 [1152, 512], P(('seq', 'fsdp'))
- gateup_adapter_b_gradient: float32 [2, 256, 6912], P(None, ('seq', 'fsdp'))
- grad_w_down: float32 [6912, 1152], P(('seq', 'fsdp'))
- down_adapter_a_gradient: float32 [6912, 256], P(('seq', 'fsdp'))
- down_adapter_b_gradient: float32 [256, 1152], P(('seq', 'fsdp'))
- grad_gain_attn: float32 [1152], P(('seq', 'fsdp'))
- grad_gain_ffn: float32 [1152], P(('seq', 'fsdp'))
The draws below stay inside these ranges and needn't reach their ends.
Inputs may be any that keep to these rules, and one draw needn't show every extreme that they name: `document_numbers`: along each row the ids never fall, and the tokens of one id are contiguous.
All inputs are finite; a program needn't handle non-finite values.
Results may differ from the reference program's by a relative error of at most 0.022.
Values may be sent and summed in bfloat16 or wider, within the bound.
A program may use at most 512 MiB of HBM per device.

```python
import math
import jax
import jax.numpy as jnp
from jax import lax

MODEL_WIDTH = 1152
QUERY_HEADS = 4
HEAD_SIZE = 256
HIDDEN_UNITS = 6912
ADAPTER_RANK = 256
SEG_DEV = 64
EXTRA = 6
ROWS = 8
ROW_LEN = 512


def draw_document_numbers(key, part):
    key = jax.random.fold_in(key, 7)
    key_start, key_finish, key_early, key_late, key_chosen = jax.random.split(key, 5)
    doc_start = jax.random.randint(key_start, (ROWS, 1), 1, SEG_DEV // 2 + 1)
    doc_finish = jax.random.randint(key_finish, (ROWS, 1), ROW_LEN - SEG_DEV // 2, ROW_LEN)
    early_cuts = 1 + jax.random.randint(key_early, (ROWS, EXTRA), 0, 1 << 20) % doc_start
    late_cuts = doc_finish + jax.random.randint(key_late, (ROWS, EXTRA), 0, 1 << 20) % (ROW_LEN - doc_finish)
    chosen = jax.random.randint(key_chosen, (ROWS, 2 * EXTRA), 0, 2)
    extra_cuts = jnp.where(chosen == 1, jnp.concatenate([early_cuts, late_cuts], axis=1), 0)
    all_cuts = jnp.concatenate([doc_start, doc_finish, extra_cuts], axis=1)
    places = jnp.arange(ROW_LEN)
    return jnp.sum((places[None, :, None] >= all_cuts[:, None, :]).astype(jnp.int32), axis=2).astype(jnp.int32)


def levels(key, dims, cuts, low, high):
    factor_of = 1.0
    for position, parts in cuts:
        heights = jax.random.uniform(jax.random.fold_in(jax.random.fold_in(key, 6), position), (parts,), jnp.float32, low / len(cuts), high / len(cuts))
        factor_of = factor_of * jnp.repeat(jnp.exp(heights), dims[position] // parts).reshape((-1,) + (1,) * (len(dims) - 1 - position))
    return factor_of


def centred(stream_key, shape, scale, bound, cuts=(), held_as=jnp.bfloat16):
    values = scale * jax.random.normal(stream_key, shape, jnp.float32)
    if cuts:
        values = values * levels(stream_key, shape, cuts, -0.22, 0.18)
    return jnp.clip(values, -bound, bound).astype(held_as)


def setup_inputs(seed: int = 0) -> dict:
    splits = jax.random.split(jax.random.key(seed), 19)
    layer_input = centred(splits[0], (ROWS, ROW_LEN, MODEL_WIDTH), 1.0, 6.0, ((0, 4), (1, 8)))
    document_numbers = draw_document_numbers(jax.random.fold_in(splits[18], 71), 0)
    cotangent = centred(splits[2], (ROWS, ROW_LEN, MODEL_WIDTH), 1.0, 6.0, ((0, 4), (1, 8)))
    shared_qkv_weight = centred(splits[3], (MODEL_WIDTH, (QUERY_HEADS + 2) * HEAD_SIZE), MODEL_WIDTH ** -0.5, 0.1875, ((0, 32),))
    qkv_adapter_a = centred(splits[4], (MODEL_WIDTH, 3 * ADAPTER_RANK), MODEL_WIDTH ** -0.5, 0.1875, ((0, 32),))
    query_adapter_b = centred(splits[5], (ADAPTER_RANK, QUERY_HEADS * HEAD_SIZE), ADAPTER_RANK ** -0.5, 0.375, ((0, 32),))
    keyvalue_adapter_b = centred(splits[6], (2, ADAPTER_RANK, HEAD_SIZE), ADAPTER_RANK ** -0.5, 0.375, ((1, 32),))
    shared_outproj_weight = centred(splits[7], (QUERY_HEADS * HEAD_SIZE, MODEL_WIDTH), (QUERY_HEADS * HEAD_SIZE // 16) ** -0.5, 0.75, ((0, 32),))
    outproj_adapter_a = centred(splits[8], (QUERY_HEADS * HEAD_SIZE, ADAPTER_RANK), (QUERY_HEADS * HEAD_SIZE // 16) ** -0.5, 0.75, ((0, 32),))
    outproj_adapter_b = centred(splits[9], (ADAPTER_RANK, MODEL_WIDTH), ADAPTER_RANK ** -0.5, 0.375, ((0, 32),))
    shared_gateup_weight = centred(splits[10], (MODEL_WIDTH, 2 * HIDDEN_UNITS), MODEL_WIDTH ** -0.5, 0.1875, ((0, 32),))
    gateup_adapter_a = centred(splits[11], (MODEL_WIDTH, 2 * ADAPTER_RANK), MODEL_WIDTH ** -0.5, 0.1875, ((0, 32),))
    gateup_adapter_b = centred(splits[12], (2, ADAPTER_RANK, HIDDEN_UNITS), ADAPTER_RANK ** -0.5, 0.375, ((1, 32),))
    shared_down_weight = centred(splits[13], (HIDDEN_UNITS, MODEL_WIDTH), HIDDEN_UNITS ** -0.5, 0.078125, ((0, 32),))
    down_adapter_a = centred(splits[14], (HIDDEN_UNITS, ADAPTER_RANK), HIDDEN_UNITS ** -0.5, 0.078125, ((0, 32),))
    down_adapter_b = centred(splits[15], (ADAPTER_RANK, MODEL_WIDTH), ADAPTER_RANK ** -0.5, 0.375, ((0, 32),))
    attention_norm_gain = jnp.clip(1.0 + 0.18 * jax.random.normal(splits[16], (MODEL_WIDTH,), jnp.float32), 0.099609375, 1.8984375).astype(jnp.bfloat16)
    feedforward_norm_gain = jnp.clip(1.0 + 0.18 * jax.random.normal(splits[17], (MODEL_WIDTH,), jnp.float32), 0.099609375, 1.8984375).astype(jnp.bfloat16)
    return dict(layer_input=layer_input, document_numbers=document_numbers, cotangent=cotangent, shared_qkv_weight=shared_qkv_weight, qkv_adapter_a=qkv_adapter_a, query_adapter_b=query_adapter_b, keyvalue_adapter_b=keyvalue_adapter_b, shared_outproj_weight=shared_outproj_weight, outproj_adapter_a=outproj_adapter_a, outproj_adapter_b=outproj_adapter_b, shared_gateup_weight=shared_gateup_weight, gateup_adapter_a=gateup_adapter_a, gateup_adapter_b=gateup_adapter_b, shared_down_weight=shared_down_weight, down_adapter_a=down_adapter_a, down_adapter_b=down_adapter_b, attention_norm_gain=attention_norm_gain, feedforward_norm_gain=feedforward_norm_gain)


EPSILON = 1e-06
ROPE_BASE = 10000.0
MASKED = -1e+30

@jax.custom_vjp
def lowrank_value(v):
    return lax.optimization_barrier(v.astype(jnp.bfloat16)).astype(jnp.float32)

@jax.custom_vjp
def lowrank_backward(v):
    return v

def low_keep(v):
    return (lowrank_value(v), None)

def low_pass(kept, grad):
    return (grad,)

def back_keep(v):
    return (v, None)

def back_low(kept, grad):
    return (lowrank_value(grad),)
lowrank_value.defvjp(low_keep, low_pass)
lowrank_backward.defvjp(back_keep, back_low)

def precise_matrix_product(left, right):
    return jnp.dot(left, right, precision=lax.Precision.HIGHEST)

def norm_apply(hidden, gain):
    return hidden * lax.rsqrt(lax.optimization_barrier(jnp.mean(hidden * hidden, axis=-1, keepdims=True)) + EPSILON) * gain

def rope_tables(positions):
    half_dim = HEAD_SIZE // 2
    spacing = jnp.exp(-(2.0 * jnp.arange(half_dim).astype(jnp.float32) / HEAD_SIZE) * math.log(ROPE_BASE))
    angle = positions.astype(jnp.float32)[..., None] * spacing
    return (jnp.cos(angle), jnp.sin(angle))

def rotate(values, cosine, sine_part):
    half_dim = values.shape[-1] // 2
    first = values[..., :half_dim]
    second = values[..., half_dim:]
    return jnp.concatenate([first * cosine - second * sine_part, second * cosine + first * sine_part], axis=-1)

def layer_row(row_in, row_ids, weight_bundle):
    shared_qkv_weight, qkv_adapter_a, query_adapter_b, keyvalue_adapter_b, shared_outproj_weight, outproj_adapter_a, outproj_adapter_b, shared_gateup_weight, gateup_adapter_a, gateup_adapter_b, shared_down_weight, down_adapter_a, down_adapter_b, attention_norm_gain, feedforward_norm_gain = weight_bundle
    length = row_in.shape[0]
    places = jnp.arange(length).astype(jnp.int32)
    same_doc = row_ids[:, None] == row_ids[None, :]
    positions = lax.optimization_barrier(jnp.sum((same_doc & (places[None, :] < places[:, None])).astype(jnp.int32), axis=1))
    allowed = same_doc & (places[None, :] <= places[:, None])
    cosine, sine_part = rope_tables(positions)
    first_norm_output = lowrank_value(norm_apply(row_in, attention_norm_gain))
    qkv_update = lowrank_backward(lowrank_value(precise_matrix_product(first_norm_output, qkv_adapter_a)))
    projection_output = precise_matrix_product(first_norm_output, shared_qkv_weight) + jnp.concatenate([precise_matrix_product(qkv_update[:, :ADAPTER_RANK], query_adapter_b), precise_matrix_product(qkv_update[:, ADAPTER_RANK:2 * ADAPTER_RANK], keyvalue_adapter_b[0]), precise_matrix_product(qkv_update[:, 2 * ADAPTER_RANK:], keyvalue_adapter_b[1])], axis=1)
    projection_output = lowrank_backward(projection_output)
    queries = projection_output[:, :QUERY_HEADS * HEAD_SIZE].reshape(length, QUERY_HEADS, HEAD_SIZE)
    queries = lowrank_value(rotate(queries, cosine[:, None, :], sine_part[:, None, :]))
    keys = lowrank_value(rotate(projection_output[:, QUERY_HEADS * HEAD_SIZE:(QUERY_HEADS + 1) * HEAD_SIZE], cosine, sine_part))
    values = lowrank_value(projection_output[:, (QUERY_HEADS + 1) * HEAD_SIZE:])
    scale = HEAD_SIZE ** (-0.5)

    def head_out(query_head):
        scores = lowrank_backward(precise_matrix_product(query_head, keys.T) * scale)
        probs = lowrank_value(jax.nn.softmax(jnp.where(allowed, scores, MASKED), axis=-1))
        return precise_matrix_product(probs, values)
    heads = lax.map(jax.checkpoint(head_out), jnp.transpose(queries, (1, 0, 2)))
    mixed_heads = lowrank_backward(lowrank_value(jnp.transpose(heads, (1, 0, 2)).reshape(length, QUERY_HEADS * HEAD_SIZE)))
    outproj_update = lowrank_backward(lowrank_value(precise_matrix_product(mixed_heads, outproj_adapter_a)))
    attention_output = lowrank_backward(precise_matrix_product(mixed_heads, shared_outproj_weight) + precise_matrix_product(outproj_update, outproj_adapter_b))
    first_residual = row_in + attention_output
    second_norm_output = lowrank_value(norm_apply(first_residual, feedforward_norm_gain))
    gateup_update = lowrank_backward(lowrank_value(precise_matrix_product(second_norm_output, gateup_adapter_a)))
    gate_up_output = precise_matrix_product(second_norm_output, shared_gateup_weight) + jnp.concatenate([precise_matrix_product(gateup_update[:, :ADAPTER_RANK], gateup_adapter_b[0]), precise_matrix_product(gateup_update[:, ADAPTER_RANK:], gateup_adapter_b[1])], axis=1)
    gate_up_output = lowrank_backward(gate_up_output)
    activation_value = lowrank_value(jax.nn.gelu(gate_up_output[:, :HIDDEN_UNITS], approximate=True) * gate_up_output[:, HIDDEN_UNITS:])
    down_update = lowrank_backward(lowrank_value(precise_matrix_product(activation_value, down_adapter_a)))
    return first_residual + precise_matrix_product(activation_value, shared_down_weight) + precise_matrix_product(down_update, down_adapter_b)

def reference(layer_input, document_numbers, cotangent, shared_qkv_weight, qkv_adapter_a, query_adapter_b, keyvalue_adapter_b, shared_outproj_weight, outproj_adapter_a, outproj_adapter_b, shared_gateup_weight, gateup_adapter_a, gateup_adapter_b, shared_down_weight, down_adapter_a, down_adapter_b, attention_norm_gain, feedforward_norm_gain):
    weight_bundle = tuple((element_entry.astype(jnp.float32) for element_entry in (shared_qkv_weight, qkv_adapter_a, query_adapter_b, keyvalue_adapter_b, shared_outproj_weight, outproj_adapter_a, outproj_adapter_b, shared_gateup_weight, gateup_adapter_a, gateup_adapter_b, shared_down_weight, down_adapter_a, down_adapter_b, attention_norm_gain, feedforward_norm_gain)))

    def step(totals, element_entry):
        row_in, row_ids, row_cot = element_entry
        result, pull = jax.vjp(lambda inner, params: layer_row(inner, row_ids, params), row_in.astype(jnp.float32), weight_bundle)
        grad_row, grad_params = pull(row_cot.astype(jnp.float32))
        totals = jax.tree.map(lambda left, right: left + right, totals, grad_params)
        return (totals, (result.astype(jnp.bfloat16), grad_row))
    zeros = jax.tree.map(jnp.zeros_like, weight_bundle)
    totals, outputs = lax.scan(step, zeros, (layer_input, document_numbers, cotangent))
    activations, grad_input = outputs
    g_qkv, g_qkv_a, g_q_b, g_kv_b, g_out, g_out_a, g_out_b, g_gate_up, g_gu_a, g_gu_b, g_down, g_down_a, g_down_b, g_gain_attn, g_gain_ffn = totals
    return (activations, grad_input, g_qkv, g_qkv_a, g_q_b, g_kv_b, g_out, g_out_a, g_out_b, g_gate_up, g_gu_a, g_gu_b, g_down, g_down_a, g_down_b, g_gain_attn, g_gain_ffn)
```

```python
import functools
import math

import jax
import jax.numpy as jnp
from jax import lax
from jax.experimental import pallas as pl
from jax.experimental.pallas import tpu as pltpu
from jax.sharding import PartitionSpec as P

HEADS = 4
HEAD = 256
RANK = 256
EPSILON = 1e-06
ROPE_BASE = 10000.0
MASKED = -1e30
MESH = pl.DeviceIdType.MESH
BF = jnp.bfloat16
F32 = jnp.float32


def mm(left, right):
    return jnp.dot(left, right, preferred_element_type=F32)


def mm_tn(left, right):
    return lax.dot_general(left, right, (((0,), (0,)), ((), ())), preferred_element_type=F32)


def mm_nt(left, right):
    return lax.dot_general(left, right, (((1,), (1,)), ((), ())), preferred_element_type=F32)


def greet(peers):
    barrier = pltpu.get_barrier_semaphore()
    for peer in peers:
        pl.semaphore_signal(barrier, inc=1, device_id=peer, device_id_type=MESH)
    pl.semaphore_wait(barrier, len(peers))


def exchange_kernel(axis, size, count, *refs):
    xs, os = refs[:count], refs[count : 2 * count]
    local, send, recv = refs[2 * count :]
    me = lax.axis_index(axis)
    greet([{axis: lax.rem(me + k, size)} for k in range(1, size)])
    copies = []
    for k in range(1, size):
        peer = lax.rem(me + k, size)
        for a in range(count):
            copy = pltpu.make_async_remote_copy(
                src_ref=xs[a].at[peer],
                dst_ref=os[a].at[me],
                send_sem=send.at[a, k],
                recv_sem=recv.at[a, k],
                device_id={axis: peer},
                device_id_type=MESH,
            )
            copy.start()
            copies.append(copy)
    for a in range(count):
        copy = pltpu.make_async_copy(xs[a].at[me], os[a].at[me], local.at[a])
        copy.start()
        copies.append(copy)
    for copy in copies:
        copy.wait()


def exchange(arrays, axis, size, collective_id):
    count = len(arrays)
    any_spec = pl.BlockSpec(memory_space=pl.ANY)
    return pl.pallas_call(
        functools.partial(exchange_kernel, axis, size, count),
        out_shape=[jax.ShapeDtypeStruct(a.shape, a.dtype) for a in arrays],
        in_specs=[any_spec] * count,
        out_specs=[any_spec] * count,
        scratch_shapes=[
            pltpu.SemaphoreType.DMA((count,)),
            pltpu.SemaphoreType.DMA((count, size)),
            pltpu.SemaphoreType.DMA((count, size)),
        ],
        compiler_params=pltpu.CompilerParams(collective_id=collective_id, has_side_effects=True),
    )(*arrays)


def spread_kernel(axis, size, count, *refs):
    xs, os = refs[:count], refs[count : 2 * count]
    local, send, recv = refs[2 * count :]
    me = lax.axis_index(axis)
    greet([{axis: lax.rem(me + k, size)} for k in range(1, size)])
    copies = []
    for k in range(1, size):
        peer = lax.rem(me + k, size)
        for a in range(count):
            copy = pltpu.make_async_remote_copy(
                src_ref=xs[a],
                dst_ref=os[a].at[me],
                send_sem=send.at[a, k],
                recv_sem=recv.at[a, k],
                device_id={axis: peer},
                device_id_type=MESH,
            )
            copy.start()
            copies.append(copy)
    for a in range(count):
        copy = pltpu.make_async_copy(xs[a], os[a].at[me], local.at[a])
        copy.start()
        copies.append(copy)
    for copy in copies:
        copy.wait()


def spread(arrays, axis, size, collective_id):
    count = len(arrays)
    any_spec = pl.BlockSpec(memory_space=pl.ANY)
    return pl.pallas_call(
        functools.partial(spread_kernel, axis, size, count),
        out_shape=[jax.ShapeDtypeStruct((size,) + a.shape, a.dtype) for a in arrays],
        in_specs=[any_spec] * count,
        out_specs=[any_spec] * count,
        scratch_shapes=[
            pltpu.SemaphoreType.DMA((count,)),
            pltpu.SemaphoreType.DMA((count, size)),
            pltpu.SemaphoreType.DMA((count, size)),
        ],
        compiler_params=pltpu.CompilerParams(collective_id=collective_id, has_side_effects=True),
    )(*arrays)


def line_gather_kernel(line, count, *refs):
    xs, os = refs[:count], refs[count : 2 * count]
    local, send, recv = refs[2 * count :]
    s = lax.axis_index("seq")
    base = s // line * line
    n2 = line // 2
    i = s - base
    p, core = i // 2, lax.rem(i, 2)
    sib = s + 1 - 2 * core
    left = base + lax.rem(i + line - 2, line)
    right = base + lax.rem(i + 2, line)
    greet([{"seq": d} for d in ([left, right, sib] if n2 > 2 else [right, sib])])

    def copy(a, blk, src, dst, k):
        return pltpu.make_async_remote_copy(
            src_ref=src,
            dst_ref=os[a].at[blk],
            send_sem=send.at[a, k],
            recv_sem=recv.at[a, blk],
            device_id={"seq": dst},
            device_id_type=MESH,
        )

    for a in range(count):

        @pl.when(p < n2 - 1)
        def _(a=a):
            copy(a, i, xs[a], right, 0).start()

        @pl.when(p > 0)
        def _(a=a):
            copy(a, i, xs[a], left, 1).start()

        copy(a, i, xs[a], sib, 2).start()
        pltpu.make_async_copy(xs[a], os[a].at[i], local.at[a]).start()
    for d in range(1, n2):
        for a in range(count):

            @pl.when(p - d >= 0)
            def _(a=a, d=d):
                blk = i - 2 * d
                copy(a, blk, os[a].at[blk], left, 0).wait_recv()

                @pl.when(p < n2 - 1)
                def _():
                    copy(a, blk, os[a].at[blk], right, 4 * d).start()

                copy(a, blk, os[a].at[blk], sib, 4 * d + 1).start()

            @pl.when(p + d < n2)
            def _(a=a, d=d):
                blk = i + 2 * d
                copy(a, blk, os[a].at[blk], right, 0).wait_recv()

                @pl.when(p > 0)
                def _():
                    copy(a, blk, os[a].at[blk], left, 4 * d + 2).start()

                copy(a, blk, os[a].at[blk], sib, 4 * d + 3).start()

    for a in range(count):
        for q in range(n2):
            blk = 2 * q + 1 - core
            copy(a, blk, os[a].at[blk], sib, 0).wait_recv()

        def sent(k, a=a):
            copy(a, i, xs[a], sib, k).wait_send()

        @pl.when(p < n2 - 1)
        def _():
            sent(0)

        @pl.when(p > 0)
        def _():
            sent(1)

        sent(2)
        for d in range(1, n2):

            @pl.when(p - d >= 0)
            def _(d=d):
                @pl.when(p < n2 - 1)
                def _():
                    sent(4 * d)

                sent(4 * d + 1)

            @pl.when(p + d < n2)
            def _(d=d):
                @pl.when(p > 0)
                def _():
                    sent(4 * d + 2)

                sent(4 * d + 3)

        pltpu.make_async_copy(xs[a], os[a].at[i], local.at[a]).wait()


def line_gather(arrays, line, collective_id):
    count = len(arrays)
    any_spec = pl.BlockSpec(memory_space=pl.ANY)
    return pl.pallas_call(
        functools.partial(line_gather_kernel, line, count),
        out_shape=[jax.ShapeDtypeStruct((line,) + a.shape, a.dtype) for a in arrays],
        in_specs=[any_spec] * count,
        out_specs=[any_spec] * count,
        scratch_shapes=[
            pltpu.SemaphoreType.DMA((count,)),
            pltpu.SemaphoreType.DMA((count, 2 * line)),
            pltpu.SemaphoreType.DMA((count, line)),
        ],
        compiler_params=pltpu.CompilerParams(collective_id=collective_id, has_side_effects=True),
    )(*arrays)


def line_sum_kernel(line, x_ref, o_ref, mine, from_sib, from_left, from_right, send, recv):
    s = lax.axis_index("seq")
    base = s // line * line
    n2 = line // 2
    i = s - base
    p, core = i // 2, lax.rem(i, 2)
    sib = s + 1 - 2 * core
    left = base + lax.rem(i + line - 2, line)
    right = base + lax.rem(i + 2, line)
    greet([{"seq": d} for d in ([left, right, sib] if n2 > 2 else [right, sib])])

    def hand_over(q):
        return pltpu.make_async_remote_copy(
            src_ref=x_ref.at[2 * q + 1 - core],
            dst_ref=from_sib.at[q],
            send_sem=send.at[q],
            recv_sem=recv.at[q],
            device_id={"seq": sib},
            device_id_type=MESH,
        )

    def rightward(q):
        return pltpu.make_async_remote_copy(
            src_ref=mine.at[q],
            dst_ref=from_left.at[q],
            send_sem=send.at[n2 + q],
            recv_sem=recv.at[n2 + q],
            device_id={"seq": right},
            device_id_type=MESH,
        )

    def leftward(q):
        return pltpu.make_async_remote_copy(
            src_ref=mine.at[q],
            dst_ref=from_right.at[q],
            send_sem=send.at[2 * n2 + q],
            recv_sem=recv.at[2 * n2 + q],
            device_id={"seq": left},
            device_id_type=MESH,
        )

    order = [q for k in range(n2) for q in ((n2 - 1 - k, k) if n2 - 1 - k > k else (k,) if n2 - 1 - k == k else ())]
    for q in order:
        hand_over(q).start()

    def add(q, other):
        mine[q] = (mine[q].astype(F32) + other[q].astype(F32)).astype(BF)

    for q in order:
        hand_over(q).wait_recv()
        mine[q] = (x_ref[2 * q + core].astype(F32) + from_sib[q].astype(F32)).astype(BF)

        @pl.when((q > p) & (p == 0))
        def _(q=q):
            rightward(q).start()

        @pl.when((q < p) & (p == n2 - 1))
        def _(q=q):
            leftward(q).start()

    for k in range(n2 - 1):
        q = n2 - 1 - k

        @pl.when((p > 0) & (p < q))
        def _(q=q):
            rightward(q).wait_recv()
            add(q, from_left)
            rightward(q).start()

        q = k

        @pl.when((p < n2 - 1) & (p > q))
        def _(q=q):
            leftward(q).wait_recv()
            add(q, from_right)
            leftward(q).start()

    for q in range(n2):

        @pl.when((p == q) & (p > 0))
        def _(q=q):
            rightward(q).wait_recv()

        @pl.when((p == q) & (p < n2 - 1))
        def _(q=q):
            leftward(q).wait_recv()

        @pl.when(p == q)
        def _(q=q):
            total = mine[q].astype(F32)
            if q > 0:
                total += from_left[q].astype(F32)
            if q < n2 - 1:
                total += from_right[q].astype(F32)
            o_ref[...] = total

    for q in range(n2):
        hand_over(q).wait_send()

        @pl.when(q > p)
        def _(q=q):
            rightward(q).wait_send()

        @pl.when(q < p)
        def _(q=q):
            leftward(q).wait_send()


def line_sum(x, line, collective_id):
    blk = x.shape[1:]
    vmem = pl.BlockSpec(memory_space=pltpu.VMEM)
    n2 = line // 2
    return pl.pallas_call(
        functools.partial(line_sum_kernel, line),
        out_shape=jax.ShapeDtypeStruct(blk, F32),
        in_specs=[vmem],
        out_specs=vmem,
        scratch_shapes=[pltpu.VMEM((n2,) + blk, BF)] * 4
        + [pltpu.SemaphoreType.DMA((3 * n2,)), pltpu.SemaphoreType.DMA((3 * n2,))],
        compiler_params=pltpu.CompilerParams(
            collective_id=collective_id, has_side_effects=True, vmem_limit_bytes=48 << 20
        ),
    )(x)


def norm_apply(hidden, gain):
    return hidden * lax.rsqrt(jnp.mean(hidden * hidden, axis=-1, keepdims=True) + EPSILON) * gain


def rope_tables(positions):
    half = HEAD // 2
    spacing = jnp.exp(-(2.0 * jnp.arange(half).astype(F32) / HEAD) * math.log(ROPE_BASE))
    angle = positions.astype(F32)[..., None] * spacing
    return jnp.cos(angle), jnp.sin(angle)


def rotate(values, cosine, sine):
    half = values.shape[-1] // 2
    a, b = values[..., :half], values[..., half:]
    return jnp.concatenate([a * cosine - b * sine, b * cosine + a * sine], axis=-1)


def unrotate(grads, cosine, sine):
    half = grads.shape[-1] // 2
    a, b = grads[..., :half], grads[..., half:]
    return jnp.concatenate([a * cosine + b * sine, b * cosine - a * sine], axis=-1)


def shards(
    S,
    F,
    layer_input,
    document_numbers,
    cotangent,
    w_qkv,
    qkv_a,
    q_b,
    kv_b,
    w_out,
    out_a,
    out_b,
    w_gu,
    gu_a,
    gu_b,
    w_down,
    down_a,
    down_b,
    gain_a,
    gain_f,
):
    R, seg, width = layer_input.shape
    L = seg * S
    own = R * seg
    G = S // R
    C = G // HEADS
    scale = HEAD**-0.5
    kb = w_qkv.shape[0]
    rb = q_b.shape[0]
    hb = w_down.shape[0]
    ob = w_out.shape[0]
    hidden = w_gu.shape[1] // 2
    hl = hidden // S
    s = lax.axis_index("seq")
    r = s // G
    head = lax.rem(s, G) // C
    chunk = lax.rem(s, C)
    qlen = L // C

    gains = jnp.pad(jnp.stack([gain_a, gain_f], axis=1), ((0, 0), (0, 126)))
    pack1 = jnp.concatenate([w_qkv, qkv_a, gu_a, gains], axis=1)
    pack2 = jnp.concatenate([q_b, kv_b[0], kv_b[1], out_b, down_b], axis=1)
    pack3 = jnp.concatenate([w_out, out_a], axis=1)
    p1, p2, p3 = spread([pack1, pack2, pack3], "fsdp", F, 0)
    ids = jnp.pad(document_numbers[:, None, :], ((0, 0), (0, 7), (0, 128 - seg)))
    p1, p2, p3, xin, cot, ids = line_gather([p1, p2, p3, layer_input, cotangent, ids], S, 1)
    p1 = p1.reshape(width, -1)
    p2 = p2.reshape(RANK, -1)
    p3 = p3.reshape(HEADS, HEAD, -1)
    xrow = lax.dynamic_index_in_dim(xin, r, 1, keepdims=False).reshape(L, width).astype(F32)
    cot = cot.transpose(1, 0, 2, 3).reshape(R * L, width)
    ids = lax.dynamic_index_in_dim(ids[:, :, 0, :seg], r, 1, keepdims=False).reshape(L)

    gw = jnp.concatenate(
        [w_gu[:, :hidden].reshape(kb, S, hl), w_gu[:, hidden:].reshape(kb, S, hl)], axis=2
    ).transpose(1, 0, 2)
    gb = jnp.concatenate([gu_b[0].reshape(rb, S, hl), gu_b[1].reshape(rb, S, hl)], axis=2).transpose(
        1, 0, 2
    )
    gw, gb = exchange([gw, gb], "seq", S, 2)
    dw = jnp.concatenate([w_down, down_a], axis=1)
    gw, gb, dw = spread([gw, gb, dw], "fsdp", F, 3)
    gw = gw.transpose(1, 0, 2, 3).reshape(width, 2 * hl)
    gb = gb.transpose(1, 0, 2, 3).reshape(RANK, 2 * hl)
    dw = dw.reshape(hl, -1)

    q0 = HEADS * HEAD
    wq = lax.dynamic_slice_in_dim(p1, head * HEAD, HEAD, 1)
    w1 = jnp.concatenate([wq, p1[:, q0 : q0 + 2 * HEAD + 3 * RANK]], axis=1)
    at = q0 + 2 * HEAD + 3 * RANK
    f_gu_a = p1[:, at : at + 2 * RANK]
    gain_one = p1[:, at + 2 * RANK].astype(F32)
    gain_two = p1[:, at + 2 * RANK + 1].astype(F32)
    f_q_b = lax.dynamic_slice_in_dim(p2, head * HEAD, HEAD, 1)
    f_k_b = p2[:, q0 : q0 + HEAD]
    f_v_b = p2[:, q0 + HEAD : q0 + 2 * HEAD]
    f_out_b = p2[:, q0 + 2 * HEAD : q0 + 2 * HEAD + width]
    f_down_b = p2[:, q0 + 2 * HEAD + width :]
    wo = lax.dynamic_index_in_dim(p3, head, 0, keepdims=False)

    place = jnp.arange(L, dtype=jnp.int32)
    same = ids[:, None] == ids[None, :]
    before = place[None, :] < place[:, None]
    positions = jnp.sum((same & before).astype(jnp.int32), axis=1)
    allowed = same & (place[None, :] <= place[:, None])
    cosine, sine = rope_tables(positions)
    norm_one = norm_apply(xrow, gain_one).astype(BF)
    pu = mm(norm_one, w1)
    u = pu[:, 3 * HEAD :].astype(BF)
    u_q, u_k, u_v = u[:, :RANK], u[:, RANK : 2 * RANK], u[:, 2 * RANK :]
    query = rotate(pu[:, :HEAD] + mm(u_q, f_q_b), cosine, sine).astype(BF)
    key = rotate(pu[:, HEAD : 2 * HEAD] + mm(u_k, f_k_b), cosine, sine).astype(BF)
    value = (pu[:, 2 * HEAD : 3 * HEAD] + mm(u_v, f_v_b)).astype(BF)
    if C > 1:
        query_c = lax.dynamic_slice_in_dim(query, chunk * qlen, qlen, 0)
        allowed = lax.dynamic_slice_in_dim(allowed, chunk * qlen, qlen, 0)
    else:
        query_c = query
    scores = jnp.where(allowed, mm_nt(query_c, key) * scale, MASKED)
    top = jnp.max(scores, axis=-1, keepdims=True)
    lse = top + jnp.log(jnp.sum(jnp.exp(scores - top), axis=-1, keepdims=True))
    probs = jnp.where(allowed, jnp.exp(scores - lse), 0.0)
    probs_low = probs.astype(BF)
    mixed = mm(probs_low, value).astype(BF)
    part = mm(mixed, wo).astype(BF)
    if C > 1:
        part = lax.dynamic_update_slice_in_dim(jnp.zeros((L, part.shape[1]), BF), part, chunk * qlen, 0)
    attn = line_sum(part.reshape(G, own, -1), G, 4)
    u_out = attn[:, width:].astype(BF)
    mine = lax.rem(s, G) * own
    x_own = lax.dynamic_slice_in_dim(xrow, mine, own, 0)
    resid = x_own + attn[:, :width] + mm(u_out, f_out_b)
    norm_two_own = norm_apply(resid, gain_two).astype(BF)
    (norm_two,) = line_gather([norm_two_own], S, 5)
    norm_two = norm_two.reshape(R * L, width)

    u_gu = mm(norm_two, f_gu_a).astype(BF)
    gu = mm(norm_two, gw)
    gate = gu[:, :hl] + mm(u_gu[:, :RANK], gb[:, :hl])
    up = gu[:, hl:] + mm(u_gu[:, RANK:], gb[:, hl:])
    d_u_down = mm_nt(cot, f_down_b).astype(BF)
    cot_u = jnp.concatenate([cot, d_u_down], axis=1)
    d_act = mm_nt(cot_u, dw)
    inner = math.sqrt(2.0 / math.pi)
    th = jnp.tanh(inner * (gate + 0.044715 * gate * gate * gate))
    gelu = 0.5 * gate * (1.0 + th)
    act = (gelu * up).astype(BF)
    slope = 0.5 * (1.0 + th) + 0.5 * gate * (1.0 - th * th) * inner * (1.0 + 3 * 0.044715 * gate * gate)
    d_gate = (d_act * up * slope).astype(BF)
    d_up = (d_act * gelu).astype(BF)
    d_gu = jnp.concatenate([d_gate, d_up], axis=1)
    d_u_gu = jnp.concatenate(
        [mm_nt(d_gate, gb[:, :hl]), mm_nt(d_up, gb[:, hl:])], axis=1
    ).astype(BF)
    d_norm_two = (mm_nt(d_gu, gw) + mm_nt(d_u_gu, f_gu_a)).astype(BF)
    d_norm_two = line_sum(d_norm_two.reshape(S, own, width), S, 6)
    ffn = mm(act, dw)
    u_down = ffn[:, width:].astype(BF)
    ffn = (ffn[:, :width] + mm(u_down, f_down_b)).astype(BF)
    ffn = line_sum(ffn.reshape(S, own, width), S, 7)
    activations = (resid + ffn).astype(BF)
    g_down = mm_tn(act, cot_u)
    g_down_b = mm_tn(u_down, cot)
    g_gu = mm_tn(norm_two, d_gu)
    g_gu_b = jnp.concatenate([mm_tn(u_gu[:, :RANK], d_gate), mm_tn(u_gu[:, RANK:], d_up)], axis=1)
    g_gu_a = mm_tn(norm_two, d_u_gu)

    def norm_back(G_in, h, g):
        q = lax.rsqrt(jnp.mean(h * h, axis=-1, keepdims=True) + EPSILON)
        gg = G_in * g
        d_gain = jnp.sum(G_in * (h * q), axis=0)
        return d_gain, q * gg - h * (q * q * q) * jnp.mean(gg * h, axis=-1, keepdims=True)

    d_gain_two, back = norm_back(d_norm_two, resid, gain_two)
    cot_own = lax.dynamic_slice_in_dim(cot, s * own, own, 0)
    d_resid = cot_own.astype(F32) + back

    d_attn_own = d_resid.astype(BF)
    (d_attn,) = line_gather([d_attn_own], G, 8)
    d_attn = d_attn.reshape(L, width)
    g_out_b = mm_tn(u_out, d_attn_own)
    if C > 1:
        d_attn = lax.dynamic_slice_in_dim(d_attn, chunk * qlen, qlen, 0)
    d_u_out = mm_nt(d_attn, f_out_b).astype(BF)
    d_attn_u = jnp.concatenate([d_attn, d_u_out], axis=1)
    d_mixed = mm_nt(d_attn_u, wo).astype(BF)
    g_out = mm_tn(mixed, d_attn_u)
    d_probs = mm_nt(d_mixed, value)
    delta = jnp.sum(probs * d_probs, axis=-1, keepdims=True)
    d_scores = (probs * (d_probs - delta)).astype(BF)
    d_query = mm(d_scores, key) * scale
    d_key = mm_tn(d_scores, query_c) * scale
    d_value = mm_tn(probs_low, d_mixed)
    if C > 1:
        d_query = lax.dynamic_update_slice_in_dim(jnp.zeros((L, HEAD), F32), d_query, chunk * qlen, 0)
    dq = unrotate(d_query, cosine, sine).astype(BF)
    dk = unrotate(d_key, cosine, sine).astype(BF)
    dv = d_value.astype(BF)
    d_u = [mm_nt(dq, f_q_b).astype(BF), mm_nt(dk, f_k_b).astype(BF), mm_nt(dv, f_v_b).astype(BF)]
    d_pu = jnp.concatenate([dq, dk, dv] + d_u, axis=1)
    d_norm_one = mm_nt(d_pu, w1).astype(BF)
    d_norm_one = line_sum(d_norm_one.reshape(G, own, width), G, 9)
    g_w1 = mm_tn(norm_one, d_pu)
    g_q_b = mm_tn(u_q, dq)
    g_kv_b = [mm_tn(u_k, dk), mm_tn(u_v, dv)]
    d_gain_one, back_one = norm_back(d_norm_one, x_own, gain_one)
    grad_input = d_resid + back_one

    per = own // seg
    outs = [activations.reshape(per, seg, width), grad_input.reshape(per, seg, width)]
    moved = []
    for o in outs:
        full = jnp.zeros((S,) + o.shape[1:], o.dtype)
        moved.append(lax.dynamic_update_slice_in_dim(full, o, lax.rem(s, G) * per, 0))
    moved = exchange(moved, "seq", S, 10)
    src = s // per
    pick = []
    for m in moved:
        rows = [lax.dynamic_index_in_dim(m, row * G + src, 0, keepdims=False) for row in range(R)]
        pick.append(jnp.stack(rows))
    activations, grad_input = pick

    def split(g, rows):
        return g.astype(BF).reshape(-1, F, rows, g.shape[1]).transpose(1, 0, 2, 3)

    d_gains = jnp.pad(jnp.stack([d_gain_one, d_gain_two], axis=1), ((0, 0), (0, 126)))
    parts = [
        split(g_w1[:, :HEAD], kb),
        split(jnp.concatenate([g_w1[:, HEAD:], g_gu_a, d_gains], axis=1), kb),
        split(g_gu, kb),
        split(g_gu_b, rb),
        split(g_q_b, rb),
        split(jnp.concatenate(g_kv_b + [g_out_b, g_down_b], axis=1), rb),
        split(g_out, ob),
        g_down.astype(BF).reshape(F, 1, hb, -1),
    ]
    parts = exchange(parts, "fsdp", F, 11)
    parts = [jnp.sum(g.astype(F32), axis=0) for g in parts]
    g_down = parts.pop()[0]
    parts = [g.astype(BF) for g in parts]
    per_head = S // HEADS
    g_out = parts[6]
    full = jnp.zeros((S,) + g_out.shape[1:], BF)
    parts[6] = lax.dynamic_update_slice_in_dim(full, g_out, head * per_head, 0)
    t_q, t_1, t_gu, t_gb, t_qb, t_2, t_out = exchange(parts, "seq", S, 12)

    def by_head(t):
        t = t.astype(F32).reshape(R, HEADS, C, t.shape[1], HEAD).sum(axis=(0, 2))
        return t.transpose(1, 0, 2).reshape(t.shape[1], HEADS * HEAD)

    def halves(t):
        t = t.astype(F32).reshape(S, t.shape[1], 2, hl).transpose(2, 1, 0, 3)
        return t.reshape(2, t.shape[1], hidden)

    t_1 = jnp.sum(t_1.astype(F32), axis=0)
    t_2 = jnp.sum(t_2.astype(F32), axis=0)
    grad_w_qkv = jnp.concatenate([by_head(t_q), t_1[:, : 2 * HEAD]], axis=1)
    g_qkv_a = t_1[:, 2 * HEAD : 2 * HEAD + 3 * RANK]
    g_gu_a = t_1[:, 2 * HEAD + 3 * RANK : 2 * HEAD + 5 * RANK]
    d_gain_one = t_1[:, 2 * HEAD + 5 * RANK]
    d_gain_two = t_1[:, 2 * HEAD + 5 * RANK + 1]
    g_gu = halves(t_gu)
    g_out = jnp.sum(t_out.astype(F32), axis=0)
    return (
        activations,
        grad_input,
        grad_w_qkv,
        g_qkv_a,
        by_head(t_qb),
        jnp.stack([t_2[:, :HEAD], t_2[:, HEAD : 2 * HEAD]]),
        g_out[:, :width],
        g_out[:, width:],
        t_2[:, 2 * HEAD : 2 * HEAD + width],
        jnp.concatenate([g_gu[0], g_gu[1]], axis=1),
        g_gu_a,
        halves(t_gb),
        g_down[:, :width],
        g_down[:, width:],
        t_2[:, 2 * HEAD + width :],
        d_gain_one,
        d_gain_two,
    )


def solution(mesh):
    both = P(("seq", "fsdp"), None)
    second = P(None, ("seq", "fsdp"), None)
    tokens = P("fsdp", "seq", None)
    gain = P(("seq", "fsdp"))
    return jax.shard_map(
        functools.partial(shards, mesh.shape["seq"], mesh.shape["fsdp"]),
        mesh=mesh,
        in_specs=(tokens, P("fsdp", "seq"), tokens)
        + (both, both, both, second, both, both, both, both, both, second, both, both, both, gain, gain),
        out_specs=(tokens, tokens)
        + (both, both, both, second, both, both, both, both, both, second, both, both, both, gain, gain),
        check_vma=False,
    )
```

```python
import functools
import math

import jax
import jax.numpy as jnp
from jax import lax
from jax.experimental import pallas as pl
from jax.experimental.pallas import tpu as pltpu
from jax.sharding import PartitionSpec as P

HEADS = 4
HEAD = 256
RANK = 256
EPSILON = 1e-06
ROPE_BASE = 10000.0
MASKED = -1e30
MESH = pl.DeviceIdType.MESH
BF = jnp.bfloat16
F32 = jnp.float32


def mm(left, right):
    return jnp.dot(left, right, preferred_element_type=F32)


def mm_tn(left, right):
    return lax.dot_general(left, right, (((0,), (0,)), ((), ())), preferred_element_type=F32)


def mm_nt(left, right):
    return lax.dot_general(left, right, (((1,), (1,)), ((), ())), preferred_element_type=F32)


def remote(src, dst, send, recv, peer):
    return pltpu.make_async_remote_copy(
        src_ref=src, dst_ref=dst, send_sem=send, recv_sem=recv, device_id=peer, device_id_type=MESH
    )


class Direct:
    steps = 0

    def __init__(self, x, axis, size, spread=False):
        self.x, self.axis, self.size, self.spread = x, axis, size, spread
        shape = ((size,) if spread else ()) + x.shape
        self.out = jax.ShapeDtypeStruct(shape, x.dtype)
        self.scratch = [
            pltpu.SemaphoreType.DMA,
            pltpu.SemaphoreType.DMA((size,)),
            pltpu.SemaphoreType.DMA((size,)),
        ]

    def bind(self, x_ref, o_ref, local, send, recv):
        me = lax.axis_index(self.axis)
        self.copies = []
        for k in range(1, self.size):
            peer = lax.rem(me + k, self.size)
            src = x_ref if self.spread else x_ref.at[peer]
            self.copies.append(remote(src, o_ref.at[me], send.at[k], recv.at[k], {self.axis: peer}))
        src = x_ref if self.spread else x_ref.at[me]
        self.copies.append(pltpu.make_async_copy(src, o_ref.at[me], local))

    def start(self):
        for copy in self.copies:
            copy.start()

    def finish(self):
        for copy in self.copies:
            copy.wait()


class Post:
    steps = 0

    def __init__(self, x, slots, sends):
        self.slots, self.sends = slots, sends
        self.x = x
        self.out = jax.ShapeDtypeStruct((slots,) + x.shape[1:], x.dtype)
        count = len(sends(0))
        self.scratch = [
            pltpu.SemaphoreType.DMA((count,)),
            pltpu.SemaphoreType.DMA((count,)),
            pltpu.SemaphoreType.DMA((slots,)),
        ]

    def bind(self, x_ref, o_ref, local, send, recv):
        s = lax.axis_index("seq")
        self.s = s
        self.plan = []
        for k, (block, device, slot) in enumerate(self.sends(s)):
            away = remote(x_ref.at[block], o_ref.at[slot], send.at[k], recv.at[slot], {"seq": device})
            here = pltpu.make_async_copy(x_ref.at[block], o_ref.at[slot], recv.at[slot])
            self.plan.append((device, away, here))
        self.arrive = [
            pltpu.make_async_copy(x_ref.at[0], o_ref.at[k], recv.at[k]) for k in range(self.slots)
        ]

    def start(self):
        for device, away, here in self.plan:
            pl.when(device != self.s)(away.start)
            pl.when(device == self.s)(here.start)

    def finish(self):
        for copy in self.arrive:
            copy.wait()
        for device, away, here in self.plan:
            pl.when(device != self.s)(away.wait_send)


class Line:
    def __init__(self, x, line):
        self.x, self.line = x, line
        self.steps = line // 2 - 1
        self.out = jax.ShapeDtypeStruct((line,) + x.shape, x.dtype)
        self.scratch = [
            pltpu.SemaphoreType.DMA,
            pltpu.SemaphoreType.DMA((2 * line,)),
            pltpu.SemaphoreType.DMA((line,)),
        ]

    def bind(self, x_ref, o_ref, local, send, recv):
        self.x_ref, self.o_ref, self.send, self.recv = x_ref, o_ref, send, recv
        line = self.line
        s = lax.axis_index("seq")
        base = s // line * line
        self.n2 = line // 2
        self.i = s - base
        self.p, self.core = self.i // 2, lax.rem(self.i, 2)
        self.sib = s + 1 - 2 * self.core
        self.left = base + lax.rem(self.i + line - 2, line)
        self.right = base + lax.rem(self.i + 2, line)
        self.own = pltpu.make_async_copy(x_ref, o_ref.at[self.i], local)

    def copy(self, blk, src, dst, k):
        return remote(src, self.o_ref.at[blk], self.send.at[k], self.recv.at[blk], {"seq": dst})

    def start(self):
        @pl.when(self.p < self.n2 - 1)
        def _():
            self.copy(self.i, self.x_ref, self.right, 0).start()

        @pl.when(self.p > 0)
        def _():
            self.copy(self.i, self.x_ref, self.left, 1).start()

        self.copy(self.i, self.x_ref, self.sib, 2).start()
        self.own.start()

    def step(self, d):
        p, n2, o = self.p, self.n2, self.o_ref

        @pl.when(p - d >= 0)
        def _():
            blk = self.i - 2 * d
            self.copy(blk, o.at[blk], self.left, 0).wait_recv()

            @pl.when(p < n2 - 1)
            def _():
                self.copy(blk, o.at[blk], self.right, 4 * d).start()

            self.copy(blk, o.at[blk], self.sib, 4 * d + 1).start()

        @pl.when(p + d < n2)
        def _():
            blk = self.i + 2 * d
            self.copy(blk, o.at[blk], self.right, 0).wait_recv()

            @pl.when(p > 0)
            def _():
                self.copy(blk, o.at[blk], self.left, 4 * d + 2).start()

            self.copy(blk, o.at[blk], self.sib, 4 * d + 3).start()

    def finish(self):
        p, n2, o = self.p, self.n2, self.o_ref

        def sent(k):
            self.copy(self.i, self.x_ref, self.sib, k).wait_send()

        for q in range(n2):
            blk = 2 * q + 1 - self.core
            self.copy(blk, o.at[blk], self.sib, 0).wait_recv()

        @pl.when(p < n2 - 1)
        def _():
            sent(0)

        @pl.when(p > 0)
        def _():
            sent(1)

        sent(2)
        for d in range(1, n2):

            @pl.when(p - d >= 0)
            def _():
                @pl.when(p < n2 - 1)
                def _():
                    sent(4 * d)

                sent(4 * d + 1)

            @pl.when(p + d < n2)
            def _():
                @pl.when(p > 0)
                def _():
                    sent(4 * d + 2)

                sent(4 * d + 3)

        self.own.wait()


class LineSum:
    vmem = True

    def __init__(self, x, line):
        self.x, self.line = x, line
        self.n2 = n2 = line // 2
        self.steps = n2 - 1
        blk = x.shape[1:]
        self.out = jax.ShapeDtypeStruct(blk, F32)
        self.scratch = [pltpu.VMEM((n2,) + blk, BF)] * 4 + [
            pltpu.SemaphoreType.DMA((3 * n2,)),
            pltpu.SemaphoreType.DMA((3 * n2,)),
        ]

    def bind(self, x_ref, o_ref, mine, from_sib, from_left, from_right, send, recv):
        self.x_ref, self.o_ref = x_ref, o_ref
        self.mine, self.from_sib, self.from_left, self.from_right = mine, from_sib, from_left, from_right
        line, n2 = self.line, self.n2
        s = lax.axis_index("seq")
        base = s // line * line
        i = s - base
        self.p, self.core = i // 2, lax.rem(i, 2)
        sib = {"seq": s + 1 - 2 * self.core}
        left = {"seq": base + lax.rem(i + line - 2, line)}
        right = {"seq": base + lax.rem(i + 2, line)}
        core = self.core
        self.hand_over = lambda q: remote(
            x_ref.at[2 * q + 1 - core], from_sib.at[q], send.at[q], recv.at[q], sib
        )
        self.rightward = lambda q: remote(
            mine.at[q], from_left.at[q], send.at[n2 + q], recv.at[n2 + q], right
        )
        self.leftward = lambda q: remote(
            mine.at[q], from_right.at[q], send.at[2 * n2 + q], recv.at[2 * n2 + q], left
        )
        order = []
        for k in range((n2 + 1) // 2):
            order += [n2 - 1 - k] + ([k] if k != n2 - 1 - k else [])
        self.order = order

    def start(self):
        for q in self.order:
            self.hand_over(q).start()

    def add(self, q, other):
        self.mine[q] = (self.mine[q].astype(F32) + other[q].astype(F32)).astype(BF)

    def step(self, d):
        p, n2 = self.p, self.n2
        if d == 1:
            for q in self.order:
                self.hand_over(q).wait_recv()
                own = self.x_ref[2 * q + self.core].astype(F32)
                self.mine[q] = (own + self.from_sib[q].astype(F32)).astype(BF)

                @pl.when((q > p) & (p == 0))
                def _():
                    self.rightward(q).start()

                @pl.when((q < p) & (p == n2 - 1))
                def _():
                    self.leftward(q).start()

        q_right = n2 - d

        @pl.when((p > 0) & (p < q_right))
        def _():
            self.rightward(q_right).wait_recv()
            self.add(q_right, self.from_left)
            self.rightward(q_right).start()

        q_left = d - 1

        @pl.when((p < n2 - 1) & (p > q_left))
        def _():
            self.leftward(q_left).wait_recv()
            self.add(q_left, self.from_right)
            self.leftward(q_left).start()

    def finish(self):
        p, n2 = self.p, self.n2
        for q in range(n2):

            @pl.when(p == q)
            def _():
                total = self.mine[q].astype(F32)
                if q > 0:
                    self.rightward(q).wait_recv()
                    total += self.from_left[q].astype(F32)
                if q < n2 - 1:
                    self.leftward(q).wait_recv()
                    total += self.from_right[q].astype(F32)
                self.o_ref[...] = total

        for q in range(n2):
            self.hand_over(q).wait_send()

            @pl.when(q > p)
            def _():
                self.rightward(q).wait_send()

            @pl.when(q < p)
            def _():
                self.leftward(q).wait_send()


def transfer_kernel(ops, axes, *refs):
    count = len(ops)
    rest = list(refs[2 * count :])
    for a, op in enumerate(ops):
        take = len(op.scratch)
        op.bind(refs[a], refs[count + a], *rest[:take])
        rest = rest[take:]
    barrier = pltpu.get_barrier_semaphore()
    for axis, size in axes:
        me = lax.axis_index(axis)
        for k in range(1, size):
            peer = {axis: lax.rem(me + k, size)}
            pl.semaphore_signal(barrier, inc=1, device_id=peer, device_id_type=MESH)
    pl.semaphore_wait(barrier, sum(size - 1 for _, size in axes))
    for op in ops:
        op.start()
    for d in range(1, 1 + max(op.steps for op in ops)):
        for op in ops:
            if d <= op.steps:
                op.step(d)
    for op in ops:
        op.finish()


def transfer(ops, axes, collective_id):
    spaces = [
        pl.BlockSpec(memory_space=pltpu.VMEM if hasattr(op, "vmem") else pl.ANY) for op in ops
    ]
    return pl.pallas_call(
        functools.partial(transfer_kernel, ops, axes),
        out_shape=[op.out for op in ops],
        in_specs=spaces,
        out_specs=spaces,
        scratch_shapes=[entry for op in ops for entry in op.scratch],
        compiler_params=pltpu.CompilerParams(
            collective_id=collective_id, has_side_effects=True, vmem_limit_bytes=48 << 20
        ),
    )(*[op.x for op in ops])


def norm_apply(hidden, gain):
    return hidden * lax.rsqrt(jnp.mean(hidden * hidden, axis=-1, keepdims=True) + EPSILON) * gain


def rope_tables(positions):
    half = HEAD // 2
    spacing = jnp.exp(-(2.0 * jnp.arange(half).astype(F32) / HEAD) * math.log(ROPE_BASE))
    angle = positions.astype(F32)[..., None] * spacing
    return jnp.cos(angle), jnp.sin(angle)


def rotate(values, cosine, sine):
    half = values.shape[-1] // 2
    a, b = values[..., :half], values[..., half:]
    return jnp.concatenate([a * cosine - b * sine, b * cosine + a * sine], axis=-1)


def unrotate(grads, cosine, sine):
    half = grads.shape[-1] // 2
    a, b = grads[..., :half], grads[..., half:]
    return jnp.concatenate([a * cosine + b * sine, b * cosine - a * sine], axis=-1)


def shards(
    S,
    F,
    layer_input,
    document_numbers,
    cotangent,
    w_qkv,
    qkv_a,
    q_b,
    kv_b,
    w_out,
    out_a,
    out_b,
    w_gu,
    gu_a,
    gu_b,
    w_down,
    down_a,
    down_b,
    gain_a,
    gain_f,
):
    R, seg, width = layer_input.shape
    L = seg * S
    own = R * seg
    G = S // R
    C = G // HEADS
    scale = HEAD**-0.5
    kb = w_qkv.shape[0]
    rb = q_b.shape[0]
    hb = w_down.shape[0]
    ob = w_out.shape[0]
    hidden = w_gu.shape[1] // 2
    hl = hidden // S
    s = lax.axis_index("seq")
    r = s // G
    head = lax.rem(s, G) // C
    chunk = lax.rem(s, C)
    qlen = L // C

    on_seq, on_fsdp = ("seq", S), ("fsdp", F)
    per_head = S // HEADS
    gains = jnp.pad(jnp.stack([gain_a, gain_f], axis=1), ((0, 0), (0, 126)))
    pack1 = jnp.concatenate([w_qkv, qkv_a, gains], axis=1)
    pack2 = jnp.concatenate([q_b, kv_b[0], kv_b[1], out_b], axis=1)
    pack3 = jnp.concatenate([w_out, out_a], axis=1)
    gw = jnp.concatenate(
        [
            jnp.concatenate([w_gu[:, :hidden].reshape(kb, S, hl), w_gu[:, hidden:].reshape(kb, S, hl)], axis=2),
            jnp.concatenate([gu_b[0].reshape(rb, S, hl), gu_b[1].reshape(rb, S, hl)], axis=2),
        ],
        axis=0,
    ).transpose(1, 0, 2)
    p1, p2, p3, gw, f_gu_a, f_down_b = transfer(
        [Direct(x, "fsdp", F, True) for x in (pack1, pack2, pack3)]
        + [Direct(gw, "seq", S)]
        + [Direct(x, "fsdp", F, True) for x in (gu_a, down_b)],
        [on_seq, on_fsdp],
        0,
    )
    dw = jnp.concatenate([w_down, down_a], axis=1)
    gw = lax.all_gather(gw, "fsdp", axis=1)
    dw = lax.all_gather(dw, "fsdp", axis=0)
    cot = lax.all_gather(cotangent.reshape(own, width), "seq", axis=0)
    f_gu_a = lax.all_gather(f_gu_a, "seq", axis=0).reshape(width, 2 * RANK)
    f_down_b = lax.all_gather(f_down_b, "seq", axis=0).reshape(RANK, width)
    ids = jnp.pad(document_numbers[:, None, :], ((0, 0), (0, 7), (0, 128 - seg)))

    def to_head(at):
        return [(0, row * G + at // per_head * C + c, lax.rem(at, per_head)) for row in range(R) for c in range(C)]

    p1, p2, xin, ids, wo = transfer(
        [Line(p1, S), Line(p2, S), Line(layer_input, S), Line(ids, S), Post(p3[None], per_head, to_head)],
        [on_seq],
        1,
    )
    p1 = p1.reshape(width, -1)
    p2 = p2.reshape(RANK, -1)
    wo = wo.reshape(HEAD, -1)
    xrow = lax.dynamic_index_in_dim(xin, r, 1, keepdims=False).reshape(L, width).astype(F32)
    cot = cot.reshape(S, R, seg, width).transpose(1, 0, 2, 3).reshape(R * L, width)
    ids = lax.dynamic_index_in_dim(ids[:, :, 0, :seg], r, 1, keepdims=False).reshape(L)
    gb = gw[:, :, kb:].reshape(RANK, 2 * hl)
    gw = gw[:, :, :kb].reshape(width, 2 * hl)
    dw = dw.reshape(hl, -1)

    q0 = HEADS * HEAD
    wq = lax.dynamic_slice_in_dim(p1, head * HEAD, HEAD, 1)
    w1 = jnp.concatenate([wq, p1[:, q0 : q0 + 2 * HEAD + 3 * RANK]], axis=1)
    at = q0 + 2 * HEAD + 3 * RANK
    gain_one = p1[:, at].astype(F32)
    gain_two = p1[:, at + 1].astype(F32)
    f_q_b = lax.dynamic_slice_in_dim(p2, head * HEAD, HEAD, 1)
    f_k_b = p2[:, q0 : q0 + HEAD]
    f_v_b = p2[:, q0 + HEAD : q0 + 2 * HEAD]
    f_out_b = p2[:, q0 + 2 * HEAD : q0 + 2 * HEAD + width]

    place = jnp.arange(L, dtype=jnp.int32)
    same = ids[:, None] == ids[None, :]
    before = place[None, :] < place[:, None]
    positions = jnp.sum((same & before).astype(jnp.int32), axis=1)
    allowed = same & (place[None, :] <= place[:, None])
    cosine, sine = rope_tables(positions)
    norm_one = norm_apply(xrow, gain_one).astype(BF)
    pu = mm(norm_one, w1)
    u = pu[:, 3 * HEAD :].astype(BF)
    u_q, u_k, u_v = u[:, :RANK], u[:, RANK : 2 * RANK], u[:, 2 * RANK :]
    query = rotate(pu[:, :HEAD] + mm(u_q, f_q_b), cosine, sine).astype(BF)
    key = rotate(pu[:, HEAD : 2 * HEAD] + mm(u_k, f_k_b), cosine, sine).astype(BF)
    value = (pu[:, 2 * HEAD : 3 * HEAD] + mm(u_v, f_v_b)).astype(BF)
    if C > 1:
        query_c = lax.dynamic_slice_in_dim(query, chunk * qlen, qlen, 0)
        allowed = lax.dynamic_slice_in_dim(allowed, chunk * qlen, qlen, 0)
    else:
        query_c = query
    scores = jnp.where(allowed, mm_nt(query_c, key) * scale, MASKED)
    top = jnp.max(scores, axis=-1, keepdims=True)
    lse = top + jnp.log(jnp.sum(jnp.exp(scores - top), axis=-1, keepdims=True))
    probs = jnp.where(allowed, jnp.exp(scores - lse), 0.0)
    probs_low = probs.astype(BF)
    mixed = mm(probs_low, value).astype(BF)
    part = mm(mixed, wo).astype(BF)
    if C > 1:
        part = lax.dynamic_update_slice_in_dim(jnp.zeros((L, part.shape[1]), BF), part, chunk * qlen, 0)
    (attn,) = transfer([LineSum(part.reshape(G, own, -1), G)], [on_seq], 4)
    u_out = attn[:, width:].astype(BF)
    mine = lax.rem(s, G) * own
    x_own = lax.dynamic_slice_in_dim(xrow, mine, own, 0)
    resid = x_own + attn[:, :width] + mm(u_out, f_out_b)
    norm_two_own = norm_apply(resid, gain_two).astype(BF)
    (norm_two,) = transfer([Line(norm_two_own, S)], [on_seq], 5)
    norm_two = norm_two.reshape(R * L, width)

    u_gu = mm(norm_two, f_gu_a).astype(BF)
    gu = mm(norm_two, gw)
    gate = gu[:, :hl] + mm(u_gu[:, :RANK], gb[:, :hl])
    up = gu[:, hl:] + mm(u_gu[:, RANK:], gb[:, hl:])
    d_u_down = mm_nt(cot, f_down_b).astype(BF)
    cot_u = jnp.concatenate([cot, d_u_down], axis=1)
    d_act = mm_nt(cot_u, dw)
    inner = math.sqrt(2.0 / math.pi)
    th = jnp.tanh(inner * (gate + 0.044715 * gate * gate * gate))
    gelu = 0.5 * gate * (1.0 + th)
    act = (gelu * up).astype(BF)
    slope = 0.5 * (1.0 + th) + 0.5 * gate * (1.0 - th * th) * inner * (1.0 + 3 * 0.044715 * gate * gate)
    d_gate = (d_act * up * slope).astype(BF)
    d_up = (d_act * gelu).astype(BF)
    d_gu = jnp.concatenate([d_gate, d_up], axis=1)
    d_u_gu = jnp.concatenate(
        [mm_nt(d_gate, gb[:, :hl]), mm_nt(d_up, gb[:, hl:])], axis=1
    ).astype(BF)
    d_norm_two = (mm_nt(d_gu, gw) + mm_nt(d_u_gu, f_gu_a)).astype(BF)
    (d_norm_two,) = transfer([LineSum(d_norm_two.reshape(S, own, width), S)], [on_seq], 6)
    ffn = mm(act, dw)
    u_down = ffn[:, width:].astype(BF)
    ffn = (ffn[:, :width] + mm(u_down, f_down_b)).astype(BF)
    (ffn,) = transfer([LineSum(ffn.reshape(S, own, width), S)], [on_seq], 7)
    activations = (resid + ffn).astype(BF)
    g_down = mm_tn(act, cot_u)
    g_down_b = mm_tn(u_down, cot)
    g_gu = mm_tn(norm_two, d_gu)
    g_gu_b = jnp.concatenate([mm_tn(u_gu[:, :RANK], d_gate), mm_tn(u_gu[:, RANK:], d_up)], axis=1)
    g_gu_a = mm_tn(norm_two, d_u_gu)

    def split(g, rows):
        return g.astype(BF).reshape(-1, F, rows, g.shape[1]).transpose(1, 0, 2, 3)

    def scatter(g, axes):
        return lax.psum_scatter(g, axes, scatter_dimension=0, tiled=True)[0]

    g_gu = scatter(jnp.concatenate([split(g_gu, kb), split(g_gu_b, rb)], axis=2), "fsdp")
    g_down = scatter(g_down.astype(BF).reshape(F, hb, -1), "fsdp").astype(F32)
    g_gu_a = scatter(g_gu_a.astype(BF).reshape(S * F, kb, -1), ("seq", "fsdp")).astype(F32)
    g_down_b = scatter(g_down_b.astype(BF).reshape(S * F, rb, -1), ("seq", "fsdp")).astype(F32)

    def norm_back(G_in, h, g):
        q = lax.rsqrt(jnp.mean(h * h, axis=-1, keepdims=True) + EPSILON)
        gg = G_in * g
        d_gain = jnp.sum(G_in * (h * q), axis=0)
        return d_gain, q * gg - h * (q * q * q) * jnp.mean(gg * h, axis=-1, keepdims=True)

    d_gain_two, back = norm_back(d_norm_two, resid, gain_two)
    cot_own = lax.dynamic_slice_in_dim(cot, s * own, own, 0)
    d_resid = cot_own.astype(F32) + back

    d_attn_own = d_resid.astype(BF)
    (d_attn,) = transfer([Line(d_attn_own, G)], [on_seq], 8)
    d_attn = d_attn.reshape(L, width)
    g_out_b = mm_tn(u_out, d_attn_own)
    if C > 1:
        d_attn = lax.dynamic_slice_in_dim(d_attn, chunk * qlen, qlen, 0)
    d_u_out = mm_nt(d_attn, f_out_b).astype(BF)
    d_attn_u = jnp.concatenate([d_attn, d_u_out], axis=1)
    d_mixed = mm_nt(d_attn_u, wo).astype(BF)
    g_out = mm_tn(mixed, d_attn_u)
    d_probs = mm_nt(d_mixed, value)
    delta = jnp.sum(probs * d_probs, axis=-1, keepdims=True)
    d_scores = (probs * (d_probs - delta)).astype(BF)
    d_query = mm(d_scores, key) * scale
    d_key = mm_tn(d_scores, query_c) * scale
    d_value = mm_tn(probs_low, d_mixed)
    if C > 1:
        d_query = lax.dynamic_update_slice_in_dim(jnp.zeros((L, HEAD), F32), d_query, chunk * qlen, 0)
    dq = unrotate(d_query, cosine, sine).astype(BF)
    dk = unrotate(d_key, cosine, sine).astype(BF)
    dv = d_value.astype(BF)
    d_u = [mm_nt(dq, f_q_b).astype(BF), mm_nt(dk, f_k_b).astype(BF), mm_nt(dv, f_v_b).astype(BF)]
    d_pu = jnp.concatenate([dq, dk, dv] + d_u, axis=1)
    d_norm_one = mm_nt(d_pu, w1).astype(BF)
    (d_norm_one,) = transfer([LineSum(d_norm_one.reshape(G, own, width), G)], [on_seq], 9)
    g_w1 = mm_tn(norm_one, d_pu)
    g_q_b = mm_tn(u_q, dq)
    g_kv_b = [mm_tn(u_k, dk), mm_tn(u_v, dv)]
    d_gain_one, back_one = norm_back(d_norm_one, x_own, gain_one)
    grad_input = d_resid + back_one

    d_gains = jnp.pad(jnp.stack([d_gain_one, d_gain_two], axis=1), ((0, 0), (0, 126)))
    t_1 = jnp.concatenate([g_w1[:, HEAD:], d_gains], axis=1).astype(BF).reshape(S, F, kb, -1)
    t_2 = jnp.concatenate(g_kv_b + [g_out_b], axis=1).astype(BF).reshape(S, F, rb, -1)
    t_1, t_2, t_q, t_qb, t_out = transfer(
        [LineSum(t_1, S), LineSum(t_2, S)]
        + [Direct(x, "fsdp", F) for x in (split(g_w1[:, :HEAD], kb), split(g_q_b, rb), split(g_out, ob))],
        [on_seq, on_fsdp],
        10,
    )

    def total(t):
        return jnp.sum(t.astype(F32), axis=0)

    per = own // seg

    def to_rows(at):
        return [(j, lax.rem(at, G) * per + j, at // G) for j in range(per)]

    def to_out(at):
        return [
            (j, lax.rem(at, G) // C * per_head + j, at // G * C + lax.rem(at, C)) for j in range(per_head)
        ]

    t_1, t_2, t_q, t_qb, t_gu, t_out, activations, grad_input = transfer(
        [Direct(t.astype(BF), "fsdp", F) for t in (t_1, t_2)]
        + [Direct(t.astype(BF), "seq", S) for t in (total(t_q), total(t_qb), g_gu)]
        + [Post(total(t_out).astype(BF), R * C, to_out)]
        + [Post(t.reshape(per, seg, width), R, to_rows) for t in (activations, grad_input)],
        [on_seq, on_fsdp],
        11,
    )

    def by_head(t):
        t = t.astype(F32).reshape(R, HEADS, C, t.shape[1], HEAD).sum(axis=(0, 2))
        return t.transpose(1, 0, 2).reshape(t.shape[1], HEADS * HEAD)

    def halves(t):
        t = t.astype(F32).reshape(S, t.shape[1], 2, hl).transpose(2, 1, 0, 3)
        return t.reshape(2, t.shape[1], hidden)

    t_1, t_2, g_out = total(t_1), total(t_2), total(t_out)
    grad_w_qkv = jnp.concatenate([by_head(t_q), t_1[:, : 2 * HEAD]], axis=1)
    g_qkv_a = t_1[:, 2 * HEAD : 2 * HEAD + 3 * RANK]
    d_gain_one = t_1[:, 2 * HEAD + 3 * RANK]
    d_gain_two = t_1[:, 2 * HEAD + 3 * RANK + 1]
    g_gu_b = halves(t_gu[:, kb:])
    g_gu = halves(t_gu[:, :kb])
    return (
        activations,
        grad_input,
        grad_w_qkv,
        g_qkv_a,
        by_head(t_qb),
        jnp.stack([t_2[:, :HEAD], t_2[:, HEAD : 2 * HEAD]]),
        g_out[:, :width],
        g_out[:, width:],
        t_2[:, 2 * HEAD :],
        jnp.concatenate([g_gu[0], g_gu[1]], axis=1),
        g_gu_a,
        g_gu_b,
        g_down[:, :width],
        g_down[:, width:],
        g_down_b,
        d_gain_one,
        d_gain_two,
    )


def solution(mesh):
    both = P(("seq", "fsdp"), None)
    second = P(None, ("seq", "fsdp"), None)
    tokens = P("fsdp", "seq", None)
    gain = P(("seq", "fsdp"))
    return jax.shard_map(
        functools.partial(shards, mesh.shape["seq"], mesh.shape["fsdp"]),
        mesh=mesh,
        in_specs=(tokens, P("fsdp", "seq"), tokens)
        + (both, both, both, second, both, both, both, both, both, second, both, both, both, gain, gain),
        out_specs=(tokens, tokens)
        + (both, both, both, second, both, both, both, both, both, second, both, both, both, gain, gain),
        check_vma=False,
    )
```

```python
import functools
import math

import jax
import jax.numpy as jnp
from jax import lax
from jax.experimental import pallas as pl
from jax.experimental.pallas import tpu as pltpu
from jax.sharding import PartitionSpec as P

HEADS = 4
HEAD = 256
RANK = 256
EPSILON = 1e-06
ROPE_BASE = 10000.0
MASKED = -1e30
MESH = pl.DeviceIdType.MESH
BF = jnp.bfloat16
F32 = jnp.float32


def mm(left, right):
    return jnp.dot(left, right, preferred_element_type=F32)


def mm_tn(left, right):
    return lax.dot_general(left, right, (((0,), (0,)), ((), ())), preferred_element_type=F32)


def mm_nt(left, right):
    return lax.dot_general(left, right, (((1,), (1,)), ((), ())), preferred_element_type=F32)


def remote(src, dst, send, recv, peer):
    return pltpu.make_async_remote_copy(
        src_ref=src, dst_ref=dst, send_sem=send, recv_sem=recv, device_id=peer, device_id_type=MESH
    )


class Direct:
    steps = 0

    def __init__(self, x, axis, size, spread=False):
        self.x, self.axis, self.size, self.spread = x, axis, size, spread
        shape = ((size,) if spread else ()) + x.shape
        self.out = jax.ShapeDtypeStruct(shape, x.dtype)
        self.scratch = [
            pltpu.SemaphoreType.DMA,
            pltpu.SemaphoreType.DMA((size,)),
            pltpu.SemaphoreType.DMA((size,)),
        ]

    def bind(self, x_ref, o_ref, local, send, recv):
        me = lax.axis_index(self.axis)
        self.copies = []
        for k in range(1, self.size):
            peer = lax.rem(me + k, self.size)
            src = x_ref if self.spread else x_ref.at[peer]
            self.copies.append(remote(src, o_ref.at[me], send.at[k], recv.at[k], {self.axis: peer}))
        src = x_ref if self.spread else x_ref.at[me]
        self.copies.append(pltpu.make_async_copy(src, o_ref.at[me], local))

    def start(self):
        for copy in self.copies:
            copy.start()

    def finish(self):
        for copy in self.copies:
            copy.wait()


class Post:
    steps = 0

    def __init__(self, x, slots, sends):
        self.slots, self.sends = slots, sends
        self.x = x
        self.out = jax.ShapeDtypeStruct((slots,) + x.shape[1:], x.dtype)
        count = len(sends(0))
        self.scratch = [
            pltpu.SemaphoreType.DMA((count,)),
            pltpu.SemaphoreType.DMA((count,)),
            pltpu.SemaphoreType.DMA((slots,)),
        ]

    def bind(self, x_ref, o_ref, local, send, recv):
        s = lax.axis_index("seq")
        self.s = s
        self.plan = []
        for k, (block, device, slot) in enumerate(self.sends(s)):
            away = remote(x_ref.at[block], o_ref.at[slot], send.at[k], recv.at[slot], {"seq": device})
            here = pltpu.make_async_copy(x_ref.at[block], o_ref.at[slot], recv.at[slot])
            self.plan.append((device, away, here))
        self.arrive = [
            pltpu.make_async_copy(x_ref.at[0], o_ref.at[k], recv.at[k]) for k in range(self.slots)
        ]

    def start(self):
        for device, away, here in self.plan:
            pl.when(device != self.s)(away.start)
            pl.when(device == self.s)(here.start)

    def finish(self):
        for copy in self.arrive:
            copy.wait()
        for device, away, here in self.plan:
            pl.when(device != self.s)(away.wait_send)


class Line:
    def __init__(self, x, line):
        self.x, self.line = x, line
        self.steps = line // 2 - 1
        self.out = jax.ShapeDtypeStruct((line,) + x.shape, x.dtype)
        self.scratch = [
            pltpu.SemaphoreType.DMA,
            pltpu.SemaphoreType.DMA((2 * line,)),
            pltpu.SemaphoreType.DMA((line,)),
        ]

    def bind(self, x_ref, o_ref, local, send, recv):
        self.x_ref, self.o_ref, self.send, self.recv = x_ref, o_ref, send, recv
        line = self.line
        s = lax.axis_index("seq")
        base = s // line * line
        self.n2 = line // 2
        self.i = s - base
        self.p, self.core = self.i // 2, lax.rem(self.i, 2)
        self.sib = s + 1 - 2 * self.core
        self.left = base + lax.rem(self.i + line - 2, line)
        self.right = base + lax.rem(self.i + 2, line)
        self.own = pltpu.make_async_copy(x_ref, o_ref.at[self.i], local)

    def copy(self, blk, src, dst, k):
        return remote(src, self.o_ref.at[blk], self.send.at[k], self.recv.at[blk], {"seq": dst})

    def start(self):
        @pl.when(self.p < self.n2 - 1)
        def _():
            self.copy(self.i, self.x_ref, self.right, 0).start()

        @pl.when(self.p > 0)
        def _():
            self.copy(self.i, self.x_ref, self.left, 1).start()

        self.copy(self.i, self.x_ref, self.sib, 2).start()
        self.own.start()

    def step(self, d):
        p, n2, o = self.p, self.n2, self.o_ref

        @pl.when(p - d >= 0)
        def _():
            blk = self.i - 2 * d
            self.copy(blk, o.at[blk], self.left, 0).wait_recv()

            @pl.when(p < n2 - 1)
            def _():
                self.copy(blk, o.at[blk], self.right, 4 * d).start()

            self.copy(blk, o.at[blk], self.sib, 4 * d + 1).start()

        @pl.when(p + d < n2)
        def _():
            blk = self.i + 2 * d
            self.copy(blk, o.at[blk], self.right, 0).wait_recv()

            @pl.when(p > 0)
            def _():
                self.copy(blk, o.at[blk], self.left, 4 * d + 2).start()

            self.copy(blk, o.at[blk], self.sib, 4 * d + 3).start()

    def finish(self):
        p, n2, o = self.p, self.n2, self.o_ref

        def sent(k):
            self.copy(self.i, self.x_ref, self.sib, k).wait_send()

        for q in range(n2):
            blk = 2 * q + 1 - self.core
            self.copy(blk, o.at[blk], self.sib, 0).wait_recv()

        @pl.when(p < n2 - 1)
        def _():
            sent(0)

        @pl.when(p > 0)
        def _():
            sent(1)

        sent(2)
        for d in range(1, n2):

            @pl.when(p - d >= 0)
            def _():
                @pl.when(p < n2 - 1)
                def _():
                    sent(4 * d)

                sent(4 * d + 1)

            @pl.when(p + d < n2)
            def _():
                @pl.when(p > 0)
                def _():
                    sent(4 * d + 2)

                sent(4 * d + 3)

        self.own.wait()


class LineSum:
    vmem = True

    def __init__(self, x, line):
        self.x, self.line = x, line
        self.n2 = n2 = line // 2
        self.steps = n2 - 1
        blk = x.shape[1:]
        self.out = jax.ShapeDtypeStruct(blk, F32)
        self.scratch = [pltpu.VMEM((n2,) + blk, BF), pltpu.VMEM((n2 + 1,) + blk, BF)] + [
            pltpu.SemaphoreType.DMA((3 * n2,)),
            pltpu.SemaphoreType.DMA((3 * n2,)),
        ]

    def bind(self, x_ref, o_ref, mine, came, send, recv):
        self.x_ref, self.o_ref, self.mine, self.came = x_ref, o_ref, mine, came
        line, n2 = self.line, self.n2
        s = lax.axis_index("seq")
        base = s // line * line
        i = s - base
        self.p, self.core = i // 2, lax.rem(i, 2)
        sib = {"seq": s + 1 - 2 * self.core}
        left = {"seq": base + lax.rem(i + line - 2, line)}
        right = {"seq": base + lax.rem(i + 2, line)}
        core = self.core
        self.hand_over = lambda q: remote(
            x_ref.at[2 * q + 1 - core], mine.at[q], send.at[q], recv.at[q], sib
        )
        self.rightward = lambda q: remote(
            mine.at[q], came.at[q + 1], send.at[n2 + q], recv.at[n2 + q], right
        )
        self.leftward = lambda q: remote(
            mine.at[q], came.at[q], send.at[2 * n2 + q], recv.at[2 * n2 + q], left
        )
        order = []
        for k in range((n2 + 1) // 2):
            order += [n2 - 1 - k] + ([k] if k != n2 - 1 - k else [])
        self.order = order

    def start(self):
        for q in self.order:
            self.hand_over(q).start()

    def add(self, q, other):
        self.mine[q] = (self.mine[q].astype(F32) + self.came[other].astype(F32)).astype(BF)

    def step(self, d):
        p, n2 = self.p, self.n2
        if d == 1:
            for q in self.order:
                self.hand_over(q).wait_recv()
                own = self.x_ref[2 * q + self.core].astype(F32)
                self.mine[q] = (own + self.mine[q].astype(F32)).astype(BF)

                @pl.when((q > p) & (p == 0))
                def _():
                    self.rightward(q).start()

                @pl.when((q < p) & (p == n2 - 1))
                def _():
                    self.leftward(q).start()

        q_right = n2 - d

        @pl.when((p > 0) & (p < q_right))
        def _():
            self.rightward(q_right).wait_recv()
            self.add(q_right, q_right + 1)
            self.rightward(q_right).start()

        q_left = d - 1

        @pl.when((p < n2 - 1) & (p > q_left))
        def _():
            self.leftward(q_left).wait_recv()
            self.add(q_left, q_left)
            self.leftward(q_left).start()

    def finish(self):
        p, n2 = self.p, self.n2
        for q in range(n2):

            @pl.when(p == q)
            def _():
                total = self.mine[q].astype(F32)
                if q > 0:
                    self.rightward(q).wait_recv()
                    total += self.came[q + 1].astype(F32)
                if q < n2 - 1:
                    self.leftward(q).wait_recv()
                    total += self.came[q].astype(F32)
                self.o_ref[...] = total

        for q in range(n2):
            self.hand_over(q).wait_send()

            @pl.when(q > p)
            def _():
                self.rightward(q).wait_send()

            @pl.when(q < p)
            def _():
                self.leftward(q).wait_send()


def transfer_kernel(ops, axes, *refs):
    count = len(ops)
    rest = list(refs[2 * count :])
    for a, op in enumerate(ops):
        take = len(op.scratch)
        op.bind(refs[a], refs[count + a], *rest[:take])
        rest = rest[take:]
    barrier = pltpu.get_barrier_semaphore()
    for axis, size in axes:
        me = lax.axis_index(axis)
        for k in range(1, size):
            peer = {axis: lax.rem(me + k, size)}
            pl.semaphore_signal(barrier, inc=1, device_id=peer, device_id_type=MESH)
    pl.semaphore_wait(barrier, sum(size - 1 for _, size in axes))
    for op in ops:
        op.start()
    for d in range(1, 1 + max(op.steps for op in ops)):
        for op in ops:
            if d <= op.steps:
                op.step(d)
    for op in ops:
        op.finish()


def transfer(ops, axes, collective_id):
    spaces = [
        pl.BlockSpec(memory_space=pltpu.VMEM if hasattr(op, "vmem") else pl.ANY) for op in ops
    ]
    return pl.pallas_call(
        functools.partial(transfer_kernel, ops, axes),
        out_shape=[op.out for op in ops],
        in_specs=spaces,
        out_specs=spaces,
        scratch_shapes=[entry for op in ops for entry in op.scratch],
        compiler_params=pltpu.CompilerParams(
            collective_id=collective_id, has_side_effects=True, vmem_limit_bytes=48 << 20
        ),
    )(*[op.x for op in ops])


def meet(axes):
    barrier = pltpu.get_barrier_semaphore()
    for axis, size in axes:
        me = lax.axis_index(axis)
        for k in range(1, size):
            peer = {axis: lax.rem(me + k, size)}
            pl.semaphore_signal(barrier, inc=1, device_id=peer, device_id_type=MESH)
    pl.semaphore_wait(barrier, sum(size - 1 for _, size in axes))


def ffn_kernel(
    dims,
    ops,
    n2_own,
    gw_in,
    dw_in,
    cot_in,
    gu_a_in,
    down_b,
    dn_sum,
    ffn_part,
    g_gw,
    g_down,
    g_gu_a,
    g_down_b,
    n2,
    gw,
    gb,
    dw,
    cot_u,
    gu_a,
    u_gu,
    act,
    d_gu,
    d_u_gu,
    u_down,
    dn,
    stage,
    stage_sem,
    cot_sem,
    *sems,
):
    S, F, R, seg, kb, rb, hb, hl, hp = dims
    own = R * seg
    width = n2_own.shape[1]
    tokens = S * own
    G = S // R
    gather, scatter = ops
    take = len(gather.scratch)
    gather.bind(n2_own, n2, *sems[:take])
    scatter.bind(dn, dn_sum, *sems[take:])
    meet([("seq", S)])
    gather.start()

    def fetch(s):
        return pltpu.make_async_copy(gw_in.at[s], stage.at[s % 2], stage_sem.at[s % 2])

    fetch(0).start()
    moves = []
    for j in range(S):
        row, i = j // G, j % G
        for e in range(R):
            at = j * own + e * seg
            src = cot_in.at[i * R + e, pl.ds(row * seg, seg), :]
            dst = cot_u.at[pl.ds(at, seg), pl.ds(0, width)]
            moves.append(pltpu.make_async_copy(src, dst, cot_sem.at[len(moves)]))
            moves[-1].start()

    for s in range(S):
        if s + 1 < S:
            fetch(s + 1).start()
        fetch(s).wait()
        for f in range(F):
            b = s * F + f
            gw[b * kb : b * kb + kb, :] = stage[s % 2, f, 0:kb, :]
            gb[b * rb : b * rb + rb, :] = stage[s % 2, f, kb : kb + rb, :]
            gu_a[b * kb : b * kb + kb, :] = gu_a_in[s, f]
        if s + 1 <= gather.steps:
            gather.step(s + 1)
    for f in range(F):
        dw[f * hb : f * hb + hb, :] = dw_in[f]
    if hp > hl:
        dw[hl:hp, :] = jnp.zeros((hp - hl, dw.shape[1]), BF)
    for move in moves:
        move.wait()
    tile = 256
    tiles = tokens // tile

    @pl.loop(0, tiles)
    def _(t):
        rows = pl.ds(pl.multiple_of(t * tile, tile), tile)
        cot_u[rows, width:] = mm_nt(cot_u[rows, :width], down_b[...]).astype(BF)

    gather.finish()
    inner = math.sqrt(2.0 / math.pi)
    per_tile = tile // own

    @pl.loop(0, tiles)
    def _(t):
        rows = pl.ds(pl.multiple_of(t * tile, tile), tile)
        n = n2[pl.ds(t * per_tile, per_tile)].reshape(tile, width)
        u = mm(n, gu_a[...]).astype(BF)
        u_gu[rows, :] = u
        d_act = mm_nt(cot_u[rows, :], dw[...])
        gate = mm(n, gw[:, :hp]) + mm(u[:, :RANK], gb[:, :hp])
        up = mm(n, gw[:, hp:]) + mm(u[:, RANK:], gb[:, hp:])
        square = gate * gate
        th = jnp.tanh(inner * gate * (1.0 + 0.044715 * square))
        half = 0.5 * (1.0 + th)
        gelu = gate * half
        act[rows, :] = (gelu * up).astype(BF)
        slope = half + 0.5 * gate * (1.0 - th * th) * (inner * (1.0 + 3 * 0.044715 * square))
        d_gate = (d_act * up * slope).astype(BF)
        d_up = (d_act * gelu).astype(BF)
        d_gu[rows, :hp] = d_gate
        d_gu[rows, hp:] = d_up
        d_u_gu[rows, :RANK] = mm_nt(d_gate, gb[:, :hp]).astype(BF)
        d_u_gu[rows, RANK:] = mm_nt(d_up, gb[:, hp:]).astype(BF)
        out = mm_nt(d_gu[rows, :], gw[...]) + mm_nt(d_u_gu[rows, :], gu_a[...])
        dn[pl.ds(t * per_tile, per_tile)] = out.astype(BF).reshape(per_tile, own, width)

    scatter.start()

    @pl.loop(0, tiles)
    def _(t):
        rows = pl.ds(pl.multiple_of(t * tile, tile), tile)
        out = mm(act[rows, :], dw[...])
        low = out[:, width:].astype(BF)
        u_down[rows, :] = low
        out = out[:, :width] + mm(low, down_b[...])
        ffn_part[pl.ds(t * per_tile, per_tile)] = out.astype(BF).reshape(per_tile, own, width)

    scatter.step(1)
    for half in range(2):
        cols = slice(half * hp, half * hp + hp)
        out = mm_tn(u_gu[:, half * RANK : half * RANK + RANK], d_gu[:, cols]).astype(BF)
        for b in range(S * F):
            g_gw[b % F, b // F, kb : kb + rb, cols] = out[b * rb : b * rb + rb, :]
    if scatter.steps >= 2:
        scatter.step(2)
    g_down_b[...] = mm_tn(u_down[...], cot_u[:, :width]).astype(BF)
    step = 128
    n_all = n2[...].reshape(tokens, width)

    @pl.loop(0, cot_u.shape[1] // step)
    def _(t):
        cols = pl.ds(pl.multiple_of(t * step, step), step)
        out = mm_tn(act[...], cot_u[:, cols]).astype(BF)
        for f in range(F):
            g_down[f, :, cols] = out[f * hb : f * hb + hb, :]

    for d in range(3, scatter.steps + 1):
        scatter.step(d)
    step = 256

    @pl.loop(0, 2 * hp // step)
    def _(t):
        cols = pl.ds(pl.multiple_of(t * step, step), step)
        out = mm_tn(n2[...].reshape(tokens, width), d_gu[:, cols]).astype(BF)
        for b in range(S * F):
            g_gw[b % F, b // F, 0:kb, cols] = out[b * kb : b * kb + kb, :]

    scatter.finish()
    out = mm_tn(n2[...].reshape(tokens, width), d_u_gu[...]).astype(BF)
    for b in range(S * F):
        g_gu_a[b // F, b % F] = out[b * kb : b * kb + kb, :]


def feed_forward(n2_own, gw, dw, cot, gu_a, down_b, dims, collective_id):
    S, F, R, seg, kb, rb, hb, hl, hp = dims
    own, width = n2_own.shape
    tokens = S * own
    gather = Line(n2_own, S)
    scatter = LineSum(jax.ShapeDtypeStruct((S, own, width), BF), S)
    vmem = pl.BlockSpec(memory_space=pltpu.VMEM)
    away = pl.BlockSpec(memory_space=pl.ANY)
    low = functools.partial(jax.ShapeDtypeStruct, dtype=BF)
    lora = width + RANK
    return pl.pallas_call(
        functools.partial(ffn_kernel, dims, (gather, scatter)),
        out_shape=[
            jax.ShapeDtypeStruct((own, width), F32),
            low((S, own, width)),
            low((F, S, kb + rb, 2 * hp)),
            low((F, hb, lora)),
            low((S, F, kb, 2 * RANK)),
            low((RANK, width)),
        ],
        in_specs=[vmem, away, vmem, away, vmem, vmem],
        out_specs=[vmem] * 6,
        scratch_shapes=[
            pltpu.VMEM(shape, BF)
            for shape in (
                (S, own, width),
                (width, 2 * hp),
                (RANK, 2 * hp),
                (hp, lora),
                (tokens, lora),
                (width, 2 * RANK),
                (tokens, 2 * RANK),
                (tokens, hp),
                (tokens, 2 * hp),
                (tokens, 2 * RANK),
                (tokens, RANK),
                (S, own, width),
                (2, F, kb + rb, 2 * hp),
            )
        ]
        + [pltpu.SemaphoreType.DMA((2,)), pltpu.SemaphoreType.DMA((S * R,))]
        + gather.scratch
        + scatter.scratch,
        compiler_params=pltpu.CompilerParams(
            collective_id=collective_id, has_side_effects=True, vmem_limit_bytes=62 << 20
        ),
    )(n2_own, gw, dw, cot, gu_a, down_b)


class Bag:
    pass


def norm_back(G_in, h, g):
    q = lax.rsqrt(jnp.mean(h * h, axis=-1, keepdims=True) + EPSILON)
    gg = G_in * g
    d_gain = jnp.sum(G_in * (h * q), axis=0, keepdims=True)
    return d_gain, q * gg - h * (q * q * q) * jnp.mean(gg * h, axis=-1, keepdims=True)


def back_kernel(dims, names, ops, *refs):
    S, F, R, seg, L, kb, rb, hb, ob = dims
    v = Bag()
    for name, ref in zip(names, refs):
        setattr(v, name, ref)
    rest = list(refs[len(names) :])
    bound = Bag()
    for name, (op, src, dst) in ops.items():
        take = len(op.scratch)
        op.bind(getattr(v, src), getattr(v, dst), *rest[:take])
        setattr(bound, name, op)
        rest = rest[take:]
    t = bound
    own = R * seg
    G = S // R
    C = G // HEADS
    qlen = L // C
    width = v.resid.shape[1]
    scale = HEAD**-0.5
    s = lax.axis_index("seq")
    chunk = lax.rem(s, C)
    meet([("seq", S), ("fsdp", F)])
    t.gw.start()
    t.down.start()

    gain_two, back = norm_back(v.d_n2[...], v.resid[...], v.gains[1:2, :])
    d_resid = v.cot_own[...].astype(F32) + back
    v.d_resid[...] = d_resid
    v.d_attn_own[...] = d_resid.astype(BF)
    t.d_attn.start()
    early = [t.ffn, t.gu_a, t.down_b] if "ffn" in ops else [t.gu_a, t.down_b]
    for op in early:
        op.start()
    for d in range(1, t.d_attn.steps + 1):
        t.d_attn.step(d)
    t.d_attn.finish()

    blocks = qlen // own
    first = chunk * blocks
    v.da[:, :width] = v.d_attn[pl.ds(first, blocks)].reshape(qlen, width)
    v.da[:, width:] = mm_nt(v.da[:, :width], v.out_b[...]).astype(BF)
    v.d_mixed[...] = mm_nt(v.da[...], v.wo[...]).astype(BF)

    @pl.loop(0, qlen // 128)
    def _(i):
        rows = pl.ds(pl.multiple_of(i * 128, 128), 128)
        p = v.probs[rows, :]
        d_probs = mm_nt(v.d_mixed[rows, :], v.value[...])
        delta = jnp.sum(p * d_probs, axis=-1, keepdims=True)
        v.d_scores[rows, :] = (p * (d_probs - delta)).astype(BF)
        v.probs_low[rows, :] = p.astype(BF)

    def unrot(g, rows):
        half = HEAD // 2
        cosine, sine = v.cosine[rows, :], v.sine[rows, :]
        a, b = g[:, :half], g[:, half:]
        return (a * cosine + b * sine).astype(BF), (b * cosine - a * sine).astype(BF)

    half = HEAD // 2
    mine = pl.ds(pl.multiple_of(chunk * qlen, own), qlen)
    if C > 1:
        v.d_pu[:, :HEAD] = jnp.zeros((L, HEAD), BF)
    v.d_pu[mine, :half], v.d_pu[mine, half:HEAD] = unrot(mm(v.d_scores[...], v.key[...]) * scale, mine)
    every = pl.ds(0, L)
    v.d_pu[:, HEAD : HEAD + half], v.d_pu[:, HEAD + half : 2 * HEAD] = unrot(
        mm_tn(v.d_scores[...], v.query[...]) * scale, every
    )
    v.d_pu[:, 2 * HEAD : 3 * HEAD] = mm_tn(v.probs_low[...], v.d_mixed[...]).astype(BF)
    for k in range(3):
        v.d_pu[:, 3 * HEAD + k * RANK : 3 * HEAD + (k + 1) * RANK] = mm_nt(
            v.d_pu[:, k * HEAD : (k + 1) * HEAD], v.up_b[k]
        ).astype(BF)

    @pl.loop(0, L // 256)
    def _(i):
        rows = pl.ds(pl.multiple_of(i * 256, 256), 256)
        out = mm_nt(v.d_pu[rows, :], v.w1[...]).astype(BF)
        v.d_attn[pl.ds(i * (256 // own), 256 // own)] = out.reshape(256 // own, own, width)

    t.d_n1.start()
    for op in early:
        op.step(1)

    out = mm_tn(v.mixed[...], v.da[...]).astype(BF)
    for j in range(HEAD // ob):
        v.t_out[j % F, j // F] = out[j * ob : j * ob + ob, :]
    t.out.start()
    out = mm_tn(v.norm_one[...], v.d_pu[:, :HEAD]).astype(BF)
    for b in range(S * F):
        v.t_q[b % F, b // F] = out[b * kb : b * kb + kb, :]
    t.q.start()
    out = mm_tn(v.u[:, :RANK], v.d_pu[:, :HEAD]).astype(BF)
    for b in range(S * F):
        v.t_qb[b % F, b // F] = out[b * rb : b * rb + rb, :]
    t.qb.start()
    t.d_n1.step(1)

    @pl.loop(0, v.t_1.shape[3] // 256)
    def _(i):
        cols = pl.ds(pl.multiple_of(i * 256, 256), 256)
        src = pl.ds(pl.multiple_of(i * 256 + 256, 256), 256)
        out = mm_tn(v.norm_one[...], v.d_pu[:, src]).astype(BF)
        for b in range(S * F):
            v.t_1[b // F, b % F, :, cols] = out[b * kb : b * kb + kb, :]

    t.one.start()
    for d in range(2, t.d_n1.steps + 1):
        t.d_n1.step(d)
    for k in range(2):
        out = mm_tn(
            v.u[:, (k + 1) * RANK : (k + 2) * RANK], v.d_pu[:, (k + 1) * HEAD : (k + 2) * HEAD]
        ).astype(BF)
        for b in range(S * F):
            v.t_2[b // F, b % F, :, k * HEAD : (k + 1) * HEAD] = out[b * rb : b * rb + rb, :]
    out = mm_tn(v.u_out[...], v.d_attn_own[...]).astype(BF)
    for b in range(S * F):
        v.t_2[b // F, b % F, :, 2 * HEAD :] = out[b * rb : b * rb + rb, :]
    t.two.start()

    t.d_n1.finish()
    gain_one, back = norm_back(v.d_n1_sum[...], v.x_own[...].astype(F32), v.gains[0:1, :])
    grad_input = v.d_resid[...] + back
    for j in range(R):
        v.grad_rows[j] = grad_input[j * seg : j * seg + seg, :]
    t.grad_input.start()
    both = jnp.concatenate([gain_one, gain_two, jnp.zeros((126, width), F32)], axis=0)
    both = jnp.transpose(both)
    for b in range(S * F):
        v.t_3[b // F, b % F] = both[b * kb : b * kb + kb, :].astype(BF)
    t.three.start()
    for d in range(2, t.gu_a.steps + 1):
        for op in early:
            op.step(d)
    late = [t.one, t.two, t.three]
    for op in late:
        op.step(1)
    for op in early:
        op.finish()
    activations = (v.resid[...] + v.ffn_sum[...]).astype(BF)
    for j in range(R):
        v.act_rows[j] = activations[j * seg : j * seg + seg, :]
    t.activations.start()

    def total(ref, at):
        out = ref[(0,) + at].astype(F32)
        for f in range(1, F):
            out += ref[(f,) + at].astype(F32)
        return out

    for name in ("q", "qb", "out"):
        getattr(t, name).finish()
        got, put = getattr(v, "r_" + name), getattr(v, "s_" + name)
        for k in range(put.shape[0]):
            put[k] = total(got, (k,)).astype(BF)
        getattr(t, name + "_home").start()
    for d in range(2, t.one.steps + 1):
        for op in late:
            op.step(d)
    t.gw.finish()

    @pl.loop(0, S)
    def _(k):
        v.s_gw[k] = total(v.r_gw, (k,)).astype(BF)

    t.gw_home.start()
    for op in late:
        op.finish()
    for name in ("one", "two", "three", "gu_a", "down_b"):
        getattr(v, "s_" + name)[...] = getattr(v, "f_" + name)[...].astype(BF)
        getattr(t, name + "_home").start()
    t.down.finish()
    v.g_down[...] = total(v.r_down, ())
    for name in ("grad_input", "activations", "q_home", "qb_home", "out_home", "gw_home"):
        getattr(t, name).finish()
    for name in ("one", "two", "three", "gu_a", "down_b"):
        getattr(t, name + "_home").finish()


def backward(given, dims, collective_id):
    S, F, R, seg, L, kb, rb, hb, ob = dims
    own = R * seg
    G = S // R
    C = G // HEADS
    qlen = L // C
    width = given["resid"].shape[1]
    per_head = S // HEADS
    hp2 = given["g_gw"].shape[3]
    lora = width + RANK
    one = 2 * HEAD + 3 * RANK
    two = 2 * HEAD + width
    low = functools.partial(jax.ShapeDtypeStruct, dtype=BF)
    full = functools.partial(jax.ShapeDtypeStruct, dtype=F32)

    def to_rows(at):
        return [(j, lax.rem(at, G) * R + j, at // G) for j in range(R)]

    def to_out(at):
        return [
            (j, lax.rem(at, G) // C * per_head + j, at // G * C + lax.rem(at, C)) for j in range(per_head)
        ]

    outs = {
        "act_home": low((R, seg, width)),
        "grad_home": full((R, seg, width)),
        "o_q": low((S, kb, HEAD)),
        "o_qb": low((S, rb, HEAD)),
        "o_out": low((R * C, ob, lora)),
        "o_gw": low((S, kb + rb, hp2)),
        "o_one": low((F, kb, one)),
        "o_two": low((F, rb, two)),
        "o_three": low((F, kb, 128)),
        "o_gu_a": low((F, kb, 2 * RANK)),
        "o_down_b": low((F, rb, width)),
        "g_down": full((hb, lora)),
    }
    scratch = {
        "d_resid": full((own, width)),
        "d_attn_own": low((own, width)),
        "d_attn": low((G, own, width)),
        "da": low((qlen, lora)),
        "d_mixed": low((qlen, HEAD)),
        "d_scores": low((qlen, L)),
        "probs_low": low((qlen, L)),
        "d_pu": low((L, 3 * HEAD + 3 * RANK)),
        "d_n1_sum": full((own, width)),
        "grad_rows": full((R, seg, width)),
        "act_rows": low((R, seg, width)),
        "ffn_sum": full((own, width)),
        "t_out": low((F, per_head, ob, lora)),
        "t_q": low((F, S, kb, HEAD)),
        "t_qb": low((F, S, rb, HEAD)),
        "t_1": low((S, F, kb, one)),
        "t_2": low((S, F, rb, two)),
        "t_3": low((S, F, kb, 128)),
        "r_out": low((F, per_head, ob, lora)),
        "r_q": low((F, S, kb, HEAD)),
        "r_qb": low((F, S, rb, HEAD)),
        "r_gw": low((F, S, kb + rb, hp2)),
        "r_down": low((F, hb, lora)),
        "s_out": low((per_head, ob, lora)),
        "s_q": low((S, kb, HEAD)),
        "s_qb": low((S, rb, HEAD)),
        "s_gw": low((S, kb + rb, hp2)),
    }
    for name, rows, cols in (
        ("one", kb, one),
        ("two", rb, two),
        ("three", kb, 128),
        ("gu_a", kb, 2 * RANK),
        ("down_b", rb, width),
    ):
        scratch["f_" + name] = full((F, rows, cols))
        scratch["s_" + name] = low((F, rows, cols))
    if "ffn_sum" in given:
        scratch.pop("ffn_sum")
    arrays = {**given, **outs, **scratch}

    def op(kind, src, dst, *more):
        return kind(arrays[src], *more), src, dst

    ops = {
        "gw": op(Direct, "g_gw", "r_gw", "fsdp", F),
        "down": op(Direct, "g_dw", "r_down", "fsdp", F),
        "d_attn": op(Line, "d_attn_own", "d_attn", G),
        "gu_a": op(LineSum, "g_gu_a", "f_gu_a", S),
        "down_b": op(LineSum, "g_down_b", "f_down_b", S),
        "d_n1": op(LineSum, "d_attn", "d_n1_sum", G),
        "out": op(Direct, "t_out", "r_out", "fsdp", F),
        "q": op(Direct, "t_q", "r_q", "fsdp", F),
        "qb": op(Direct, "t_qb", "r_qb", "fsdp", F),
        "one": op(LineSum, "t_1", "f_one", S),
        "two": op(LineSum, "t_2", "f_two", S),
        "three": op(LineSum, "t_3", "f_three", S),
        "grad_input": op(Post, "grad_rows", "grad_home", R, to_rows),
        "activations": op(Post, "act_rows", "act_home", R, to_rows),
        "q_home": op(Direct, "s_q", "o_q", "seq", S),
        "qb_home": op(Direct, "s_qb", "o_qb", "seq", S),
        "out_home": op(Post, "s_out", "o_out", R * C, to_out),
        "gw_home": op(Direct, "s_gw", "o_gw", "seq", S),
    }
    if "ffn_part" in given:
        ops["ffn"] = op(LineSum, "ffn_part", "ffn_sum", S)
    for name in ("one", "two", "three", "gu_a", "down_b"):
        ops[name + "_home"] = op(Direct, "s_" + name, "o_" + name, "fsdp", F)
    vmem = pl.BlockSpec(memory_space=pltpu.VMEM)
    away = pl.BlockSpec(memory_space=pl.ANY)
    names = list(given) + list(outs) + list(scratch)
    result = pl.pallas_call(
        functools.partial(back_kernel, dims, names, ops),
        out_shape=list(outs.values()),
        in_specs=[away if name in ("g_gw", "g_dw") else vmem for name in given],
        out_specs=[vmem if name == "g_down" else away for name in outs],
        scratch_shapes=[pltpu.VMEM(a.shape, a.dtype) for a in scratch.values()]
        + [entry for kind, _, _ in ops.values() for entry in kind.scratch],
        compiler_params=pltpu.CompilerParams(
            collective_id=collective_id, has_side_effects=True, vmem_limit_bytes=62 << 20
        ),
    )(*given.values())
    return dict(zip(outs, result))


def norm_apply(hidden, gain):
    return hidden * lax.rsqrt(jnp.mean(hidden * hidden, axis=-1, keepdims=True) + EPSILON) * gain


def rope_tables(positions):
    half = HEAD // 2
    spacing = jnp.exp(-(2.0 * jnp.arange(half).astype(F32) / HEAD) * math.log(ROPE_BASE))
    angle = positions.astype(F32)[..., None] * spacing
    return jnp.cos(angle), jnp.sin(angle)


def rotate(values, cosine, sine):
    half = values.shape[-1] // 2
    a, b = values[..., :half], values[..., half:]
    return jnp.concatenate([a * cosine - b * sine, b * cosine + a * sine], axis=-1)


def unrotate(grads, cosine, sine):
    half = grads.shape[-1] // 2
    a, b = grads[..., :half], grads[..., half:]
    return jnp.concatenate([a * cosine + b * sine, b * cosine - a * sine], axis=-1)


def shards(
    S,
    F,
    layer_input,
    document_numbers,
    cotangent,
    w_qkv,
    qkv_a,
    q_b,
    kv_b,
    w_out,
    out_a,
    out_b,
    w_gu,
    gu_a,
    gu_b,
    w_down,
    down_a,
    down_b,
    gain_a,
    gain_f,
):
    R, seg, width = layer_input.shape
    L = seg * S
    own = R * seg
    G = S // R
    C = G // HEADS
    scale = HEAD**-0.5
    kb = w_qkv.shape[0]
    rb = q_b.shape[0]
    hb = w_down.shape[0]
    ob = w_out.shape[0]
    hidden = w_gu.shape[1] // 2
    hl = hidden // S
    hp = (hl + 127) // 128 * 128
    s = lax.axis_index("seq")
    r = s // G
    head = lax.rem(s, G) // C
    chunk = lax.rem(s, C)
    qlen = L // C

    on_seq, on_fsdp = ("seq", S), ("fsdp", F)
    per_head = S // HEADS
    gains = jnp.pad(jnp.stack([gain_a, gain_f], axis=1), ((0, 0), (0, 126)))
    pack1 = jnp.concatenate([w_qkv, qkv_a, gains], axis=1)
    pack2 = jnp.concatenate([q_b, kv_b[0], kv_b[1], out_b], axis=1)
    pack3 = jnp.concatenate([w_out, out_a], axis=1)

    def shares(w):
        w = w.reshape(w.shape[0], 2, S, hl).transpose(2, 0, 1, 3)
        return jnp.pad(w, ((0, 0), (0, 0), (0, 0), (0, hp - hl))).reshape(S, w.shape[1], 2 * hp)

    gw = shares(jnp.concatenate([w_gu, jnp.concatenate([gu_b[0], gu_b[1]], axis=1)], axis=0))
    p1, p2, p3, gw, f_gu_a, f_down_b = transfer(
        [Direct(x, "fsdp", F, True) for x in (pack1, pack2, pack3)]
        + [Direct(gw, "seq", S)]
        + [Direct(x, "fsdp", F, True) for x in (gu_a, down_b)],
        [on_seq, on_fsdp],
        0,
    )
    dw = jnp.concatenate([w_down, down_a], axis=1)
    gw = lax.all_gather(gw, "fsdp", axis=1)
    dw = lax.all_gather(dw, "fsdp", axis=0)
    cot = lax.all_gather(cotangent.reshape(own, width), "seq", axis=0)
    f_gu_a = lax.all_gather(f_gu_a, "seq", axis=0)
    f_down_b = lax.all_gather(f_down_b, "seq", axis=0).reshape(RANK, width)
    ids = jnp.pad(document_numbers[:, None, :], ((0, 0), (0, 7), (0, 128 - seg)))

    def to_head(at):
        return [(0, row * G + at // per_head * C + c, lax.rem(at, per_head)) for row in range(R) for c in range(C)]

    p1, p2, xin, ids, wo = transfer(
        [Line(p1, S), Line(p2, S), Line(layer_input, S), Line(ids, S), Post(p3[None], per_head, to_head)],
        [on_seq],
        1,
    )
    p1 = p1.reshape(width, -1)
    p2 = p2.reshape(RANK, -1)
    wo = wo.reshape(HEAD, -1)
    xrow = lax.dynamic_index_in_dim(xin, r, 1, keepdims=False).reshape(L, width).astype(F32)
    ids = lax.dynamic_index_in_dim(ids[:, :, 0, :seg], r, 1, keepdims=False).reshape(L)
    q0 = HEADS * HEAD
    wq = lax.dynamic_slice_in_dim(p1, head * HEAD, HEAD, 1)
    w1 = jnp.concatenate([wq, p1[:, q0 : q0 + 2 * HEAD + 3 * RANK]], axis=1)
    at = q0 + 2 * HEAD + 3 * RANK
    gain_one = p1[:, at].astype(F32)
    gain_two = p1[:, at + 1].astype(F32)
    f_q_b = lax.dynamic_slice_in_dim(p2, head * HEAD, HEAD, 1)
    f_k_b = p2[:, q0 : q0 + HEAD]
    f_v_b = p2[:, q0 + HEAD : q0 + 2 * HEAD]
    f_out_b = p2[:, q0 + 2 * HEAD : q0 + 2 * HEAD + width]

    place = jnp.arange(L, dtype=jnp.int32)
    same = ids[:, None] == ids[None, :]
    before = place[None, :] < place[:, None]
    positions = jnp.sum((same & before).astype(jnp.int32), axis=1)
    allowed = same & (place[None, :] <= place[:, None])
    cosine, sine = rope_tables(positions)
    norm_one = norm_apply(xrow, gain_one).astype(BF)
    pu = mm(norm_one, w1)
    u = pu[:, 3 * HEAD :].astype(BF)
    u_q, u_k, u_v = u[:, :RANK], u[:, RANK : 2 * RANK], u[:, 2 * RANK :]
    query = rotate(pu[:, :HEAD] + mm(u_q, f_q_b), cosine, sine).astype(BF)
    key = rotate(pu[:, HEAD : 2 * HEAD] + mm(u_k, f_k_b), cosine, sine).astype(BF)
    value = (pu[:, 2 * HEAD : 3 * HEAD] + mm(u_v, f_v_b)).astype(BF)
    if C > 1:
        query_c = lax.dynamic_slice_in_dim(query, chunk * qlen, qlen, 0)
        allowed = lax.dynamic_slice_in_dim(allowed, chunk * qlen, qlen, 0)
    else:
        query_c = query
    scores = jnp.where(allowed, mm_nt(query_c, key) * scale, MASKED)
    top = jnp.max(scores, axis=-1, keepdims=True)
    lse = top + jnp.log(jnp.sum(jnp.exp(scores - top), axis=-1, keepdims=True))
    probs = jnp.where(allowed, jnp.exp(scores - lse), 0.0)
    probs_low = probs.astype(BF)
    mixed = mm(probs_low, value).astype(BF)
    part = mm(mixed, wo).astype(BF)
    if C > 1:
        part = lax.dynamic_update_slice_in_dim(jnp.zeros((L, part.shape[1]), BF), part, chunk * qlen, 0)
    (attn,) = transfer([LineSum(part.reshape(G, own, -1), G)], [on_seq], 4)
    u_out = attn[:, width:].astype(BF)
    mine = lax.rem(s, G) * own
    x_own = lax.dynamic_slice_in_dim(xrow, mine, own, 0)
    resid = x_own + attn[:, :width] + mm(u_out, f_out_b)
    norm_two_own = norm_apply(resid, gain_two).astype(BF)

    dims = (S, F, R, seg, kb, rb, hb, hl, hp)
    d_norm_two, ffn, g_gu, g_down, g_gu_a, g_down_b = feed_forward(
        norm_two_own, gw, dw, cot, f_gu_a, f_down_b, dims, 5
    )
    cot_own = lax.dynamic_slice_in_dim(cot, lax.rem(s, G) * R, R, 0).reshape(R, R, seg, width)
    cot_own = lax.dynamic_index_in_dim(cot_own, r, 1, keepdims=False).reshape(own, width)

    ffn = {"ffn_part": ffn}
    if S * own > 1024:
        ffn = {"ffn_sum": transfer([LineSum(ffn["ffn_part"], S)], [on_seq], 7)[0]}
    got = backward(
        dict(
            d_n2=d_norm_two,
            resid=resid,
            gains=jnp.pad(jnp.stack([gain_one, gain_two]), ((0, 6), (0, 0))),
            cot_own=cot_own,
            x_own=x_own.astype(BF),
            out_b=f_out_b,
            wo=wo,
            w1=w1,
            up_b=jnp.stack([f_q_b, f_k_b, f_v_b]),
            norm_one=norm_one,
            u=u,
            u_out=u_out,
            query=query_c,
            key=key,
            value=value,
            cosine=cosine,
            sine=sine,
            probs=probs,
            mixed=mixed,
            **ffn,
            g_gw=g_gu,
            g_dw=g_down,
            g_gu_a=g_gu_a,
            g_down_b=g_down_b.reshape(S, F, rb, width),
        ),
        (S, F, R, seg, L, kb, rb, hb, ob),
        8,
    )

    def total(t):
        return jnp.sum(t.astype(F32), axis=0)

    def by_head(t):
        t = t.astype(F32).reshape(R, HEADS, C, t.shape[1], HEAD).sum(axis=(0, 2))
        return t.transpose(1, 0, 2).reshape(t.shape[1], HEADS * HEAD)

    def halves(t):
        rows = t.shape[1]
        t = t.astype(F32).reshape(S, rows, 2, hp)[..., :hl].transpose(2, 1, 0, 3)
        return t.reshape(2, rows, hidden)

    t_1, t_2, t_3, g_out = (total(got[name]) for name in ("o_one", "o_two", "o_three", "o_out"))
    g_gu = halves(got["o_gw"][:, :kb])
    g_down = got["g_down"]
    return (
        got["act_home"],
        got["grad_home"],
        jnp.concatenate([by_head(got["o_q"]), t_1[:, : 2 * HEAD]], axis=1),
        t_1[:, 2 * HEAD :],
        by_head(got["o_qb"]),
        jnp.stack([t_2[:, :HEAD], t_2[:, HEAD : 2 * HEAD]]),
        g_out[:, :width],
        g_out[:, width:],
        t_2[:, 2 * HEAD :],
        jnp.concatenate([g_gu[0], g_gu[1]], axis=1),
        total(got["o_gu_a"]),
        halves(got["o_gw"][:, kb:]),
        g_down[:, :width],
        g_down[:, width:],
        total(got["o_down_b"]),
        t_3[:, 0],
        t_3[:, 1],
    )


def solution(mesh):
    both = P(("seq", "fsdp"), None)
    second = P(None, ("seq", "fsdp"), None)
    tokens = P("fsdp", "seq", None)
    gain = P(("seq", "fsdp"))
    return jax.shard_map(
        functools.partial(shards, mesh.shape["seq"], mesh.shape["fsdp"]),
        mesh=mesh,
        in_specs=(tokens, P("fsdp", "seq"), tokens)
        + (both, both, both, second, both, both, both, both, both, second, both, both, both, gain, gain),
        out_specs=(tokens, tokens)
        + (both, both, both, second, both, both, both, both, both, second, both, both, both, gain, gain),
        check_vma=False,
    )
```

```python
import functools
import math

import jax
import jax.numpy as jnp
from jax import lax
from jax.experimental import pallas as pl
from jax.experimental.pallas import tpu as pltpu
from jax.sharding import PartitionSpec as P

HEADS = 4
HEAD = 256
RANK = 256
EPSILON = 1e-06
ROPE_BASE = 10000.0
MASKED = -1e30
FFN = "ffn"
ROWS = tuple("abcdefgh")
MESH = pl.DeviceIdType.MESH
BF = jnp.bfloat16
F32 = jnp.float32


def mm(left, right):
    return jnp.dot(left, right, preferred_element_type=F32)


def mm_tn(left, right):
    return lax.dot_general(left, right, (((0,), (0,)), ((), ())), preferred_element_type=F32)


def mm_nt(left, right):
    return lax.dot_general(left, right, (((1,), (1,)), ((), ())), preferred_element_type=F32)


def remote(src, dst, send, recv, peer):
    return pltpu.make_async_remote_copy(
        src_ref=src, dst_ref=dst, send_sem=send, recv_sem=recv, device_id=peer, device_id_type=MESH
    )


class Bag:
    def __init__(self, entries=()):
        self.__dict__.update(entries)


class Slot(jax.ShapeDtypeStruct):
    pass


def named(*groups):
    slots = {}
    for group in groups:
        for name, a in group.items():
            slots[name] = Slot(a.shape, a.dtype)
    return slots


def unpack(slots, ops, refs):
    refs = list(refs)
    where = {id(slot): ref for slot, ref in zip(slots.values(), refs)}
    v = Bag(zip(slots, refs))
    rest = refs[len(slots) :]
    bound = Bag()
    for name, (op, src, dst) in ops.items():
        take = len(op.scratch)
        src, dst = (
            where[id(x[0])].at[x[1]] if isinstance(x, tuple) else where[id(x)] for x in (src, dst)
        )
        op.bind(src, dst, *rest[:take])
        setattr(bound, name, op)
        rest = rest[take:]
    return v, bound


class Direct:
    steps = 0

    def relay(self):
        pass

    def __init__(self, x, axis, size, spread=False):
        self.x, self.axis, self.size, self.spread = x, axis, size, spread
        shape = ((size,) if spread else ()) + x.shape
        self.out = jax.ShapeDtypeStruct(shape, x.dtype)
        self.scratch = [
            pltpu.SemaphoreType.DMA,
            pltpu.SemaphoreType.DMA((size,)),
            pltpu.SemaphoreType.DMA((size,)),
        ]

    def bind(self, x_ref, o_ref, local, send, recv):
        me = lax.axis_index(self.axis)
        self.copies = []
        for k in range(1, self.size):
            peer = lax.rem(me + k, self.size)
            src = x_ref if self.spread else x_ref.at[peer]
            self.copies.append(remote(src, o_ref.at[me], send.at[k], recv.at[k], {self.axis: peer}))
        src = x_ref if self.spread else x_ref.at[me]
        self.copies.append(pltpu.make_async_copy(src, o_ref.at[me], local))

    def start(self):
        for copy in self.copies:
            copy.start()

    def finish(self):
        for copy in self.copies:
            copy.wait()


class Square:
    steps = 0

    def __init__(self, x, dim):
        self.x = x
        size = x.shape[dim]
        half = size // 2 if dim == 0 else size // 256 * 128
        first = (slice(None),) * dim
        self.cut = (first + (pl.ds(0, half),), first + (pl.ds(half, size - half),))
        self.out = jax.ShapeDtypeStruct((4,) + x.shape, x.dtype)
        self.scratch = [
            pltpu.SemaphoreType.DMA,
            pltpu.SemaphoreType.DMA((3, 2)),
            pltpu.SemaphoreType.DMA((3, 2)),
        ]

    def bind(self, x_ref, o_ref, local, send, recv):
        me = lax.axis_index("fsdp")
        near_x, near_y, far = me + 1 - 2 * lax.rem(me, 2), lax.rem(me + 2, 4), 3 - me
        cut = self.cut

        def move(src, owner, part, way, peer):
            dst = o_ref.at[owner].at[cut[part]]
            src = dst if src is None else src.at[cut[part]]
            return remote(src, dst, send.at[way, part], recv.at[way, part], {"fsdp": peer})

        self.to_x = [move(x_ref, me, part, 0, near_x) for part in range(2)]
        self.to_y = [move(x_ref, me, part, 1, near_y) for part in range(2)]
        self.from_x = [move(None, near_x, part, 0, near_x) for part in range(2)]
        self.from_y = [move(None, near_y, part, 1, near_y) for part in range(2)]
        self.on_y = move(None, near_x, 0, 2, near_y)
        self.on_x = move(None, near_y, 1, 2, near_x)
        self.from_far = [move(None, far, part, 2, near_x) for part in range(2)]
        self.own = pltpu.make_async_copy(x_ref, o_ref.at[me], local)

    def start(self):
        self.to_x[0].start()
        self.to_y[1].start()
        self.to_x[1].start()
        self.to_y[0].start()
        self.own.start()

    def relay(self):
        self.from_x[0].wait_recv()
        self.on_y.start()
        self.from_y[1].wait_recv()
        self.on_x.start()

    def finish(self):
        self.from_x[1].wait_recv()
        self.from_y[0].wait_recv()
        for part in range(2):
            self.from_far[part].wait_recv()
            self.to_x[part].wait_send()
            self.to_y[part].wait_send()
        self.on_y.wait_send()
        self.on_x.wait_send()
        self.own.wait()


class Post:
    steps = 0

    def __init__(self, x, slots, sends):
        self.slots, self.sends = slots, sends
        self.x = x
        count = len(sends(0))
        self.scratch = [
            pltpu.SemaphoreType.DMA((count,)),
            pltpu.SemaphoreType.DMA((count,)),
            pltpu.SemaphoreType.DMA((slots,)),
        ]

    def bind(self, x_ref, o_ref, local, send, recv):
        s = lax.axis_index("seq")
        self.s = s
        self.plan = []
        for k, (block, device, slot) in enumerate(self.sends(s)):
            src = x_ref if block is None else x_ref.at[block]
            away = remote(src, o_ref.at[slot], send.at[k], recv.at[slot], {"seq": device})
            here = pltpu.make_async_copy(src, o_ref.at[slot], recv.at[slot])
            self.plan.append((device, away, here))
        self.arrive = [
            pltpu.make_async_copy(o_ref.at[k], o_ref.at[k], recv.at[k]) for k in range(self.slots)
        ]

    def start(self):
        for device, away, here in self.plan:
            pl.when(device != self.s)(away.start)
            pl.when(device == self.s)(here.start)

    def finish(self):
        for copy in self.arrive:
            copy.wait()
        for device, away, here in self.plan:
            pl.when(device != self.s)(away.wait_send)


class Line:
    def __init__(self, x, line, span=None):
        self.x, self.line = x, line
        self.lo, self.hi = span or (0, line // 2)
        self.steps = line // 2 - 1
        self.out = jax.ShapeDtypeStruct((line,) + x.shape, x.dtype)
        self.scratch = [
            pltpu.SemaphoreType.DMA,
            pltpu.SemaphoreType.DMA((2 * line,)),
            pltpu.SemaphoreType.DMA((line,)),
        ]

    def bind(self, x_ref, o_ref, local, send, recv):
        self.x_ref, self.o_ref, self.send, self.recv = x_ref, o_ref, send, recv
        line = self.line
        s = lax.axis_index("seq")
        base = s // line * line
        self.n2 = line // 2
        self.i = s - base
        self.p, self.core = self.i // 2, lax.rem(self.i, 2)
        self.sib = s + 1 - 2 * self.core
        self.left = base + lax.rem(self.i + line - 2, line)
        self.right = base + lax.rem(self.i + 2, line)
        self.own = pltpu.make_async_copy(x_ref, o_ref.at[self.i], local)
        self.inside = (self.p >= self.lo) & (self.p < self.hi)

    def copy(self, blk, src, dst, k):
        return remote(src, self.o_ref.at[blk], self.send.at[k], self.recv.at[blk], {"seq": dst})

    def start(self):
        @pl.when(self.p + 1 < self.hi)
        def _():
            self.copy(self.i, self.x_ref, self.right, 0).start()

        @pl.when(self.p > self.lo)
        def _():
            self.copy(self.i, self.x_ref, self.left, 1).start()

        @pl.when(self.inside)
        def _():
            self.copy(self.i, self.x_ref, self.sib, 2).start()

        self.own.start()

    def step(self, d):
        p, n2, o = self.p, self.n2, self.o_ref

        @pl.when((p - d >= 0) & (p < self.hi))
        def _():
            blk = self.i - 2 * d
            self.copy(blk, o.at[blk], self.left, 0).wait_recv()

            @pl.when(p + 1 < self.hi)
            def _():
                self.copy(blk, o.at[blk], self.right, 4 * d).start()

            @pl.when(self.inside)
            def _():
                self.copy(blk, o.at[blk], self.sib, 4 * d + 1).start()

        @pl.when((p + d < n2) & (p >= self.lo))
        def _():
            blk = self.i + 2 * d
            self.copy(blk, o.at[blk], self.right, 0).wait_recv()

            @pl.when(p > self.lo)
            def _():
                self.copy(blk, o.at[blk], self.left, 4 * d + 2).start()

            @pl.when(self.inside)
            def _():
                self.copy(blk, o.at[blk], self.sib, 4 * d + 3).start()

    def finish(self):
        p, n2, o = self.p, self.n2, self.o_ref

        def sent(k, sure):
            @pl.when(sure)
            def _():
                self.copy(self.i, self.x_ref, self.sib, k).wait_send()

        @pl.when(self.inside)
        def _():
            for q in range(n2):
                blk = 2 * q + 1 - self.core
                self.copy(blk, o.at[blk], self.sib, 0).wait_recv()

        sent(0, p + 1 < self.hi)
        sent(1, p > self.lo)
        sent(2, self.inside)
        for d in range(1, n2):
            sent(4 * d, (p - d >= 0) & (p + 1 < self.hi))
            sent(4 * d + 1, (p - d >= 0) & self.inside)
            sent(4 * d + 2, (p + d < n2) & (p > self.lo))
            sent(4 * d + 3, (p + d < n2) & self.inside)
        self.own.wait()


class Grid:
    def __init__(self, x, S, F):
        self.x, self.S, self.F = x, S, F
        self.n2 = n2 = S // 2
        self.steps = n2 - 1
        self.out = jax.ShapeDtypeStruct((S, F) + x.shape, x.dtype)
        self.scratch = [
            pltpu.SemaphoreType.DMA,
            pltpu.SemaphoreType.DMA((2, n2)),
            pltpu.SemaphoreType.DMA((n2, F)),
            pltpu.SemaphoreType.DMA((n2, F)),
            pltpu.SemaphoreType.DMA((S, F)),
        ]

    def bind(self, x_ref, o_ref, local, z_send, f_send, s_send, recv):
        self.x_ref, self.o_ref, self.recv = x_ref, o_ref, recv
        self.z_send, self.f_send, self.s_send = z_send, f_send, s_send
        s, self.f = lax.axis_index("seq"), lax.axis_index("fsdp")
        self.p, self.core = s // 2, lax.rem(s, 2)
        self.s = s
        self.sib = {"seq": s + 1 - 2 * self.core}
        self.left = {"seq": lax.rem(s + self.S - 2, self.S)}
        self.right = {"seq": lax.rem(s + 2, self.S)}
        self.own = pltpu.make_async_copy(x_ref, o_ref.at[s, self.f], local)
        self.square = self.F == 4
        self.near = (1, 2) if self.square else range(1, self.F)

    def place(self, k):
        f = self.f
        if self.square:
            return (f, f + 1 - 2 * lax.rem(f, 2), lax.rem(f + 2, 4), 3 - f)[k]
        return lax.rem(f + self.F - k, self.F)

    def peer(self, k):
        return {"fsdp": self.place(k) if self.square else lax.rem(self.f + k, self.F)}

    def copy(self, q, f, send, peer):
        blk = 2 * q + self.core
        dst = self.o_ref.at[blk, f]
        return remote(dst, dst, send, self.recv.at[blk, f], peer)

    def first(self, send, peer):
        return remote(self.x_ref, self.o_ref.at[self.s, self.f], send, self.recv.at[self.s, self.f], peer)

    def start(self):
        p, n2 = self.p, self.n2

        @pl.when(p < n2 - 1)
        def _():
            self.first(self.z_send.at[0, p], self.right).start()

        @pl.when(p > 0)
        def _():
            self.first(self.z_send.at[1, p], self.left).start()

        for k in self.near:
            self.first(self.f_send.at[p, k], self.peer(k)).start()
        self.first(self.s_send.at[p, 0], self.sib).start()
        self.own.start()

    def pass_on(self, q):
        for k in self.near:
            self.copy(q, self.f, self.f_send.at[q, k], self.peer(k)).start()
        self.copy(q, self.f, self.s_send.at[q, 0], self.sib).start()

    def arrived(self, q, f):
        self.copy(q, f, self.s_send.at[q, 0], self.sib).wait_recv()

    def step(self, d):
        p, n2 = self.p, self.n2

        @pl.when(p - d >= 0)
        def _():
            self.arrived(p - d, self.f)

            @pl.when(p < n2 - 1)
            def _():
                self.copy(p - d, self.f, self.z_send.at[0, p - d], self.right).start()

            self.pass_on(p - d)

        @pl.when(p + d < n2)
        def _():
            self.arrived(p + d, self.f)

            @pl.when(p > 0)
            def _():
                self.copy(p + d, self.f, self.z_send.at[1, p + d], self.left).start()

            self.pass_on(p + d)

    def relay(self, k):
        f = self.place(k)
        for q in range(self.n2):
            self.arrived(q, f)
            self.copy(q, f, self.s_send.at[q, k], self.sib).start()
            if self.square and ((k == 1 and q < self.n2 // 2) or (k == 2 and q >= self.n2 // 2)):
                self.copy(q, f, self.f_send.at[q, 3], self.peer(3 - k)).start()

    def finish(self):
        p, n2 = self.p, self.n2
        for q in range(n2):
            for k in range(self.F):
                f = self.place(k)
                blk = 2 * q + 1 - self.core
                dst = self.o_ref.at[blk, f]
                remote(dst, dst, self.s_send.at[q, k], self.recv.at[blk, f], self.sib).wait_recv()
        for q in range(n2):

            @pl.when((q <= p) & (p < n2 - 1))
            def _():
                self.first(self.z_send.at[0, q], self.right).wait_send()

            @pl.when((q >= p) & (p > 0))
            def _():
                self.first(self.z_send.at[1, q], self.left).wait_send()

            for k in range(self.F):
                self.first(self.s_send.at[q, k], self.sib).wait_send()
                if k:
                    self.first(self.f_send.at[q, k], self.sib).wait_send()
        self.own.wait()


class LineSum:
    vmem = True

    def __init__(self, x, line):
        self.x, self.line = x, line
        self.n2 = n2 = line // 2
        self.steps = n2 - 1
        blk = x.shape[1:]
        self.out = jax.ShapeDtypeStruct(blk, F32)
        self.scratch = [pltpu.VMEM((n2,) + blk, BF), pltpu.VMEM((n2 + 1,) + blk, BF)] + [
            pltpu.SemaphoreType.DMA((3 * n2,)),
            pltpu.SemaphoreType.DMA((3 * n2,)),
        ]

    def bind(self, x_ref, o_ref, mine, came, send, recv):
        self.x_ref, self.o_ref, self.mine, self.came = x_ref, o_ref, mine, came
        line, n2 = self.line, self.n2
        s = lax.axis_index("seq")
        base = s // line * line
        i = s - base
        self.p, self.core = i // 2, lax.rem(i, 2)
        sib = {"seq": s + 1 - 2 * self.core}
        left = {"seq": base + lax.rem(i + line - 2, line)}
        right = {"seq": base + lax.rem(i + 2, line)}
        core = self.core
        self.hand_over = lambda q: remote(
            x_ref.at[2 * q + 1 - core], mine.at[q], send.at[q], recv.at[q], sib
        )
        self.rightward = lambda q: remote(
            mine.at[q], came.at[q + 1], send.at[n2 + q], recv.at[n2 + q], right
        )
        self.leftward = lambda q: remote(
            mine.at[q], came.at[q], send.at[2 * n2 + q], recv.at[2 * n2 + q], left
        )
        order = []
        for k in range((n2 + 1) // 2):
            order += [n2 - 1 - k] + ([k] if k != n2 - 1 - k else [])
        self.order = order

    def start(self):
        for q in self.order:
            self.hand_over(q).start()

    def add(self, q, other):
        self.mine[q] = (self.mine[q].astype(F32) + self.came[other].astype(F32)).astype(BF)

    def step(self, d):
        p, n2 = self.p, self.n2
        if d == 1:
            for q in self.order:
                self.hand_over(q).wait_recv()
                own = self.x_ref[2 * q + self.core].astype(F32)
                self.mine[q] = (own + self.mine[q].astype(F32)).astype(BF)

                @pl.when((q > p) & (p == 0))
                def _():
                    self.rightward(q).start()

                @pl.when((q < p) & (p == n2 - 1))
                def _():
                    self.leftward(q).start()

        q_right = n2 - d

        @pl.when((p > 0) & (p < q_right))
        def _():
            self.rightward(q_right).wait_recv()
            self.add(q_right, q_right + 1)
            self.rightward(q_right).start()

        q_left = d - 1

        @pl.when((p < n2 - 1) & (p > q_left))
        def _():
            self.leftward(q_left).wait_recv()
            self.add(q_left, q_left)
            self.leftward(q_left).start()

    def finish(self):
        p, n2 = self.p, self.n2
        for q in range(n2):

            @pl.when(p == q)
            def _():
                total = self.mine[q].astype(F32)
                if q > 0:
                    self.rightward(q).wait_recv()
                    total += self.came[q + 1].astype(F32)
                if q < n2 - 1:
                    self.leftward(q).wait_recv()
                    total += self.came[q].astype(F32)
                self.o_ref[...] = total

        for q in range(n2):
            self.hand_over(q).wait_send()

            @pl.when(q > p)
            def _():
                self.rightward(q).wait_send()

            @pl.when(q < p)
            def _():
                self.leftward(q).wait_send()


def transfer_kernel(ops, axes, *refs):
    count = len(ops)
    rest = list(refs[2 * count :])
    for a, op in enumerate(ops):
        take = len(op.scratch)
        op.bind(refs[a], refs[count + a], *rest[:take])
        rest = rest[take:]
    barrier = pltpu.get_barrier_semaphore()
    for axis, size in axes:
        me = lax.axis_index(axis)
        for k in range(1, size):
            peer = {axis: lax.rem(me + k, size)}
            pl.semaphore_signal(barrier, inc=1, device_id=peer, device_id_type=MESH)
    pl.semaphore_wait(barrier, sum(size - 1 for _, size in axes))
    for op in ops:
        op.start()
    for d in range(1, 1 + max(op.steps for op in ops)):
        for op in ops:
            if d <= op.steps:
                op.step(d)
    for op in ops:
        op.finish()


def transfer(ops, axes, collective_id):
    spaces = [
        pl.BlockSpec(memory_space=pltpu.VMEM if hasattr(op, "vmem") else pl.ANY) for op in ops
    ]
    return pl.pallas_call(
        functools.partial(transfer_kernel, ops, axes),
        out_shape=[op.out for op in ops],
        in_specs=spaces,
        out_specs=spaces,
        scratch_shapes=[entry for op in ops for entry in op.scratch],
        compiler_params=pltpu.CompilerParams(
            collective_id=collective_id, has_side_effects=True, vmem_limit_bytes=48 << 20
        ),
    )(*[op.x for op in ops])


def meet(axes):
    barrier = pltpu.get_barrier_semaphore()
    for axis, size in axes:
        me = lax.axis_index(axis)
        for k in range(1, size):
            peer = {axis: lax.rem(me + k, size)}
            pl.semaphore_signal(barrier, inc=1, device_id=peer, device_id_type=MESH)
    pl.semaphore_wait(barrier, sum(size - 1 for _, size in axes))


def ffn_kernel(dims, slots, ops, *refs):
    S, F, R, seg, kb, rb, hb, hl, hp = dims
    v, t = unpack(slots, ops, refs[2:])
    stage_sem, cot_sem = refs[:2]
    own = R * seg
    width = v.n2_own.shape[1]
    tokens = S * own
    G = S // R
    gather, scatter = t.n2, t.d_n2
    early = [t.gu_a, t.down_b, t.ffn] if hasattr(t, FFN) else []
    n2, gw, gb, dw, cot_u, gu_a, down_b = v.n2, v.w, v.gb, v.w_down, v.cot_u, v.w_gu_a, v.down_b
    u_gu, act, d_gu, d_u_gu = v.u_gu, v.act, v.d_gu, v.d_u_gu
    meet([("seq", S), ("fsdp", F)])
    gather.start()

    def fetch(s):
        return pltpu.make_async_copy(v.gw.at[:, s], v.stage.at[s % 2], stage_sem.at[s % 2])

    fetch(0).start()
    moves = []
    for j in range(S):
        row, i = j // G, j % G
        for e in range(R):
            at = j * own + e * seg
            src = v.cot.at[i * R + e, row]
            dst = cot_u.at[pl.ds(at, seg), pl.ds(0, width)]
            moves.append(pltpu.make_async_copy(src, dst, cot_sem.at[len(moves)]))
            moves[-1].start()

    for s in range(S):
        if s + 1 < S:
            fetch(s + 1).start()
        fetch(s).wait()
        for f in range(F):
            b = s * F + f
            gw[b * kb : b * kb + kb, :] = v.stage[s % 2, f, 0:kb, :]
            gb[b * rb : b * rb + rb, :] = v.stage[s % 2, f, kb : kb + rb, :]
            gu_a[b * kb : b * kb + kb, :] = v.gu_a[s, f]
        if s + 1 <= gather.steps:
            gather.step(s + 1)
    for move in moves:
        move.wait()
    tile = 256
    tiles = tokens // tile

    @pl.loop(0, tiles)
    def _(k):
        rows = pl.ds(pl.multiple_of(k * tile, tile), tile)
        cot_u[rows, width:] = mm_nt(cot_u[rows, :width], down_b[...]).astype(BF)

    for f in range(F):
        dw[f * hb : f * hb + hb, :] = v.dw[f]
    if hp > hl:
        dw[hl:hp, :] = jnp.zeros((hp - hl, dw.shape[1]), BF)
    gather.finish()
    inner = math.sqrt(2.0 / math.pi)
    per_tile = tile // own

    @pl.loop(0, tiles)
    def _(k):
        rows = pl.ds(pl.multiple_of(k * tile, tile), tile)
        n = n2[pl.ds(k * per_tile, per_tile)].reshape(tile, width)
        u = mm(n, gu_a[...]).astype(BF)
        u_gu[rows, :] = u
        d_act = mm_nt(cot_u[rows, :], dw[...])
        gate = mm(n, gw[:, :hp]) + mm(u[:, :RANK], gb[:, :hp])
        up = mm(n, gw[:, hp:]) + mm(u[:, RANK:], gb[:, hp:])
        square = gate * gate
        th = jnp.tanh(inner * gate * (1.0 + 0.044715 * square))
        half = 0.5 * (1.0 + th)
        gelu = gate * half
        act[rows, :] = (gelu * up).astype(BF)
        slope = half + 0.5 * gate * (1.0 - th * th) * (inner * (1.0 + 3 * 0.044715 * square))
        d_gate = (d_act * up * slope).astype(BF)
        d_up = (d_act * gelu).astype(BF)
        d_gu[rows, :hp] = d_gate
        d_gu[rows, hp:] = d_up
        d_u_gu[rows, :RANK] = mm_nt(d_gate, gb[:, :hp]).astype(BF)
        d_u_gu[rows, RANK:] = mm_nt(d_up, gb[:, hp:]).astype(BF)
        out = mm_nt(d_gu[rows, :], gw[...]) + mm_nt(d_u_gu[rows, :], gu_a[...])
        v.dn[pl.ds(k * per_tile, per_tile)] = out.astype(BF).reshape(per_tile, own, width)

    scatter.start()

    def gate_or_up(half, part, move):
        base = half * hp
        out = mm_tn(u_gu[:, half * RANK : half * RANK + RANK], d_gu[:, base : base + hp]).astype(BF)
        for b in range(S * F):
            part[b % F, b // F, kb : kb + rb, :] = out[b * rb : b * rb + rb, :]

        def columns(src, dst):
            out = mm_tn(n2[...].reshape(tokens, width), d_gu[:, src]).astype(BF)
            for b in range(S * F):
                part[b % F, b // F, 0:kb, dst] = out[b * kb : b * kb + kb, :]

        @pl.loop(0, hp // 256)
        def _(k):
            at = pl.multiple_of(k * 256, 128)
            columns(pl.ds(pl.multiple_of(base + at, 128), 256), pl.ds(at, 256))

        left = hp % 256
        if left:
            columns(slice(base + hp - left, base + hp), slice(hp - left, hp))
        move.start()

    gate_or_up(0, v.part_gate, t.gate)
    scatter.step(1)
    gate_or_up(1, v.part_up, t.up)
    if scatter.steps >= 2:
        scatter.step(2)

    @pl.loop(0, tiles)
    def _(k):
        rows = pl.ds(pl.multiple_of(k * tile, tile), tile)
        out = mm(act[rows, :], dw[...])
        low = out[:, width:].astype(BF)
        v.u_down[rows, :] = low
        out = out[:, :width] + mm(low, down_b[...])
        v.ffn_part[pl.ds(k * per_tile, per_tile)] = out.astype(BF).reshape(per_tile, own, width)

    for d in range(3, scatter.steps + 1):
        scatter.step(d)
    for op in early[2:]:
        op.start()
    scatter.finish()
    out = mm_tn(v.u_down[...], cot_u[:, :width]).astype(BF)
    for b in range(S * F):
        v.g_down_b[b // F, b % F] = out[b * rb : b * rb + rb, :]
    out = mm_tn(n2[...].reshape(tokens, width), d_u_gu[...]).astype(BF)
    for b in range(S * F):
        v.g_gu_a[b // F, b % F] = out[b * kb : b * kb + kb, :]
    for op in early[:2]:
        op.start()
    for op in early[2:] + early[:2]:
        op.step(1)
    step = 128

    @pl.loop(0, cot_u.shape[1] // step)
    def _(k):
        cols = pl.ds(pl.multiple_of(k * step, step), step)
        out = mm_tn(act[...], cot_u[:, cols]).astype(BF)
        for f in range(F):
            v.part_down[f, :, cols] = out[f * hb : f * hb + hb, :]

    for op in early:
        for d in range(2, op.steps + 1):
            op.step(d)
    for op in early:
        op.finish()

    for move, came, put in ((t.gate, v.came_gate, v.sum_gate), (t.up, v.came_up, v.sum_up)):

        def load(s):
            return pltpu.make_async_copy(
                came.at[:, s], v.stage.at[s % 2].at[:, :, pl.ds(0, hp)], stage_sem.at[s % 2]
            )

        move.finish()
        load(0).start()
        for s in range(S):
            if s + 1 < S:
                load(s + 1).start()
            load(s).wait()
            total = v.stage[s % 2, 0, :, :hp].astype(F32)
            for f in range(1, F):
                total += v.stage[s % 2, f, :, :hp].astype(F32)
            put[s] = total.astype(BF)


def over_fsdp(ref, at, F):
    out = ref[(0,) + at].astype(F32)
    for f in range(1, F):
        out += ref[(f,) + at].astype(F32)
    return out


def feed_forward(given, dims, apart, collective_id):
    S, F, R, seg, kb, rb, hb, hl, hp = dims
    g = Bag(given)
    own, width = g.n2_own.shape
    tokens = S * own
    low = functools.partial(jax.ShapeDtypeStruct, dtype=BF)
    full = functools.partial(jax.ShapeDtypeStruct, dtype=F32)
    lora = width + RANK
    outs = dict(
        dn_sum=full((own, width)),
        part_down=low((F, hb, lora)),
        sum_gate=low((S, kb + rb, hp)),
        sum_up=low((S, kb + rb, hp)),
        came_gate=low((F, S, kb + rb, hp)),
        came_up=low((F, S, kb + rb, hp)),
    )
    scratch = dict(
        n2=low((S, own, width)),
        w=low((width, 2 * hp)),
        gb=low((RANK, 2 * hp)),
        w_down=low((hp, lora)),
        cot_u=low((tokens, lora)),
        w_gu_a=low((width, 2 * RANK)),
        u_gu=low((tokens, 2 * RANK)),
        act=low((tokens, hp)),
        d_gu=low((tokens, 2 * hp)),
        d_u_gu=low((tokens, 2 * RANK)),
        u_down=low((tokens, RANK)),
        dn=low((S, own, width)),
        stage=low((2, F, kb + rb, 2 * hp)),
        part_gate=low((F, S, kb + rb, hp)),
        part_up=low((F, S, kb + rb, hp)),
    )
    parts = dict(
        ffn_part=low((S, own, width)),
        g_gu_a=low((S, F, kb, 2 * RANK)),
        g_down_b=low((S, F, rb, width)),
    )
    if apart:
        outs.update(parts)
    else:
        scratch.update(parts)
        outs.update(
            ffn_sum=full((own, width)),
            f_gu_a=full((F, kb, 2 * RANK)),
            f_down_b=full((F, rb, width)),
        )
    slots = named(given, outs, scratch)
    a = Bag(slots)

    def op(kind, src, dst, *more):
        return kind(src, *more), src, dst

    ops = dict(
        n2=op(Line, a.n2_own, a.n2, S),
        d_n2=op(LineSum, a.dn, a.dn_sum, S),
        gate=op(Direct, a.part_gate, a.came_gate, "fsdp", F),
        up=op(Direct, a.part_up, a.came_up, "fsdp", F),
    )
    if not apart:
        ops.update(
            ffn=op(LineSum, a.ffn_part, a.ffn_sum, S),
            gu_a=op(LineSum, a.g_gu_a, a.f_gu_a, S),
            down_b=op(LineSum, a.g_down_b, a.f_down_b, S),
        )
    vmem = pl.BlockSpec(memory_space=pltpu.VMEM)
    away = pl.BlockSpec(memory_space=pl.ANY)
    far = [id(x) for x in (a.gw, a.cot, a.came_gate, a.came_up)]

    def kernel(*refs):
        count = len(slots)
        ffn_kernel(dims, slots, ops, *refs[count : count + 2], *refs[:count], *refs[count + 2 :])

    result = pl.pallas_call(
        kernel,
        out_shape=list(outs.values()),
        in_specs=[away if id(slots[name]) in far else vmem for name in given],
        out_specs=[away if id(slots[name]) in far else vmem for name in outs],
        scratch_shapes=[pltpu.VMEM(x.shape, x.dtype) for x in scratch.values()]
        + [pltpu.SemaphoreType.DMA((2,)), pltpu.SemaphoreType.DMA((S * R,))]
        + [entry for kind, _, _ in ops.values() for entry in kind.scratch],
        compiler_params=pltpu.CompilerParams(
            collective_id=collective_id, has_side_effects=True, vmem_limit_bytes=62 << 20
        ),
    )(*given.values())
    return Bag(zip(outs, result))


def front_kernel(dims, slots, ops, *refs):
    S, F, R, seg, kb, rb, ob = dims
    v, t = unpack(slots, ops, refs)
    own = R * seg
    L = S * seg
    G = S // R
    C = G // HEADS
    qlen = L // C
    width = v.x.shape[2]
    scale = HEAD**-0.5
    s = lax.axis_index("seq")
    r = s // G
    head = lax.rem(s, G) // C
    chunk = lax.rem(s, C)
    meet([("seq", S), ("fsdp", F)])

    n_qkv, n_a, n_q = v.w_qkv.shape[1], v.qkv_a.shape[1], v.q_b.shape[1]
    v.p1[:, :n_qkv] = v.w_qkv[...]
    v.p1[:, n_qkv : n_qkv + n_a] = v.qkv_a[...]
    v.p1[:, n_qkv + n_a :] = v.gain_pair[...]
    t.one.start()
    v.p2[:, :n_q] = v.q_b[...]
    v.p2[:, n_q : n_q + HEAD] = v.kv_b[0]
    v.p2[:, n_q + HEAD : n_q + 2 * HEAD] = v.kv_b[1]
    v.p2[:, n_q + 2 * HEAD :] = v.add_out_b[...]
    t.two.start()
    rows_in = [getattr(t, ROWS[j]) for j in range(R)]
    for op in rows_in:
        op.start()
    t.ids.start()
    first = [t.one, t.two, t.ids] + rows_in
    v.p3[:, :width] = v.w_out[...]
    v.p3[:, width:] = v.out_a[...]
    t.three.start()
    hidden = v.w_gu.shape[1] // 2
    hl = hidden // S
    hp = v.gws.shape[2] // 2
    for half in range(2):
        for j in range(S):
            at = half * hidden + j * hl
            v.gws[j, 0:kb, half * hp : half * hp + hl] = v.w_gu[:, at : at + hl]
            v.gws[j, kb:, half * hp : half * hp + hl] = v.gu_b[half, :, j * hl : j * hl + hl]
            if hp > hl:
                v.gws[j, :, half * hp + hl : half * hp + hp] = jnp.zeros((kb + rb, hp - hl), BF)
    t.gw.start()
    v.dws[:, :width] = v.w_down[...]
    v.dws[:, width:] = v.down_a[...]
    later = [t.gu_a, t.down_b]
    for op in later:
        op.start()
    for d in range(1, t.one.steps + 1):
        for op in first:
            op.step(d)
    t.cot.start()
    t.three.finish()
    t.wo.start()
    t.ids.finish()

    for j in range(S):
        ids = jnp.where(r == 0, v.ids_all[j, 0:1, :], v.ids_all[j, 1:2, :])
        for row in range(2, R):
            ids = jnp.where(r == row, v.ids_all[j, row : row + 1, :], ids)
        v.id_row[:, j * seg : j * seg + seg] = ids.astype(F32)
    id_row = v.id_row[...]
    v.id_cols[...] = jnp.transpose(jnp.broadcast_to(id_row, (128, L)))
    lane = lax.broadcasted_iota(jnp.int32, (128, HEAD // 2), 1).astype(F32)
    spacing = jnp.exp(lane * (-2.0 / HEAD * math.log(ROPE_BASE)))
    places = lax.broadcasted_iota(jnp.int32, (128, L), 1)
    steps = lax.broadcasted_iota(jnp.int32, (128, L), 0)

    @pl.loop(0, L // 128)
    def _(i):
        rows = pl.ds(pl.multiple_of(i * 128, 128), 128)
        before = (v.id_cols[rows, 0:1] == id_row) & (places < steps + i * 128)
        position = jnp.sum(jnp.where(before, 1.0, 0.0), axis=1, keepdims=True)
        angle = position * spacing
        v.cosine[rows, :] = jnp.cos(angle)
        v.sine[rows, :] = jnp.sin(angle)

    for k in range(1, F):
        for op in (t.one, t.two):
            op.relay(k)
    t.dw.start()
    for d in range(1, t.gu_a.steps + 1):
        for op in later:
            op.step(d)
    t.gw.finish()
    t.gw_all.start()
    for op in (t.one, t.two):
        op.finish()
    for op in rows_in:
        op.finish()

    q_cols = pl.ds(pl.multiple_of(head * HEAD, HEAD), HEAD)
    rest_of = HEADS * HEAD
    wide = 2 * HEAD + 3 * RANK
    for j in range(S):
        for f in range(F):
            at = (j * F + f) * kb
            v.w1[at : at + kb, :HEAD] = v.p1_all[j, f, :, q_cols]
            v.w1[at : at + kb, HEAD:] = v.p1_all[j, f, :, rest_of : rest_of + wide]
            v.gain_cols[at : at + kb, :] = v.p1_all[j, f, :, rest_of + wide :].astype(F32)
            at = (j * F + f) * rb
            v.up_b[0, at : at + rb, :] = v.p2_all[j, f, :, q_cols]
            v.up_b[1, at : at + rb, :] = v.p2_all[j, f, :, rest_of : rest_of + HEAD]
            v.up_b[2, at : at + rb, :] = v.p2_all[j, f, :, rest_of + HEAD : rest_of + 2 * HEAD]
            v.out_b[at : at + rb, :] = v.p2_all[j, f, :, rest_of + 2 * HEAD :]
    v.gains[...] = jnp.transpose(v.gain_cols[...])[0:8, :]

    def norm(h, g):
        return (h * lax.rsqrt(jnp.mean(h * h, axis=-1, keepdims=True) + EPSILON) * g).astype(BF)

    for j in range(S):
        v.norm_one[j * seg : j * seg + seg, :] = norm(v.x_all[r, j].astype(F32), v.gains[0:1, :])
    mine = lax.rem(s, G) * R
    for e in range(R):
        v.x_own[e * seg : e * seg + seg, :] = v.x_all[r, mine + e]

    half = HEAD // 2

    @pl.loop(0, L // 256)
    def _(i):
        rows = pl.ds(pl.multiple_of(i * 256, 256), 256)
        pu = mm(v.norm_one[rows, :], v.w1[...])
        u = pu[:, 3 * HEAD :].astype(BF)
        v.u[rows, :] = u
        cosine, sine = v.cosine[rows, :], v.sine[rows, :]
        for k, ref in ((0, v.q_all), (1, v.key)):
            out = pu[:, k * HEAD : (k + 1) * HEAD] + mm(u[:, k * RANK : (k + 1) * RANK], v.up_b[k])
            a, b = out[:, :half], out[:, half:]
            ref[rows, :half] = (a * cosine - b * sine).astype(BF)
            ref[rows, half:] = (b * cosine + a * sine).astype(BF)
        out = pu[:, 2 * HEAD : 3 * HEAD] + mm(u[:, 2 * RANK :], v.up_b[2])
        v.value[rows, :] = out.astype(BF)

    t.cot.step(1)
    for k in range(1, F):
        for op in later:
            op.relay(k)
    t.wo.finish()
    for j in range(S // HEADS):
        for f in range(F):
            at = (j * F + f) * ob
            v.wo[at : at + ob, :] = v.wo_in[j, f]
    from_row = pl.multiple_of(chunk * qlen, own)
    v.query[...] = v.q_all[pl.ds(from_row, qlen), :]
    if C > 1:
        v.part[...] = jnp.zeros(v.part.shape, BF)

    @pl.loop(0, qlen // 128)
    def _(i):
        rows = pl.ds(pl.multiple_of(i * 128, 128), 128)
        here = pl.multiple_of(from_row + i * 128, own)
        allowed = (v.id_cols[pl.ds(here, 128), 0:1] == id_row) & (places <= steps + here)
        scores = jnp.where(allowed, mm_nt(v.query[rows, :], v.key[...]) * scale, MASKED)
        top = jnp.max(scores, axis=-1, keepdims=True)
        lse = top + jnp.log(jnp.sum(jnp.exp(scores - top), axis=-1, keepdims=True))
        probs = jnp.where(allowed, jnp.exp(scores - lse), 0.0)
        v.probs[rows, :] = probs
        mixed = mm(probs.astype(BF), v.value[...]).astype(BF)
        v.mixed[rows, :] = mixed
        out = mm(mixed, v.wo[...]).astype(BF)
        v.part[pl.ds(here // own, 128 // own)] = out.reshape(128 // own, own, out.shape[1])

    t.attn.start()
    t.gw_all.relay()
    t.dw.relay()
    for d in range(1, t.attn.steps + 1):
        t.attn.step(d)
    t.attn.finish()
    u_out = v.attn[:, width:].astype(BF)
    v.u_out[...] = u_out
    resid = v.x_own[...].astype(F32) + v.attn[:, :width] + mm(u_out, v.out_b[...])
    v.resid[...] = resid
    v.n2_own[...] = norm(resid, v.gains[1:2, :])

    for d in range(2, t.cot.steps + 1):
        t.cot.step(d)
    for op in later + [t.cot, t.gw_all, t.dw]:
        op.finish()


def forward(given, dims, collective_id):
    S, F, R, seg, kb, rb, ob = dims
    own = R * seg
    L = S * seg
    G = S // R
    C = G // HEADS
    qlen = L // C
    width = given["x"].shape[2]
    per_head = S // HEADS
    lora = width + RANK
    low = functools.partial(jax.ShapeDtypeStruct, dtype=BF)
    full = functools.partial(jax.ShapeDtypeStruct, dtype=F32)

    g = Bag(given)
    wide = g.w_qkv.shape[1] + g.qkv_a.shape[1] + 128
    thin = g.q_b.shape[1] + 2 * HEAD + width
    hb = g.w_down.shape[0]
    hp = (g.w_gu.shape[1] // 2 // S + 127) // 128 * 128

    def like(array, *lead):
        return jax.ShapeDtypeStruct(lead + array.shape, array.dtype)

    outs = dict(
        w1=low((width, 3 * HEAD + 3 * RANK)),
        norm_one=low((L, width)),
        u=low((L, 3 * RANK)),
        query=low((qlen, HEAD)),
        key=low((L, HEAD)),
        value=low((L, HEAD)),
        cosine=full((L, HEAD // 2)),
        sine=full((L, HEAD // 2)),
        probs=full((qlen, L)),
        mixed=low((qlen, HEAD)),
        u_out=low((own, RANK)),
        resid=full((own, width)),
        n2_own=low((own, width)),
        x_own=low((own, width)),
        gains=full((8, width)),
        out_b=low((RANK, width)),
        wo=low((HEAD, lora)),
        up_b=low((3, RANK, HEAD)),
        gw_all=low((F, S, kb + rb, 2 * hp)),
        dw_all=low((F, hb, lora)),
        cot_all=like(g.cot, S),
        gu_a_all=like(g.gu_a, S, F),
        down_b_all=like(g.down_b, S, F),
        gw_mid=low((S, kb + rb, 2 * hp)),
    )
    scratch = dict(
        p1=low((kb, wide)),
        p2=low((rb, thin)),
        p3=low((ob, lora)),
        gws=low((S, kb + rb, 2 * hp)),
        dws=low((hb, lora)),
        p1_all=low((S, F, kb, wide)),
        p2_all=low((S, F, rb, thin)),
        x_all=low((R, S, seg, width)),
        ids_all=like(g.ids, S),
        p3_all=low((F, ob, lora)),
        wo_in=low((per_head, F, ob, lora)),
        id_row=full((1, L)),
        id_cols=full((L, 128)),
        gain_cols=full((width, 128)),
        q_all=low((L, HEAD)),
        part=low((G, own, lora)),
        attn=full((own, lora)),
    )
    slots = named(given, outs, scratch)
    a = Bag(slots)

    far = [id(x) for x in (a.gw_all, a.dw_all, a.cot_all, a.gu_a_all, a.down_b_all, a.gw_mid)]
    far += [id(x) for x in (a.x, a.ids, a.cot, a.gu_a, a.down_b)]

    def to_head(at):
        return [
            (None, row * G + at // per_head * C + c, lax.rem(at, per_head))
            for row in range(R)
            for c in range(C)
        ]

    def op(kind, src, dst, *more):
        return kind(src, *more), src, dst

    ops = dict(
        one=op(Grid, a.p1, a.p1_all, S, F),
        two=op(Grid, a.p2, a.p2_all, S, F),
        ids=op(Line, a.ids, a.ids_all, S),
        three=op(Direct, a.p3, a.p3_all, "fsdp", F, True),
        wo=op(Post, a.p3_all, a.wo_in, per_head, to_head),
        gw=op(Direct, a.gws, a.gw_mid, "seq", S),
        dw=op(Square, a.dws, a.dw_all, 1) if F == 4 else op(Direct, a.dws, a.dw_all, "fsdp", F, True),
        gw_all=op(Square, a.gw_mid, a.gw_all, 0) if F == 4 else op(Direct, a.gw_mid, a.gw_all, "fsdp", F, True),
        cot=op(Line, a.cot, a.cot_all, S),
        gu_a=op(Grid, a.gu_a, a.gu_a_all, S, F),
        down_b=op(Grid, a.down_b, a.down_b_all, S, F),
        attn=op(LineSum, a.part, a.attn, G),
    )
    for j in range(R):
        span = (j * G // 2, (j + 1) * G // 2)
        ops[ROWS[j]] = Line(jax.ShapeDtypeStruct((seg, width), BF), S, span), (a.x, j), (a.x_all, j)
    vmem = pl.BlockSpec(memory_space=pltpu.VMEM)
    away = pl.BlockSpec(memory_space=pl.ANY)
    result = pl.pallas_call(
        functools.partial(front_kernel, dims, slots, ops),
        out_shape=list(outs.values()),
        in_specs=[away if id(slots[name]) in far else vmem for name in given],
        out_specs=[away if id(slots[name]) in far else vmem for name in outs],
        scratch_shapes=[pltpu.VMEM(a.shape, a.dtype) for a in scratch.values()]
        + [entry for kind, _, _ in ops.values() for entry in kind.scratch],
        compiler_params=pltpu.CompilerParams(
            collective_id=collective_id, has_side_effects=True, vmem_limit_bytes=62 << 20
        ),
    )(*given.values())
    return Bag(zip(outs, result))


def norm_back(G_in, h, g):
    q = lax.rsqrt(jnp.mean(h * h, axis=-1, keepdims=True) + EPSILON)
    gg = G_in * g
    d_gain = jnp.sum(G_in * (h * q), axis=0, keepdims=True)
    return d_gain, q * gg - h * (q * q * q) * jnp.mean(gg * h, axis=-1, keepdims=True)


def back_kernel(dims, slots, ops, *refs):
    S, F, R, seg, L, kb, rb, hb, ob = dims
    v, t = unpack(slots, ops, refs)
    own = R * seg
    G = S // R
    C = G // HEADS
    qlen = L // C
    width = v.resid.shape[1]
    scale = HEAD**-0.5
    s = lax.axis_index("seq")
    chunk = lax.rem(s, C)
    meet([("seq", S), ("fsdp", F)])
    t.down.start()

    gain_two, back = norm_back(v.d_n2[...], v.resid[...], v.gains[1:2, :])
    d_resid = v.cot_own[...].astype(F32) + back
    v.d_resid[...] = d_resid
    v.d_attn_own[...] = d_resid.astype(BF)
    t.d_attn.start()
    activations = (v.resid[...] + v.ffn_sum[...]).astype(BF)
    for j in range(R):
        v.act_rows[j] = activations[j * seg : j * seg + seg, :]
    t.activations.start()
    for put, got, home in ((v.s_gu_a, v.f_gu_a, t.gu_a_home), (v.s_down_b, v.f_down_b, t.down_b_home)):
        put[...] = got[...].astype(BF)
        home.start()
    t.gate_home.start()
    t.up_home.start()
    for d in range(1, t.d_attn.steps + 1):
        t.d_attn.step(d)
    t.d_attn.finish()

    blocks = qlen // own
    first = chunk * blocks
    v.da[:, :width] = v.d_attn[pl.ds(first, blocks)].reshape(qlen, width)
    v.da[:, width:] = mm_nt(v.da[:, :width], v.out_b[...]).astype(BF)
    v.d_mixed[...] = mm_nt(v.da[...], v.wo[...]).astype(BF)

    @pl.loop(0, qlen // 128)
    def _(i):
        rows = pl.ds(pl.multiple_of(i * 128, 128), 128)
        p = v.probs[rows, :]
        d_probs = mm_nt(v.d_mixed[rows, :], v.value[...])
        delta = jnp.sum(p * d_probs, axis=-1, keepdims=True)
        v.d_scores[rows, :] = (p * (d_probs - delta)).astype(BF)
        v.probs_low[rows, :] = p.astype(BF)

    def unrot(g, rows):
        half = HEAD // 2
        cosine, sine = v.cosine[rows, :], v.sine[rows, :]
        a, b = g[:, :half], g[:, half:]
        return (a * cosine + b * sine).astype(BF), (b * cosine - a * sine).astype(BF)

    half = HEAD // 2
    mine = pl.ds(pl.multiple_of(chunk * qlen, own), qlen)
    if C > 1:
        v.d_pu[:, :HEAD] = jnp.zeros((L, HEAD), BF)
    v.d_pu[mine, :half], v.d_pu[mine, half:HEAD] = unrot(mm(v.d_scores[...], v.key[...]) * scale, mine)
    every = pl.ds(0, L)
    v.d_pu[:, HEAD : HEAD + half], v.d_pu[:, HEAD + half : 2 * HEAD] = unrot(
        mm_tn(v.d_scores[...], v.query[...]) * scale, every
    )
    v.d_pu[:, 2 * HEAD : 3 * HEAD] = mm_tn(v.probs_low[...], v.d_mixed[...]).astype(BF)
    for k in range(3):
        v.d_pu[:, 3 * HEAD + k * RANK : 3 * HEAD + (k + 1) * RANK] = mm_nt(
            v.d_pu[:, k * HEAD : (k + 1) * HEAD], v.up_b[k]
        ).astype(BF)

    @pl.loop(0, L // 256)
    def _(i):
        rows = pl.ds(pl.multiple_of(i * 256, 256), 256)
        out = mm_nt(v.d_pu[rows, :], v.w1[...]).astype(BF)
        v.d_attn[pl.ds(i * (256 // own), 256 // own)] = out.reshape(256 // own, own, width)

    t.d_n1.start()

    out = mm_tn(v.mixed[...], v.da[...]).astype(BF)
    for j in range(HEAD // ob):
        v.t_out[j % F, j // F] = out[j * ob : j * ob + ob, :]
    t.out.start()
    out = mm_tn(v.norm_one[...], v.d_pu[:, :HEAD]).astype(BF)
    for b in range(S * F):
        v.t_q[b % F, b // F] = out[b * kb : b * kb + kb, :]
    t.q.start()
    out = mm_tn(v.u[:, :RANK], v.d_pu[:, :HEAD]).astype(BF)
    for b in range(S * F):
        v.t_qb[b % F, b // F] = out[b * rb : b * rb + rb, :]
    t.qb.start()
    t.d_n1.step(1)

    @pl.loop(0, v.t_1.shape[3] // 256)
    def _(i):
        cols = pl.ds(pl.multiple_of(i * 256, 256), 256)
        src = pl.ds(pl.multiple_of(i * 256 + 256, 256), 256)
        out = mm_tn(v.norm_one[...], v.d_pu[:, src]).astype(BF)
        for b in range(S * F):
            v.t_1[b // F, b % F, :, cols] = out[b * kb : b * kb + kb, :]

    t.one.start()
    for d in range(2, t.d_n1.steps + 1):
        t.d_n1.step(d)
    for k in range(2):
        out = mm_tn(
            v.u[:, (k + 1) * RANK : (k + 2) * RANK], v.d_pu[:, (k + 1) * HEAD : (k + 2) * HEAD]
        ).astype(BF)
        for b in range(S * F):
            v.t_2[b // F, b % F, :, k * HEAD : (k + 1) * HEAD] = out[b * rb : b * rb + rb, :]
    out = mm_tn(v.u_out[...], v.d_attn_own[...]).astype(BF)
    for b in range(S * F):
        v.t_2[b // F, b % F, :, 2 * HEAD :] = out[b * rb : b * rb + rb, :]
    t.two.start()

    t.d_n1.finish()
    gain_one, back = norm_back(v.d_n1_sum[...], v.x_own[...].astype(F32), v.gains[0:1, :])
    grad_input = v.d_resid[...] + back
    for j in range(R):
        v.grad_rows[j] = grad_input[j * seg : j * seg + seg, :]
    t.grad_input.start()
    both = jnp.concatenate([gain_one, gain_two, jnp.zeros((126, width), F32)], axis=0)
    both = jnp.transpose(both)
    for b in range(S * F):
        v.t_3[b // F, b % F] = both[b * kb : b * kb + kb, :].astype(BF)
    t.three.start()
    late = [t.one, t.two, t.three]
    for op in late:
        op.step(1)
    for move, got, put, home in (
        (t.q, v.r_q, v.s_q, t.q_home),
        (t.qb, v.r_qb, v.s_qb, t.qb_home),
        (t.out, v.r_out, v.s_out, t.out_home),
    ):
        move.finish()
        for k in range(put.shape[0]):
            put[k] = over_fsdp(got, (k,), F).astype(BF)
        home.start()
    for d in range(2, t.one.steps + 1):
        for op in late:
            op.step(d)
    for op in late:
        op.finish()
    for put, got, home in (
        (v.s_one, v.f_one, t.one_home),
        (v.s_two, v.f_two, t.two_home),
        (v.s_three, v.f_three, t.three_home),
    ):
        put[...] = got[...].astype(BF)
        home.start()
    homes = [t.one_home, t.two_home, t.three_home, t.gu_a_home, t.down_b_home]
    homes += [t.gate_home, t.up_home, t.down]
    for move in [t.grad_input, t.activations, t.q_home, t.qb_home, t.out_home] + homes:
        move.finish()


def backward(given, dims, collective_id):
    S, F, R, seg, L, kb, rb, hb, ob = dims
    own = R * seg
    G = S // R
    C = G // HEADS
    qlen = L // C
    width = given["resid"].shape[1]
    per_head = S // HEADS
    hp = given["sum_up"].shape[2]
    lora = width + RANK
    one = 2 * HEAD + 3 * RANK
    two = 2 * HEAD + width
    low = functools.partial(jax.ShapeDtypeStruct, dtype=BF)
    full = functools.partial(jax.ShapeDtypeStruct, dtype=F32)

    def to_rows(at):
        return [(j, lax.rem(at, G) * R + j, at // G) for j in range(R)]

    def to_out(at):
        return [
            (j, lax.rem(at, G) // C * per_head + j, at // G * C + lax.rem(at, C)) for j in range(per_head)
        ]

    outs = dict(
        act_home=low((R, seg, width)),
        grad_home=full((R, seg, width)),
        o_q=low((S, kb, HEAD)),
        o_qb=low((S, rb, HEAD)),
        o_out=low((R * C, ob, lora)),
        o_gate=low((S, kb + rb, hp)),
        o_up=low((S, kb + rb, hp)),
        o_down=low((F, hb, lora)),
        o_one=low((F, kb, one)),
        o_two=low((F, rb, two)),
        o_three=low((F, kb, 128)),
        o_gu_a=low((F, kb, 2 * RANK)),
        o_down_b=low((F, rb, width)),
    )
    scratch = dict(
        d_resid=full((own, width)),
        d_attn_own=low((own, width)),
        d_attn=low((G, own, width)),
        da=low((qlen, lora)),
        d_mixed=low((qlen, HEAD)),
        d_scores=low((qlen, L)),
        probs_low=low((qlen, L)),
        d_pu=low((L, 3 * HEAD + 3 * RANK)),
        d_n1_sum=full((own, width)),
        grad_rows=full((R, seg, width)),
        act_rows=low((R, seg, width)),
        t_out=low((F, per_head, ob, lora)),
        t_q=low((F, S, kb, HEAD)),
        t_qb=low((F, S, rb, HEAD)),
        t_1=low((S, F, kb, one)),
        t_2=low((S, F, rb, two)),
        t_3=low((S, F, kb, 128)),
        r_out=low((F, per_head, ob, lora)),
        r_q=low((F, S, kb, HEAD)),
        r_qb=low((F, S, rb, HEAD)),
        s_out=low((per_head, ob, lora)),
        s_q=low((S, kb, HEAD)),
        s_qb=low((S, rb, HEAD)),
    )
    scratch.update(
        f_one=full((F, kb, one)),
        s_one=low((F, kb, one)),
        f_two=full((F, rb, two)),
        s_two=low((F, rb, two)),
        f_three=full((F, kb, 128)),
        s_three=low((F, kb, 128)),
        s_gu_a=low((F, kb, 2 * RANK)),
        s_down_b=low((F, rb, width)),
    )
    slots = named(given, outs, scratch)
    a = Bag(slots)

    def op(kind, src, dst, *more):
        return kind(src, *more), src, dst

    ops = dict(
        down=op(Direct, a.part_down, a.o_down, "fsdp", F),
        d_attn=op(Line, a.d_attn_own, a.d_attn, G),
        d_n1=op(LineSum, a.d_attn, a.d_n1_sum, G),
        out=op(Direct, a.t_out, a.r_out, "fsdp", F),
        q=op(Direct, a.t_q, a.r_q, "fsdp", F),
        qb=op(Direct, a.t_qb, a.r_qb, "fsdp", F),
        one=op(LineSum, a.t_1, a.f_one, S),
        two=op(LineSum, a.t_2, a.f_two, S),
        three=op(LineSum, a.t_3, a.f_three, S),
        grad_input=op(Post, a.grad_rows, a.grad_home, R, to_rows),
        activations=op(Post, a.act_rows, a.act_home, R, to_rows),
        q_home=op(Direct, a.s_q, a.o_q, "seq", S),
        qb_home=op(Direct, a.s_qb, a.o_qb, "seq", S),
        out_home=op(Post, a.s_out, a.o_out, R * C, to_out),
        gate_home=op(Direct, a.sum_gate, a.o_gate, "seq", S),
        up_home=op(Direct, a.sum_up, a.o_up, "seq", S),
    )
    ops.update(
        one_home=op(Direct, a.s_one, a.o_one, "fsdp", F),
        two_home=op(Direct, a.s_two, a.o_two, "fsdp", F),
        three_home=op(Direct, a.s_three, a.o_three, "fsdp", F),
        gu_a_home=op(Direct, a.s_gu_a, a.o_gu_a, "fsdp", F),
        down_b_home=op(Direct, a.s_down_b, a.o_down_b, "fsdp", F),
    )
    far = [id(x) for x in (a.part_down, a.sum_gate, a.sum_up)]
    vmem = pl.BlockSpec(memory_space=pltpu.VMEM)
    away = pl.BlockSpec(memory_space=pl.ANY)
    result = pl.pallas_call(
        functools.partial(back_kernel, dims, slots, ops),
        out_shape=list(outs.values()),
        in_specs=[away if id(slots[name]) in far else vmem for name in given],
        out_specs=[away] * len(outs),
        scratch_shapes=[pltpu.VMEM(a.shape, a.dtype) for a in scratch.values()]
        + [entry for kind, _, _ in ops.values() for entry in kind.scratch],
        compiler_params=pltpu.CompilerParams(
            collective_id=collective_id, has_side_effects=True, vmem_limit_bytes=62 << 20
        ),
    )(*given.values())
    return Bag(zip(outs, result))


def finish_kernel(dims, slots, *refs):
    S, F, R, kb, rb, hb, ob, hidden, hl, width = dims
    buffers, sem = refs[len(slots) : -1], refs[-1]
    copies = [pltpu.make_async_copy(refs[k], buffers[k], sem.at[k]) for k in range(len(buffers))]
    for copy in copies:
        copy.start()
    for copy in copies:
        copy.wait()
    v = Bag(zip(slots, buffers + refs[len(buffers) : len(slots)]))
    G = S // R
    C = G // HEADS
    v.activations[...] = v.act_home[...]
    v.grad_input[...] = v.grad_home[...]

    def of_head(ref, head):
        parts = [ref[row * G + head * C + c].astype(F32) for row in range(R) for c in range(C)]
        return sum(parts[1:], parts[0])

    for head in range(HEADS):
        cols = slice(head * HEAD, head * HEAD + HEAD)
        v.w_qkv[:, cols] = of_head(v.o_q, head)
        v.q_b[:, cols] = of_head(v.o_qb, head)
    out = over_fsdp(v.o_one, (), F)
    v.w_qkv[:, HEADS * HEAD :] = out[:, : 2 * HEAD]
    v.qkv_a[...] = out[:, 2 * HEAD :]
    out = over_fsdp(v.o_two, (), F)
    v.kv_b[0] = out[:, :HEAD]
    v.kv_b[1] = out[:, HEAD : 2 * HEAD]
    v.out_b[...] = out[:, 2 * HEAD :]
    v.gains[...] = over_fsdp(v.o_three, (), F)
    v.gu_a[...] = over_fsdp(v.o_gu_a, (), F)
    v.down_b[...] = over_fsdp(v.o_down_b, (), F)
    out = over_fsdp(v.o_down, (), F)
    v.w_down[...] = out[:, :width]
    v.down_a[...] = out[:, width:]
    out = over_fsdp(v.o_out, (), R * C)
    v.w_out[...] = out[:, :width]
    v.out_a[...] = out[:, width:]
    for half, ref in ((0, v.o_gate), (1, v.o_up)):
        for j in range(S):
            at = half * hidden + j * hl
            v.w_gu[:, at : at + hl] = ref[j, 0:kb, :hl].astype(F32)
            v.gu_b[half, :, j * hl : j * hl + hl] = ref[j, kb:, :hl].astype(F32)


def finish(got, dims):
    S, F, R, kb, rb, hb, ob, hidden, hl, width = dims
    full = functools.partial(jax.ShapeDtypeStruct, dtype=F32)
    given = vars(got)
    outs = dict(
        activations=got.act_home,
        grad_input=got.grad_home,
        w_qkv=full((kb, (HEADS + 2) * HEAD)),
        qkv_a=full((kb, 3 * RANK)),
        q_b=full((rb, HEADS * HEAD)),
        kv_b=full((2, rb, HEAD)),
        w_out=full((ob, width)),
        out_a=full((ob, RANK)),
        out_b=full((rb, width)),
        w_gu=full((kb, 2 * hidden)),
        gu_a=full((kb, 2 * RANK)),
        gu_b=full((2, rb, hidden)),
        w_down=full((hb, width)),
        down_a=full((hb, RANK)),
        down_b=full((rb, width)),
        gains=full((kb, 128)),
    )
    slots = named(given, outs)
    vmem = pl.BlockSpec(memory_space=pltpu.VMEM)
    result = pl.pallas_call(
        functools.partial(finish_kernel, dims, slots),
        out_shape=[jax.ShapeDtypeStruct(x.shape, x.dtype) for x in outs.values()],
        in_specs=[pl.BlockSpec(memory_space=pl.ANY)] * len(given),
        out_specs=[vmem] * len(outs),
        scratch_shapes=[pltpu.VMEM(x.shape, x.dtype) for x in given.values()]
        + [pltpu.SemaphoreType.DMA((len(given),))],
        compiler_params=pltpu.CompilerParams(vmem_limit_bytes=48 << 20),
    )(*given.values())
    return Bag(zip(outs, result))


def shards(
    S,
    F,
    layer_input,
    document_numbers,
    cotangent,
    w_qkv,
    qkv_a,
    q_b,
    kv_b,
    w_out,
    out_a,
    out_b,
    w_gu,
    gu_a,
    gu_b,
    w_down,
    down_a,
    down_b,
    gain_a,
    gain_f,
):
    R, seg, width = layer_input.shape
    L = seg * S
    own = R * seg
    G = S // R
    C = G // HEADS
    scale = HEAD**-0.5
    kb = w_qkv.shape[0]
    rb = q_b.shape[0]
    hb = w_down.shape[0]
    ob = w_out.shape[0]
    hidden = w_gu.shape[1] // 2
    hl = hidden // S
    hp = (hl + 127) // 128 * 128
    s = lax.axis_index("seq")
    r = s // G
    head = lax.rem(s, G) // C
    chunk = lax.rem(s, C)
    qlen = L // C

    on_seq = ("seq", S)
    h = forward(
        dict(
            x=layer_input,
            ids=document_numbers,
            cot=cotangent,
            w_qkv=w_qkv,
            qkv_a=qkv_a,
            gain_pair=jnp.pad(jnp.stack([gain_a, gain_f], axis=1), ((0, 0), (0, 126))),
            q_b=q_b,
            kv_b=kv_b,
            add_out_b=out_b,
            w_out=w_out,
            out_a=out_a,
            w_gu=w_gu,
            gu_b=gu_b,
            w_down=w_down,
            down_a=down_a,
            gu_a=gu_a,
            down_b=down_b,
        ),
        (S, F, R, seg, kb, rb, ob),
        0,
    )
    cot = h.cot_all

    dims = (S, F, R, seg, kb, rb, hb, hl, hp)
    apart = S * own > 1024
    ffn = feed_forward(
        dict(
            n2_own=h.n2_own,
            gw=h.gw_all,
            dw=h.dw_all,
            cot=cot,
            gu_a=h.gu_a_all,
            down_b=h.down_b_all.reshape(RANK, width),
        ),
        dims,
        apart,
        5,
    )
    if apart:
        ffn.ffn_sum, ffn.f_gu_a, ffn.f_down_b = transfer(
            [LineSum(x, S) for x in (ffn.ffn_part, ffn.g_gu_a, ffn.g_down_b)], [on_seq], 7
        )
    cot_own = lax.dynamic_slice_in_dim(cot, lax.rem(s, G) * R, R, 0)
    cot_own = lax.dynamic_index_in_dim(cot_own, r, 1, keepdims=False).reshape(own, width)

    got = backward(
        dict(
            d_n2=ffn.dn_sum,
            cot_own=cot_own,
            resid=h.resid,
            gains=h.gains,
            x_own=h.x_own,
            out_b=h.out_b,
            wo=h.wo,
            w1=h.w1,
            up_b=h.up_b,
            norm_one=h.norm_one,
            u=h.u,
            u_out=h.u_out,
            query=h.query,
            key=h.key,
            value=h.value,
            cosine=h.cosine,
            sine=h.sine,
            probs=h.probs,
            mixed=h.mixed,
            ffn_sum=ffn.ffn_sum,
            f_gu_a=ffn.f_gu_a,
            f_down_b=ffn.f_down_b,
            part_down=ffn.part_down,
            sum_gate=ffn.sum_gate,
            sum_up=ffn.sum_up,
        ),
        (S, F, R, seg, L, kb, rb, hb, ob),
        8,
    )

    done = finish(got, (S, F, R, kb, rb, hb, ob, hidden, hl, width))
    return (
        done.activations,
        done.grad_input,
        done.w_qkv,
        done.qkv_a,
        done.q_b,
        done.kv_b,
        done.w_out,
        done.out_a,
        done.out_b,
        done.w_gu,
        done.gu_a,
        done.gu_b,
        done.w_down,
        done.down_a,
        done.down_b,
        done.gains[:, 0],
        done.gains[:, 1],
    )


def solution(mesh):
    both = P(("seq", "fsdp"), None)
    second = P(None, ("seq", "fsdp"), None)
    tokens = P("fsdp", "seq", None)
    gain = P(("seq", "fsdp"))
    return jax.shard_map(
        functools.partial(shards, mesh.shape["seq"], mesh.shape["fsdp"]),
        mesh=mesh,
        in_specs=(tokens, P("fsdp", "seq"), tokens)
        + (both, both, both, second, both, both, both, both, both, second, both, both, both, gain, gain),
        out_specs=(tokens, tokens)
        + (both, both, both, second, both, both, both, both, both, second, both, both, both, gain, gain),
        check_vma=False,
    )
```

```python
import functools
import math

import jax
import jax.numpy as jnp
from jax import lax
from jax.experimental import pallas as pl
from jax.experimental.pallas import tpu as pltpu
from jax.sharding import PartitionSpec as P

HEADS = 4
HEAD = 256
RANK = 256
EPSILON = 1e-06
ROPE_BASE = 10000.0
MASKED = -1e30
FFN = "ffn"
ROWS = tuple("abcdefgh")
MESH = pl.DeviceIdType.MESH
BF = jnp.bfloat16
F32 = jnp.float32


def mm(left, right):
    return jnp.dot(left, right, preferred_element_type=F32)


def mm_tn(left, right):
    return lax.dot_general(left, right, (((0,), (0,)), ((), ())), preferred_element_type=F32)


def mm_nt(left, right):
    return lax.dot_general(left, right, (((1,), (1,)), ((), ())), preferred_element_type=F32)


def remote(src, dst, send, recv, peer):
    return pltpu.make_async_remote_copy(
        src_ref=src, dst_ref=dst, send_sem=send, recv_sem=recv, device_id=peer, device_id_type=MESH
    )


class Bag:
    def __init__(self, entries=()):
        self.__dict__.update(entries)


class Slot(jax.ShapeDtypeStruct):
    pass


def named(*groups):
    slots = {}
    for group in groups:
        for name, a in group.items():
            slots[name] = Slot(a.shape, a.dtype)
    return slots


def unpack(slots, ops, refs):
    refs = list(refs)
    where = {id(slot): ref for slot, ref in zip(slots.values(), refs)}
    v = Bag(zip(slots, refs))
    rest = refs[len(slots) :]
    bound = Bag()
    for name, (op, src, dst) in ops.items():
        take = len(op.scratch)
        src, dst = (
            where[id(x[0])].at[x[1]] if isinstance(x, tuple) else where[id(x)] for x in (src, dst)
        )
        op.bind(src, dst, *rest[:take])
        setattr(bound, name, op)
        rest = rest[take:]
    return v, bound


class Direct:
    steps = 0

    def relay(self):
        pass

    def __init__(self, x, axis, size, spread=False):
        self.x, self.axis, self.size, self.spread = x, axis, size, spread
        shape = ((size,) if spread else ()) + x.shape
        self.out = jax.ShapeDtypeStruct(shape, x.dtype)
        self.scratch = [
            pltpu.SemaphoreType.DMA,
            pltpu.SemaphoreType.DMA((size,)),
            pltpu.SemaphoreType.DMA((size,)),
        ]

    def bind(self, x_ref, o_ref, local, send, recv):
        me = lax.axis_index(self.axis)
        self.copies = []
        for k in range(1, self.size):
            peer = lax.rem(me + k, self.size)
            src = x_ref if self.spread else x_ref.at[peer]
            self.copies.append(remote(src, o_ref.at[me], send.at[k], recv.at[k], {self.axis: peer}))
        src = x_ref if self.spread else x_ref.at[me]
        self.copies.append(pltpu.make_async_copy(src, o_ref.at[me], local))

    def start(self):
        for copy in self.copies:
            copy.start()

    def finish(self):
        for copy in self.copies:
            copy.wait()


class Square:
    steps = 0

    def __init__(self, x, dim):
        self.x = x
        size = x.shape[dim]
        half = size // 2 if dim == 0 else size // 256 * 128
        first = (slice(None),) * dim
        self.cut = (first + (pl.ds(0, half),), first + (pl.ds(half, size - half),))
        self.out = jax.ShapeDtypeStruct((4,) + x.shape, x.dtype)
        self.scratch = [
            pltpu.SemaphoreType.DMA,
            pltpu.SemaphoreType.DMA((3, 2)),
            pltpu.SemaphoreType.DMA((3, 2)),
        ]

    def bind(self, x_ref, o_ref, local, send, recv):
        me = lax.axis_index("fsdp")
        near_x, near_y, far = me + 1 - 2 * lax.rem(me, 2), lax.rem(me + 2, 4), 3 - me
        cut = self.cut

        def move(src, owner, part, way, peer):
            dst = o_ref.at[owner].at[cut[part]]
            src = dst if src is None else src.at[cut[part]]
            return remote(src, dst, send.at[way, part], recv.at[way, part], {"fsdp": peer})

        self.to_x = [move(x_ref, me, part, 0, near_x) for part in range(2)]
        self.to_y = [move(x_ref, me, part, 1, near_y) for part in range(2)]
        self.from_x = [move(None, near_x, part, 0, near_x) for part in range(2)]
        self.from_y = [move(None, near_y, part, 1, near_y) for part in range(2)]
        self.on_y = move(None, near_x, 0, 2, near_y)
        self.on_x = move(None, near_y, 1, 2, near_x)
        self.from_far = [move(None, far, part, 2, near_x) for part in range(2)]
        self.own = pltpu.make_async_copy(x_ref, o_ref.at[me], local)

    def start(self):
        self.to_x[0].start()
        self.to_y[1].start()
        self.to_x[1].start()
        self.to_y[0].start()
        self.own.start()

    def relay(self):
        self.from_x[0].wait_recv()
        self.on_y.start()
        self.from_y[1].wait_recv()
        self.on_x.start()

    def finish(self):
        self.from_x[1].wait_recv()
        self.from_y[0].wait_recv()
        for part in range(2):
            self.from_far[part].wait_recv()
            self.to_x[part].wait_send()
            self.to_y[part].wait_send()
        self.on_y.wait_send()
        self.on_x.wait_send()
        self.own.wait()


class Post:
    steps = 0

    def __init__(self, x, slots, sends):
        self.slots, self.sends = slots, sends
        self.x = x
        count = len(sends(0))
        self.scratch = [
            pltpu.SemaphoreType.DMA((count,)),
            pltpu.SemaphoreType.DMA((count,)),
            pltpu.SemaphoreType.DMA((slots,)),
        ]

    def bind(self, x_ref, o_ref, local, send, recv):
        s = lax.axis_index("seq")
        self.s = s
        self.plan = []
        for k, (block, device, slot) in enumerate(self.sends(s)):
            src = x_ref if block is None else x_ref.at[block]
            away = remote(src, o_ref.at[slot], send.at[k], recv.at[slot], {"seq": device})
            here = pltpu.make_async_copy(src, o_ref.at[slot], recv.at[slot])
            self.plan.append((device, away, here))
        self.arrive = [
            pltpu.make_async_copy(o_ref.at[k], o_ref.at[k], recv.at[k]) for k in range(self.slots)
        ]

    def start(self):
        for device, away, here in self.plan:
            pl.when(device != self.s)(away.start)
            pl.when(device == self.s)(here.start)

    def finish(self):
        for copy in self.arrive:
            copy.wait()
        for device, away, here in self.plan:
            pl.when(device != self.s)(away.wait_send)


class Line:
    def __init__(self, x, line, span=None):
        self.x, self.line = x, line
        self.lo, self.hi = span or (0, line // 2)
        self.steps = line // 2 - 1
        self.out = jax.ShapeDtypeStruct((line,) + x.shape, x.dtype)
        self.scratch = [
            pltpu.SemaphoreType.DMA,
            pltpu.SemaphoreType.DMA((2 * line,)),
            pltpu.SemaphoreType.DMA((line,)),
        ]

    def bind(self, x_ref, o_ref, local, send, recv):
        self.x_ref, self.o_ref, self.send, self.recv = x_ref, o_ref, send, recv
        line = self.line
        s = lax.axis_index("seq")
        base = s // line * line
        self.n2 = line // 2
        self.i = s - base
        self.p, self.core = self.i // 2, lax.rem(self.i, 2)
        self.sib = s + 1 - 2 * self.core
        self.left = base + lax.rem(self.i + line - 2, line)
        self.right = base + lax.rem(self.i + 2, line)
        self.own = pltpu.make_async_copy(x_ref, o_ref.at[self.i], local)
        self.inside = (self.p >= self.lo) & (self.p < self.hi)

    def copy(self, blk, src, dst, k):
        return remote(src, self.o_ref.at[blk], self.send.at[k], self.recv.at[blk], {"seq": dst})

    def start(self):
        @pl.when(self.p + 1 < self.hi)
        def _():
            self.copy(self.i, self.x_ref, self.right, 0).start()

        @pl.when(self.p > self.lo)
        def _():
            self.copy(self.i, self.x_ref, self.left, 1).start()

        @pl.when(self.inside)
        def _():
            self.copy(self.i, self.x_ref, self.sib, 2).start()

        self.own.start()

    def step(self, d):
        p, n2, o = self.p, self.n2, self.o_ref

        @pl.when((p - d >= 0) & (p < self.hi))
        def _():
            blk = self.i - 2 * d
            self.copy(blk, o.at[blk], self.left, 0).wait_recv()

            @pl.when(p + 1 < self.hi)
            def _():
                self.copy(blk, o.at[blk], self.right, 4 * d).start()

            @pl.when(self.inside)
            def _():
                self.copy(blk, o.at[blk], self.sib, 4 * d + 1).start()

        @pl.when((p + d < n2) & (p >= self.lo))
        def _():
            blk = self.i + 2 * d
            self.copy(blk, o.at[blk], self.right, 0).wait_recv()

            @pl.when(p > self.lo)
            def _():
                self.copy(blk, o.at[blk], self.left, 4 * d + 2).start()

            @pl.when(self.inside)
            def _():
                self.copy(blk, o.at[blk], self.sib, 4 * d + 3).start()

    def from_core(self, q):
        blk = 2 * q + 1 - self.core
        self.copy(blk, self.o_ref.at[blk], self.sib, 0).wait_recv()

    def finish(self):
        @pl.when(self.inside)
        def _():
            for q in range(self.n2):
                self.from_core(q)

        self.settle()
        self.own.wait()

    def settle(self):
        p, n2 = self.p, self.n2

        def sent(k, sure):
            @pl.when(sure)
            def _():
                self.copy(self.i, self.x_ref, self.sib, k).wait_send()

        sent(0, p + 1 < self.hi)
        sent(1, p > self.lo)
        sent(2, self.inside)
        for d in range(1, n2):
            sent(4 * d, (p - d >= 0) & (p + 1 < self.hi))
            sent(4 * d + 1, (p - d >= 0) & self.inside)
            sent(4 * d + 2, (p + d < n2) & (p > self.lo))
            sent(4 * d + 3, (p + d < n2) & self.inside)


class Grid:
    def __init__(self, x, S, F):
        self.x, self.S, self.F = x, S, F
        self.n2 = n2 = S // 2
        self.steps = n2 - 1
        self.out = jax.ShapeDtypeStruct((S, F) + x.shape, x.dtype)
        self.scratch = [
            pltpu.SemaphoreType.DMA,
            pltpu.SemaphoreType.DMA((2, n2)),
            pltpu.SemaphoreType.DMA((n2, F)),
            pltpu.SemaphoreType.DMA((n2, F)),
            pltpu.SemaphoreType.DMA((S, F)),
        ]

    def bind(self, x_ref, o_ref, local, z_send, f_send, s_send, recv):
        self.x_ref, self.o_ref, self.recv = x_ref, o_ref, recv
        self.z_send, self.f_send, self.s_send = z_send, f_send, s_send
        s, self.f = lax.axis_index("seq"), lax.axis_index("fsdp")
        self.p, self.core = s // 2, lax.rem(s, 2)
        self.s = s
        self.sib = {"seq": s + 1 - 2 * self.core}
        self.left = {"seq": lax.rem(s + self.S - 2, self.S)}
        self.right = {"seq": lax.rem(s + 2, self.S)}
        self.own = pltpu.make_async_copy(x_ref, o_ref.at[s, self.f], local)
        self.square = self.F == 4
        self.near = (1, 2) if self.square else range(1, self.F)

    def place(self, k):
        f = self.f
        if self.square:
            return (f, f + 1 - 2 * lax.rem(f, 2), lax.rem(f + 2, 4), 3 - f)[k]
        return lax.rem(f + self.F - k, self.F)

    def peer(self, k):
        return {"fsdp": self.place(k) if self.square else lax.rem(self.f + k, self.F)}

    def copy(self, q, f, send, peer):
        blk = 2 * q + self.core
        dst = self.o_ref.at[blk, f]
        return remote(dst, dst, send, self.recv.at[blk, f], peer)

    def first(self, send, peer):
        return remote(self.x_ref, self.o_ref.at[self.s, self.f], send, self.recv.at[self.s, self.f], peer)

    def start(self):
        p, n2 = self.p, self.n2

        @pl.when(p < n2 - 1)
        def _():
            self.first(self.z_send.at[0, p], self.right).start()

        @pl.when(p > 0)
        def _():
            self.first(self.z_send.at[1, p], self.left).start()

        for k in self.near:
            self.first(self.f_send.at[p, k], self.peer(k)).start()
        self.first(self.s_send.at[p, 0], self.sib).start()
        self.own.start()

    def pass_on(self, q):
        for k in self.near:
            self.copy(q, self.f, self.f_send.at[q, k], self.peer(k)).start()
        self.copy(q, self.f, self.s_send.at[q, 0], self.sib).start()

    def arrived(self, q, f):
        self.copy(q, f, self.s_send.at[q, 0], self.sib).wait_recv()

    def step(self, d):
        p, n2 = self.p, self.n2

        @pl.when(p - d >= 0)
        def _():
            self.arrived(p - d, self.f)

            @pl.when(p < n2 - 1)
            def _():
                self.copy(p - d, self.f, self.z_send.at[0, p - d], self.right).start()

            self.pass_on(p - d)

        @pl.when(p + d < n2)
        def _():
            self.arrived(p + d, self.f)

            @pl.when(p > 0)
            def _():
                self.copy(p + d, self.f, self.z_send.at[1, p + d], self.left).start()

            self.pass_on(p + d)

    def relay(self, k):
        f = self.place(k)
        for q in range(self.n2):
            self.arrived(q, f)
            self.copy(q, f, self.s_send.at[q, k], self.sib).start()
            if self.square and ((k == 1 and q < self.n2 // 2) or (k == 2 and q >= self.n2 // 2)):
                self.copy(q, f, self.f_send.at[q, 3], self.peer(3 - k)).start()

    def finish(self):
        p, n2 = self.p, self.n2
        for q in range(n2):
            for k in range(self.F):
                f = self.place(k)
                blk = 2 * q + 1 - self.core
                dst = self.o_ref.at[blk, f]
                remote(dst, dst, self.s_send.at[q, k], self.recv.at[blk, f], self.sib).wait_recv()
        for q in range(n2):

            @pl.when((q <= p) & (p < n2 - 1))
            def _():
                self.first(self.z_send.at[0, q], self.right).wait_send()

            @pl.when((q >= p) & (p > 0))
            def _():
                self.first(self.z_send.at[1, q], self.left).wait_send()

            for k in range(self.F):
                self.first(self.s_send.at[q, k], self.sib).wait_send()
                if k:
                    self.first(self.f_send.at[q, k], self.sib).wait_send()
        self.own.wait()


class LineSum:
    vmem = True

    def __init__(self, x, line):
        self.x, self.line = x, line
        self.n2 = n2 = line // 2
        self.steps = n2 - 1
        blk = x.shape[1:]
        self.out = jax.ShapeDtypeStruct(blk, F32)
        self.scratch = [pltpu.VMEM((n2,) + blk, BF), pltpu.VMEM((n2 + 1,) + blk, BF)] + [
            pltpu.SemaphoreType.DMA((3 * n2,)),
            pltpu.SemaphoreType.DMA((3 * n2,)),
        ]

    def bind(self, x_ref, o_ref, mine, came, send, recv):
        self.x_ref, self.o_ref, self.mine, self.came = x_ref, o_ref, mine, came
        line, n2 = self.line, self.n2
        s = lax.axis_index("seq")
        base = s // line * line
        i = s - base
        self.p, self.core = i // 2, lax.rem(i, 2)
        sib = {"seq": s + 1 - 2 * self.core}
        left = {"seq": base + lax.rem(i + line - 2, line)}
        right = {"seq": base + lax.rem(i + 2, line)}
        core = self.core
        self.hand_over = lambda q: remote(
            x_ref.at[2 * q + 1 - core], mine.at[q], send.at[q], recv.at[q], sib
        )
        self.rightward = lambda q: remote(
            mine.at[q], came.at[q + 1], send.at[n2 + q], recv.at[n2 + q], right
        )
        self.leftward = lambda q: remote(
            mine.at[q], came.at[q], send.at[2 * n2 + q], recv.at[2 * n2 + q], left
        )
        order = []
        for k in range((n2 + 1) // 2):
            order += [n2 - 1 - k] + ([k] if k != n2 - 1 - k else [])
        self.order = order

    def start(self):
        for q in self.order:
            self.hand_over(q).start()

    def add(self, q, other):
        self.mine[q] = (self.mine[q].astype(F32) + self.came[other].astype(F32)).astype(BF)

    def step(self, d):
        p, n2 = self.p, self.n2
        if d == 1:
            for q in self.order:
                self.hand_over(q).wait_recv()
                own = self.x_ref[2 * q + self.core].astype(F32)
                self.mine[q] = (own + self.mine[q].astype(F32)).astype(BF)

                @pl.when((q > p) & (p == 0))
                def _():
                    self.rightward(q).start()

                @pl.when((q < p) & (p == n2 - 1))
                def _():
                    self.leftward(q).start()

        q_right = n2 - d

        @pl.when((p > 0) & (p < q_right))
        def _():
            self.rightward(q_right).wait_recv()
            self.add(q_right, q_right + 1)
            self.rightward(q_right).start()

        q_left = d - 1

        @pl.when((p < n2 - 1) & (p > q_left))
        def _():
            self.leftward(q_left).wait_recv()
            self.add(q_left, q_left)
            self.leftward(q_left).start()

    def finish(self):
        p, n2 = self.p, self.n2
        for q in range(n2):

            @pl.when(p == q)
            def _():
                total = self.mine[q].astype(F32)
                if q > 0:
                    self.rightward(q).wait_recv()
                    total += self.came[q + 1].astype(F32)
                if q < n2 - 1:
                    self.leftward(q).wait_recv()
                    total += self.came[q].astype(F32)
                self.o_ref[...] = total

        for q in range(n2):
            self.hand_over(q).wait_send()

            @pl.when(q > p)
            def _():
                self.rightward(q).wait_send()

            @pl.when(q < p)
            def _():
                self.leftward(q).wait_send()


def transfer_kernel(ops, axes, *refs):
    count = len(ops)
    rest = list(refs[2 * count :])
    for a, op in enumerate(ops):
        take = len(op.scratch)
        op.bind(refs[a], refs[count + a], *rest[:take])
        rest = rest[take:]
    barrier = pltpu.get_barrier_semaphore()
    for axis, size in axes:
        me = lax.axis_index(axis)
        for k in range(1, size):
            peer = {axis: lax.rem(me + k, size)}
            pl.semaphore_signal(barrier, inc=1, device_id=peer, device_id_type=MESH)
    pl.semaphore_wait(barrier, sum(size - 1 for _, size in axes))
    for op in ops:
        op.start()
    for d in range(1, 1 + max(op.steps for op in ops)):
        for op in ops:
            if d <= op.steps:
                op.step(d)
    for op in ops:
        op.finish()


def transfer(ops, axes, collective_id):
    spaces = [
        pl.BlockSpec(memory_space=pltpu.VMEM if hasattr(op, "vmem") else pl.ANY) for op in ops
    ]
    return pl.pallas_call(
        functools.partial(transfer_kernel, ops, axes),
        out_shape=[op.out for op in ops],
        in_specs=spaces,
        out_specs=spaces,
        scratch_shapes=[entry for op in ops for entry in op.scratch],
        compiler_params=pltpu.CompilerParams(
            collective_id=collective_id, has_side_effects=True, vmem_limit_bytes=48 << 20
        ),
    )(*[op.x for op in ops])


def meet(axes):
    barrier = pltpu.get_barrier_semaphore()
    for axis, size in axes:
        me = lax.axis_index(axis)
        for k in range(1, size):
            peer = {axis: lax.rem(me + k, size)}
            pl.semaphore_signal(barrier, inc=1, device_id=peer, device_id_type=MESH)
    pl.semaphore_wait(barrier, sum(size - 1 for _, size in axes))


def ffn_kernel(dims, slots, ops, *refs):
    S, F, R, seg, kb, rb, hb, hl, hp = dims
    v, t = unpack(slots, ops, refs[2:])
    stage_sem, cot_sem = refs[:2]
    own = R * seg
    width = v.n2_own.shape[1]
    tokens = S * own
    G = S // R
    gather, scatter = t.n2, t.d_n2
    early = [t.gu_a, t.down_b, t.ffn] if hasattr(t, FFN) else []
    n2, gw, gb, dw, cot_u, gu_a, down_b = v.n2, v.w, v.gb, v.w_down, v.cot_u, v.w_gu_a, v.down_b
    u_gu, act, d_gu, d_u_gu = v.u_gu, v.act, v.d_gu, v.d_u_gu
    meet([("seq", S), ("fsdp", F)])
    gather.start()

    def fetch(s):
        return pltpu.make_async_copy(v.gw.at[:, s], v.stage.at[s % 2], stage_sem.at[s % 2])

    fetch(0).start()
    moves = []
    for j in range(S):
        row, i = j // G, j % G
        for e in range(R):
            at = j * own + e * seg
            src = v.cot.at[i * R + e, row]
            dst = cot_u.at[pl.ds(at, seg), pl.ds(0, width)]
            moves.append(pltpu.make_async_copy(src, dst, cot_sem.at[len(moves)]))
            moves[-1].start()

    for s in range(S):
        if s + 1 < S:
            fetch(s + 1).start()
        fetch(s).wait()
        for f in range(F):
            b = s * F + f
            gw[b * kb : b * kb + kb, :] = v.stage[s % 2, f, 0:kb, :]
            gb[b * rb : b * rb + rb, :] = v.stage[s % 2, f, kb : kb + rb, :]
            gu_a[b * kb : b * kb + kb, :] = v.gu_a[s, f]
        if s == S // 2 and gather.steps >= 1:
            gather.step(1)
    for move in moves:
        move.wait()
    tile = 2 * own
    tiles = tokens // tile

    @pl.loop(0, tiles)
    def _(k):
        rows = pl.ds(pl.multiple_of(k * tile, tile), tile)
        cot_u[rows, width:] = mm_nt(cot_u[rows, :width], down_b[...]).astype(BF)

    for f in range(F):
        dw[f * hb : f * hb + hb, :] = v.dw[f]
    if hp > hl:
        dw[hl:hp, :] = jnp.zeros((hp - hl, dw.shape[1]), BF)
    gather.own.wait()
    if gather.steps >= 2:
        gather.step(2)
    inner = math.sqrt(2.0 / math.pi)
    per_tile = 2

    def one_chip(k):
        rows = pl.ds(pl.multiple_of(k * tile, tile), tile)
        n = n2[pl.ds(k * per_tile, per_tile)].reshape(tile, width)
        u = mm(n, gu_a[...]).astype(BF)
        u_gu[rows, :] = u
        d_act = mm_nt(cot_u[rows, :], dw[...])
        gate = mm(n, gw[:, :hp]) + mm(u[:, :RANK], gb[:, :hp])
        up = mm(n, gw[:, hp:]) + mm(u[:, RANK:], gb[:, hp:])
        square = gate * gate
        th = jnp.tanh(inner * gate * (1.0 + 0.044715 * square))
        half = 0.5 * (1.0 + th)
        gelu = gate * half
        act[rows, :] = (gelu * up).astype(BF)
        slope = half + 0.5 * gate * (1.0 - th * th) * (inner * (1.0 + 3 * 0.044715 * square))
        d_gate = (d_act * up * slope).astype(BF)
        d_up = (d_act * gelu).astype(BF)
        d_gu[rows, :hp] = d_gate
        d_gu[rows, hp:] = d_up
        d_u_gu[rows, :RANK] = mm_nt(d_gate, gb[:, :hp]).astype(BF)
        d_u_gu[rows, RANK:] = mm_nt(d_up, gb[:, hp:]).astype(BF)
        out = mm_nt(d_gu[rows, :], gw[...]) + mm_nt(d_u_gu[rows, :], gu_a[...])
        v.dn[pl.ds(k * per_tile, per_tile)] = out.astype(BF).reshape(per_tile, own, width)

    @pl.loop(0, 2 * tiles - 1)
    def _(turn):
        for d in range(3, gather.steps + 1):

            @pl.when(turn == 2 * d - 3)
            def _():
                gather.step(d)

        away = (turn + 1) // 2
        k = jnp.where(lax.rem(turn, 2) == 1, gather.p - away, gather.p + away)

        @pl.when((k >= 0) & (k < tiles))
        def _():
            gather.from_core(k)
            one_chip(k)

    gather.settle()
    scatter.start()

    def gate_or_up(half, part, move):
        base = half * hp
        out = mm_tn(u_gu[:, half * RANK : half * RANK + RANK], d_gu[:, base : base + hp]).astype(BF)
        for b in range(S * F):
            part[b % F, b // F, kb : kb + rb, :] = out[b * rb : b * rb + rb, :]

        def columns(src, dst):
            out = mm_tn(n2[...].reshape(tokens, width), d_gu[:, src]).astype(BF)
            for b in range(S * F):
                part[b % F, b // F, 0:kb, dst] = out[b * kb : b * kb + kb, :]

        @pl.loop(0, hp // 256)
        def _(k):
            at = pl.multiple_of(k * 256, 128)
            columns(pl.ds(pl.multiple_of(base + at, 128), 256), pl.ds(at, 256))

        left = hp % 256
        if left:
            columns(slice(base + hp - left, base + hp), slice(hp - left, hp))
        move.start()

    gate_or_up(0, v.part_gate, t.gate)
    scatter.step(1)
    gate_or_up(1, v.part_up, t.up)
    if scatter.steps >= 2:
        scatter.step(2)

    @pl.loop(0, tiles)
    def _(k):
        rows = pl.ds(pl.multiple_of(k * tile, tile), tile)
        out = mm(act[rows, :], dw[...])
        low = out[:, width:].astype(BF)
        v.u_down[rows, :] = low
        out = out[:, :width] + mm(low, down_b[...])
        v.ffn_part[pl.ds(k * per_tile, per_tile)] = out.astype(BF).reshape(per_tile, own, width)

    for d in range(3, scatter.steps + 1):
        scatter.step(d)
    for op in early[2:]:
        op.start()
    scatter.finish()
    out = mm_tn(v.u_down[...], cot_u[:, :width]).astype(BF)
    for b in range(S * F):
        v.g_down_b[b // F, b % F] = out[b * rb : b * rb + rb, :]
    out = mm_tn(n2[...].reshape(tokens, width), d_u_gu[...]).astype(BF)
    for b in range(S * F):
        v.g_gu_a[b // F, b % F] = out[b * kb : b * kb + kb, :]
    for op in early[:2]:
        op.start()
    for op in early:
        op.step(1)
    step = 128

    @pl.loop(0, cot_u.shape[1] // step)
    def _(k):
        cols = pl.ds(pl.multiple_of(k * step, step), step)
        out = mm_tn(act[...], cot_u[:, cols]).astype(BF)
        for f in range(F):
            v.part_down[f, :, cols] = out[f * hb : f * hb + hb, :]

    def sum_up(move, came, put):
        def load(s):
            return pltpu.make_async_copy(
                came.at[:, s], v.stage.at[s % 2].at[:, :, pl.ds(0, hp)], stage_sem.at[s % 2]
            )

        move.finish()
        load(0).start()
        for s in range(S):
            if s + 1 < S:
                load(s + 1).start()
            load(s).wait()
            total = v.stage[s % 2, 0, :, :hp].astype(F32)
            for f in range(1, F):
                total += v.stage[s % 2, f, :, :hp].astype(F32)
            put[s] = total.astype(BF)

    for d in range(2, scatter.steps + 1):
        for op in early:
            op.step(d)
        if d == 2:
            sum_up(t.gate, v.came_gate, v.sum_gate)
    for op in early:
        op.finish()
    sum_up(t.up, v.came_up, v.sum_up)


def over_fsdp(ref, at, F):
    out = ref[(0,) + at].astype(F32)
    for f in range(1, F):
        out += ref[(f,) + at].astype(F32)
    return out


def feed_forward(given, dims, apart, collective_id):
    S, F, R, seg, kb, rb, hb, hl, hp = dims
    g = Bag(given)
    own, width = g.n2_own.shape
    tokens = S * own
    low = functools.partial(jax.ShapeDtypeStruct, dtype=BF)
    full = functools.partial(jax.ShapeDtypeStruct, dtype=F32)
    lora = width + RANK
    outs = dict(
        dn_sum=full((own, width)),
        part_down=low((F, hb, lora)),
        sum_gate=low((S, kb + rb, hp)),
        sum_up=low((S, kb + rb, hp)),
        came_gate=low((F, S, kb + rb, hp)),
        came_up=low((F, S, kb + rb, hp)),
    )
    scratch = dict(
        n2=low((S, own, width)),
        w=low((width, 2 * hp)),
        gb=low((RANK, 2 * hp)),
        w_down=low((hp, lora)),
        cot_u=low((tokens, lora)),
        w_gu_a=low((width, 2 * RANK)),
        u_gu=low((tokens, 2 * RANK)),
        act=low((tokens, hp)),
        d_gu=low((tokens, 2 * hp)),
        d_u_gu=low((tokens, 2 * RANK)),
        u_down=low((tokens, RANK)),
        dn=low((S, own, width)),
        stage=low((2, F, kb + rb, 2 * hp)),
        part_gate=low((F, S, kb + rb, hp)),
        part_up=low((F, S, kb + rb, hp)),
    )
    parts = dict(
        ffn_part=low((S, own, width)),
        g_gu_a=low((S, F, kb, 2 * RANK)),
        g_down_b=low((S, F, rb, width)),
    )
    if apart:
        outs.update(parts)
    else:
        scratch.update(parts)
        outs.update(
            ffn_sum=full((own, width)),
            f_gu_a=full((F, kb, 2 * RANK)),
            f_down_b=full((F, rb, width)),
        )
    slots = named(given, outs, scratch)
    a = Bag(slots)

    def op(kind, src, dst, *more):
        return kind(src, *more), src, dst

    ops = dict(
        n2=op(Line, a.n2_own, a.n2, S),
        d_n2=op(LineSum, a.dn, a.dn_sum, S),
        gate=op(Direct, a.part_gate, a.came_gate, "fsdp", F),
        up=op(Direct, a.part_up, a.came_up, "fsdp", F),
    )
    if not apart:
        ops.update(
            ffn=op(LineSum, a.ffn_part, a.ffn_sum, S),
            gu_a=op(LineSum, a.g_gu_a, a.f_gu_a, S),
            down_b=op(LineSum, a.g_down_b, a.f_down_b, S),
        )
    vmem = pl.BlockSpec(memory_space=pltpu.VMEM)
    away = pl.BlockSpec(memory_space=pl.ANY)
    far = [id(x) for x in (a.gw, a.cot, a.came_gate, a.came_up)]

    def kernel(*refs):
        count = len(slots)
        ffn_kernel(dims, slots, ops, *refs[count : count + 2], *refs[:count], *refs[count + 2 :])

    result = pl.pallas_call(
        kernel,
        out_shape=list(outs.values()),
        in_specs=[away if id(slots[name]) in far else vmem for name in given],
        out_specs=[away if id(slots[name]) in far else vmem for name in outs],
        scratch_shapes=[pltpu.VMEM(x.shape, x.dtype) for x in scratch.values()]
        + [pltpu.SemaphoreType.DMA((2,)), pltpu.SemaphoreType.DMA((S * R,))]
        + [entry for kind, _, _ in ops.values() for entry in kind.scratch],
        compiler_params=pltpu.CompilerParams(
            collective_id=collective_id, has_side_effects=True, vmem_limit_bytes=62 << 20
        ),
    )(*given.values())
    return Bag(zip(outs, result))


def front_kernel(dims, slots, ops, *refs):
    S, F, R, seg, kb, rb, ob = dims
    v, t = unpack(slots, ops, refs)
    own = R * seg
    L = S * seg
    G = S // R
    C = G // HEADS
    qlen = L // C
    width = v.x.shape[2]
    scale = HEAD**-0.5
    s = lax.axis_index("seq")
    r = s // G
    head = lax.rem(s, G) // C
    chunk = lax.rem(s, C)
    meet([("seq", S), ("fsdp", F)])

    n_qkv, n_a, n_q = v.w_qkv.shape[1], v.qkv_a.shape[1], v.q_b.shape[1]
    v.p1[:, :n_qkv] = v.w_qkv[...]
    v.p1[:, n_qkv : n_qkv + n_a] = v.qkv_a[...]
    v.p1[:, n_qkv + n_a :] = v.gain_pair[...]
    t.one.start()
    v.p2[:, :n_q] = v.q_b[...]
    v.p2[:, n_q : n_q + HEAD] = v.kv_b[0]
    v.p2[:, n_q + HEAD : n_q + 2 * HEAD] = v.kv_b[1]
    v.p2[:, n_q + 2 * HEAD :] = v.add_out_b[...]
    t.two.start()
    rows_in = [getattr(t, ROWS[j]) for j in range(R)]
    for op in rows_in:
        op.start()
    t.ids.start()
    first = [t.one, t.two, t.ids] + rows_in
    v.p3[:, :width] = v.w_out[...]
    v.p3[:, width:] = v.out_a[...]
    t.three.start()
    hidden = v.w_gu.shape[1] // 2
    hl = hidden // S
    hp = v.gws.shape[2] // 2
    for half in range(2):
        for j in range(S):
            at = half * hidden + j * hl
            v.gws[j, 0:kb, half * hp : half * hp + hl] = v.w_gu[:, at : at + hl]
            v.gws[j, kb:, half * hp : half * hp + hl] = v.gu_b[half, :, j * hl : j * hl + hl]
            if hp > hl:
                v.gws[j, :, half * hp + hl : half * hp + hp] = jnp.zeros((kb + rb, hp - hl), BF)
    t.gw.start()
    v.dws[:, :width] = v.w_down[...]
    v.dws[:, width:] = v.down_a[...]
    t.dw.start()
    later = [t.gu_a, t.down_b]
    for op in later:
        op.start()
    for d in range(1, t.one.steps + 1):
        for op in first:
            op.step(d)
    t.cot.start()
    t.three.finish()
    t.wo.start()
    t.ids.finish()

    for j in range(S):
        ids = jnp.where(r == 0, v.ids_all[j, 0:1, :], v.ids_all[j, 1:2, :])
        for row in range(2, R):
            ids = jnp.where(r == row, v.ids_all[j, row : row + 1, :], ids)
        v.id_row[:, j * seg : j * seg + seg] = ids.astype(F32)
    id_row = v.id_row[...]
    v.id_cols[...] = jnp.transpose(jnp.broadcast_to(id_row, (128, L)))
    lane = lax.broadcasted_iota(jnp.int32, (128, HEAD // 2), 1).astype(F32)
    spacing = jnp.exp(lane * (-2.0 / HEAD * math.log(ROPE_BASE)))
    places = lax.broadcasted_iota(jnp.int32, (128, L), 1)
    steps = lax.broadcasted_iota(jnp.int32, (128, L), 0)

    @pl.loop(0, L // 128)
    def _(i):
        rows = pl.ds(pl.multiple_of(i * 128, 128), 128)
        before = (v.id_cols[rows, 0:1] == id_row) & (places < steps + i * 128)
        position = jnp.sum(jnp.where(before, 1.0, 0.0), axis=1, keepdims=True)
        angle = position * spacing
        v.cosine[rows, :] = jnp.cos(angle)
        v.sine[rows, :] = jnp.sin(angle)

    for k in range(1, F):
        for op in (t.one, t.two):
            op.relay(k)
    for d in range(1, t.gu_a.steps + 1):
        for op in later:
            op.step(d)
    for op in (t.one, t.two):
        op.finish()
    for op in rows_in:
        op.finish()

    q_cols = pl.ds(pl.multiple_of(head * HEAD, HEAD), HEAD)
    rest_of = HEADS * HEAD
    wide = 2 * HEAD + 3 * RANK
    for j in range(S):
        for f in range(F):
            at = (j * F + f) * kb
            v.w1[at : at + kb, :HEAD] = v.p1_all[j, f, :, q_cols]
            v.w1[at : at + kb, HEAD:] = v.p1_all[j, f, :, rest_of : rest_of + wide]
            v.gain_cols[at : at + kb, :] = v.p1_all[j, f, :, rest_of + wide :].astype(F32)
            at = (j * F + f) * rb
            v.up_b[0, at : at + rb, :] = v.p2_all[j, f, :, q_cols]
            v.up_b[1, at : at + rb, :] = v.p2_all[j, f, :, rest_of : rest_of + HEAD]
            v.up_b[2, at : at + rb, :] = v.p2_all[j, f, :, rest_of + HEAD : rest_of + 2 * HEAD]
            v.out_b[at : at + rb, :] = v.p2_all[j, f, :, rest_of + 2 * HEAD :]
    v.gains[...] = jnp.transpose(v.gain_cols[...])[0:8, :]

    def norm(h, g):
        return (h * lax.rsqrt(jnp.mean(h * h, axis=-1, keepdims=True) + EPSILON) * g).astype(BF)

    for j in range(S):
        v.norm_one[j * seg : j * seg + seg, :] = norm(v.x_all[r, j].astype(F32), v.gains[0:1, :])
    mine = lax.rem(s, G) * R
    for e in range(R):
        v.x_own[e * seg : e * seg + seg, :] = v.x_all[r, mine + e]

    for k in range(1, F):
        for op in later:
            op.relay(k)
    half = HEAD // 2

    @pl.loop(0, L // 256)
    def _(i):
        rows = pl.ds(pl.multiple_of(i * 256, 256), 256)
        pu = mm(v.norm_one[rows, :], v.w1[...])
        u = pu[:, 3 * HEAD :].astype(BF)
        v.u[rows, :] = u
        cosine, sine = v.cosine[rows, :], v.sine[rows, :]
        for k, ref in ((0, v.q_all), (1, v.key)):
            out = pu[:, k * HEAD : (k + 1) * HEAD] + mm(u[:, k * RANK : (k + 1) * RANK], v.up_b[k])
            a, b = out[:, :half], out[:, half:]
            ref[rows, :half] = (a * cosine - b * sine).astype(BF)
            ref[rows, half:] = (b * cosine + a * sine).astype(BF)
        out = pu[:, 2 * HEAD : 3 * HEAD] + mm(u[:, 2 * RANK :], v.up_b[2])
        v.value[rows, :] = out.astype(BF)

    t.gw.finish()
    t.gw_all.start()
    t.cot.step(1)
    t.wo.finish()
    for j in range(S // HEADS):
        for f in range(F):
            at = (j * F + f) * ob
            v.wo[at : at + ob, :] = v.wo_in[j, f]
    from_row = pl.multiple_of(chunk * qlen, own)
    v.query[...] = v.q_all[pl.ds(from_row, qlen), :]
    if C > 1:
        v.part[...] = jnp.zeros(v.part.shape, BF)

    @pl.loop(0, qlen // 128)
    def _(i):
        rows = pl.ds(pl.multiple_of(i * 128, 128), 128)
        here = pl.multiple_of(from_row + i * 128, own)
        allowed = (v.id_cols[pl.ds(here, 128), 0:1] == id_row) & (places <= steps + here)
        scores = jnp.where(allowed, mm_nt(v.query[rows, :], v.key[...]) * scale, MASKED)
        top = jnp.max(scores, axis=-1, keepdims=True)
        lse = top + jnp.log(jnp.sum(jnp.exp(scores - top), axis=-1, keepdims=True))
        probs = jnp.where(allowed, jnp.exp(scores - lse), 0.0)
        v.probs[rows, :] = probs
        mixed = mm(probs.astype(BF), v.value[...]).astype(BF)
        v.mixed[rows, :] = mixed
        out = mm(mixed, v.wo[...]).astype(BF)
        v.part[pl.ds(here // own, 128 // own)] = out.reshape(128 // own, own, out.shape[1])

    t.attn.start()
    t.gw_all.relay()
    for d in range(1, t.attn.steps + 1):
        t.attn.step(d)
    t.attn.finish()
    u_out = v.attn[:, width:].astype(BF)
    v.u_out[...] = u_out
    resid = v.x_own[...].astype(F32) + v.attn[:, :width] + mm(u_out, v.out_b[...])
    v.resid[...] = resid
    v.n2_own[...] = norm(resid, v.gains[1:2, :])

    for d in range(2, t.cot.steps + 1):
        t.cot.step(d)
    for op in later + [t.cot, t.gw_all, t.dw]:
        op.finish()


def forward(given, dims, collective_id):
    S, F, R, seg, kb, rb, ob = dims
    own = R * seg
    L = S * seg
    G = S // R
    C = G // HEADS
    qlen = L // C
    width = given["x"].shape[2]
    per_head = S // HEADS
    lora = width + RANK
    low = functools.partial(jax.ShapeDtypeStruct, dtype=BF)
    full = functools.partial(jax.ShapeDtypeStruct, dtype=F32)

    g = Bag(given)
    wide = g.w_qkv.shape[1] + g.qkv_a.shape[1] + 128
    thin = g.q_b.shape[1] + 2 * HEAD + width
    hb = g.w_down.shape[0]
    hp = (g.w_gu.shape[1] // 2 // S + 127) // 128 * 128

    def like(array, *lead):
        return jax.ShapeDtypeStruct(lead + array.shape, array.dtype)

    outs = dict(
        w1=low((width, 3 * HEAD + 3 * RANK)),
        norm_one=low((L, width)),
        u=low((L, 3 * RANK)),
        query=low((qlen, HEAD)),
        key=low((L, HEAD)),
        value=low((L, HEAD)),
        cosine=full((L, HEAD // 2)),
        sine=full((L, HEAD // 2)),
        probs=full((qlen, L)),
        mixed=low((qlen, HEAD)),
        u_out=low((own, RANK)),
        resid=full((own, width)),
        n2_own=low((own, width)),
        x_own=low((own, width)),
        gains=full((8, width)),
        out_b=low((RANK, width)),
        wo=low((HEAD, lora)),
        up_b=low((3, RANK, HEAD)),
        gw_all=low((F, S, kb + rb, 2 * hp)),
        dw_all=low((F, hb, lora)),
        cot_all=like(g.cot, S),
        gu_a_all=like(g.gu_a, S, F),
        down_b_all=like(g.down_b, S, F),
        gw_mid=low((S, kb + rb, 2 * hp)),
    )
    scratch = dict(
        p1=low((kb, wide)),
        p2=low((rb, thin)),
        p3=low((ob, lora)),
        gws=low((S, kb + rb, 2 * hp)),
        dws=low((hb, lora)),
        p1_all=low((S, F, kb, wide)),
        p2_all=low((S, F, rb, thin)),
        x_all=low((R, S, seg, width)),
        ids_all=like(g.ids, S),
        p3_all=low((F, ob, lora)),
        wo_in=low((per_head, F, ob, lora)),
        id_row=full((1, L)),
        id_cols=full((L, 128)),
        gain_cols=full((width, 128)),
        q_all=low((L, HEAD)),
        part=low((G, own, lora)),
        attn=full((own, lora)),
    )
    slots = named(given, outs, scratch)
    a = Bag(slots)

    far = [id(x) for x in (a.gw_all, a.dw_all, a.cot_all, a.gu_a_all, a.down_b_all, a.gw_mid)]
    far += [id(x) for x in (a.x, a.ids, a.cot, a.gu_a, a.down_b)]

    def to_head(at):
        return [
            (None, row * G + at // per_head * C + c, lax.rem(at, per_head))
            for row in range(R)
            for c in range(C)
        ]

    def op(kind, src, dst, *more):
        return kind(src, *more), src, dst

    ops = dict(
        one=op(Grid, a.p1, a.p1_all, S, F),
        two=op(Grid, a.p2, a.p2_all, S, F),
        ids=op(Line, a.ids, a.ids_all, S),
        three=op(Direct, a.p3, a.p3_all, "fsdp", F, True),
        wo=op(Post, a.p3_all, a.wo_in, per_head, to_head),
        gw=op(Direct, a.gws, a.gw_mid, "seq", S),
        dw=op(Direct, a.dws, a.dw_all, "fsdp", F, True),
        gw_all=op(Square, a.gw_mid, a.gw_all, 0) if F == 4 else op(Direct, a.gw_mid, a.gw_all, "fsdp", F, True),
        cot=op(Line, a.cot, a.cot_all, S),
        gu_a=op(Grid, a.gu_a, a.gu_a_all, S, F),
        down_b=op(Grid, a.down_b, a.down_b_all, S, F),
        attn=op(LineSum, a.part, a.attn, G),
    )
    for j in range(R):
        span = (j * G // 2, (j + 1) * G // 2)
        ops[ROWS[j]] = Line(jax.ShapeDtypeStruct((seg, width), BF), S, span), (a.x, j), (a.x_all, j)
    vmem = pl.BlockSpec(memory_space=pltpu.VMEM)
    away = pl.BlockSpec(memory_space=pl.ANY)
    result = pl.pallas_call(
        functools.partial(front_kernel, dims, slots, ops),
        out_shape=list(outs.values()),
        in_specs=[away if id(slots[name]) in far else vmem for name in given],
        out_specs=[away if id(slots[name]) in far else vmem for name in outs],
        scratch_shapes=[pltpu.VMEM(a.shape, a.dtype) for a in scratch.values()]
        + [entry for kind, _, _ in ops.values() for entry in kind.scratch],
        compiler_params=pltpu.CompilerParams(
            collective_id=collective_id, has_side_effects=True, vmem_limit_bytes=62 << 20
        ),
    )(*given.values())
    return Bag(zip(outs, result))


def norm_back(G_in, h, g):
    q = lax.rsqrt(jnp.mean(h * h, axis=-1, keepdims=True) + EPSILON)
    gg = G_in * g
    d_gain = jnp.sum(G_in * (h * q), axis=0, keepdims=True)
    return d_gain, q * gg - h * (q * q * q) * jnp.mean(gg * h, axis=-1, keepdims=True)


def back_kernel(dims, slots, ops, *refs):
    S, F, R, seg, L, kb, rb, hb, ob = dims
    v, t = unpack(slots, ops, refs)
    own = R * seg
    G = S // R
    C = G // HEADS
    qlen = L // C
    width = v.resid.shape[1]
    scale = HEAD**-0.5
    s = lax.axis_index("seq")
    chunk = lax.rem(s, C)
    meet([("seq", S), ("fsdp", F)])
    t.down.start()

    gain_two, back = norm_back(v.d_n2[...], v.resid[...], v.gains[1:2, :])
    d_resid = v.cot_own[...].astype(F32) + back
    v.d_resid[...] = d_resid
    v.d_attn_own[...] = d_resid.astype(BF)
    t.d_attn.start()
    activations = (v.resid[...] + v.ffn_sum[...]).astype(BF)
    for j in range(R):
        v.act_rows[j] = activations[j * seg : j * seg + seg, :]
    t.activations.start()
    for put, got, home in ((v.s_gu_a, v.f_gu_a, t.gu_a_home), (v.s_down_b, v.f_down_b, t.down_b_home)):
        put[...] = got[...].astype(BF)
        home.start()
    t.gate_home.start()
    t.up_home.start()
    for d in range(1, t.d_attn.steps + 1):
        t.d_attn.step(d)
    t.d_attn.finish()

    blocks = qlen // own
    first = chunk * blocks
    v.da[:, :width] = v.d_attn[pl.ds(first, blocks)].reshape(qlen, width)
    v.da[:, width:] = mm_nt(v.da[:, :width], v.out_b[...]).astype(BF)
    v.d_mixed[...] = mm_nt(v.da[...], v.wo[...]).astype(BF)

    @pl.loop(0, qlen // 128)
    def _(i):
        rows = pl.ds(pl.multiple_of(i * 128, 128), 128)
        p = v.probs[rows, :]
        d_probs = mm_nt(v.d_mixed[rows, :], v.value[...])
        delta = jnp.sum(p * d_probs, axis=-1, keepdims=True)
        v.d_scores[rows, :] = (p * (d_probs - delta)).astype(BF)
        v.probs_low[rows, :] = p.astype(BF)

    def unrot(g, rows):
        half = HEAD // 2
        cosine, sine = v.cosine[rows, :], v.sine[rows, :]
        a, b = g[:, :half], g[:, half:]
        return (a * cosine + b * sine).astype(BF), (b * cosine - a * sine).astype(BF)

    half = HEAD // 2
    mine = pl.ds(pl.multiple_of(chunk * qlen, own), qlen)
    if C > 1:
        v.d_pu[:, :HEAD] = jnp.zeros((L, HEAD), BF)
    v.d_pu[mine, :half], v.d_pu[mine, half:HEAD] = unrot(mm(v.d_scores[...], v.key[...]) * scale, mine)
    every = pl.ds(0, L)
    v.d_pu[:, HEAD : HEAD + half], v.d_pu[:, HEAD + half : 2 * HEAD] = unrot(
        mm_tn(v.d_scores[...], v.query[...]) * scale, every
    )
    v.d_pu[:, 2 * HEAD : 3 * HEAD] = mm_tn(v.probs_low[...], v.d_mixed[...]).astype(BF)
    for k in range(3):
        v.d_pu[:, 3 * HEAD + k * RANK : 3 * HEAD + (k + 1) * RANK] = mm_nt(
            v.d_pu[:, k * HEAD : (k + 1) * HEAD], v.up_b[k]
        ).astype(BF)

    @pl.loop(0, L // 256)
    def _(i):
        rows = pl.ds(pl.multiple_of(i * 256, 256), 256)
        out = mm_nt(v.d_pu[rows, :], v.w1[...]).astype(BF)
        v.d_attn[pl.ds(i * (256 // own), 256 // own)] = out.reshape(256 // own, own, width)

    t.d_n1.start()

    out = mm_tn(v.mixed[...], v.da[...]).astype(BF)
    for j in range(HEAD // ob):
        v.t_out[j % F, j // F] = out[j * ob : j * ob + ob, :]
    t.out.start()
    out = mm_tn(v.norm_one[...], v.d_pu[:, :HEAD]).astype(BF)
    for b in range(S * F):
        v.t_q[b % F, b // F] = out[b * kb : b * kb + kb, :]
    t.q.start()
    out = mm_tn(v.u[:, :RANK], v.d_pu[:, :HEAD]).astype(BF)
    for b in range(S * F):
        v.t_qb[b % F, b // F] = out[b * rb : b * rb + rb, :]
    t.qb.start()
    t.d_n1.step(1)

    @pl.loop(0, v.t_1.shape[3] // 256)
    def _(i):
        cols = pl.ds(pl.multiple_of(i * 256, 256), 256)
        src = pl.ds(pl.multiple_of(i * 256 + 256, 256), 256)
        out = mm_tn(v.norm_one[...], v.d_pu[:, src]).astype(BF)
        for b in range(S * F):
            v.t_1[b // F, b % F, :, cols] = out[b * kb : b * kb + kb, :]

    t.one.start()
    for d in range(2, t.d_n1.steps + 1):
        t.d_n1.step(d)
    for k in range(2):
        out = mm_tn(
            v.u[:, (k + 1) * RANK : (k + 2) * RANK], v.d_pu[:, (k + 1) * HEAD : (k + 2) * HEAD]
        ).astype(BF)
        for b in range(S * F):
            v.t_2[b // F, b % F, :, k * HEAD : (k + 1) * HEAD] = out[b * rb : b * rb + rb, :]
    out = mm_tn(v.u_out[...], v.d_attn_own[...]).astype(BF)
    for b in range(S * F):
        v.t_2[b // F, b % F, :, 2 * HEAD :] = out[b * rb : b * rb + rb, :]
    t.two.start()

    t.d_n1.finish()
    gain_one, back = norm_back(v.d_n1_sum[...], v.x_own[...].astype(F32), v.gains[0:1, :])
    grad_input = v.d_resid[...] + back
    for j in range(R):
        v.grad_rows[j] = grad_input[j * seg : j * seg + seg, :]
    t.grad_input.start()
    both = jnp.concatenate([gain_one, gain_two, jnp.zeros((126, width), F32)], axis=0)
    both = jnp.transpose(both)
    for b in range(S * F):
        v.t_3[b // F, b % F] = both[b * kb : b * kb + kb, :].astype(BF)
    t.three.start()
    late = [t.one, t.two, t.three]
    for op in late:
        op.step(1)
    for move, got, put, home in (
        (t.q, v.r_q, v.s_q, t.q_home),
        (t.qb, v.r_qb, v.s_qb, t.qb_home),
        (t.out, v.r_out, v.s_out, t.out_home),
    ):
        move.finish()
        for k in range(put.shape[0]):
            put[k] = over_fsdp(got, (k,), F).astype(BF)
        home.start()
    for d in range(2, t.one.steps + 1):
        for op in late:
            op.step(d)
    for op in late:
        op.finish()
    for put, got, home in (
        (v.s_one, v.f_one, t.one_home),
        (v.s_two, v.f_two, t.two_home),
        (v.s_three, v.f_three, t.three_home),
    ):
        put[...] = got[...].astype(BF)
        home.start()
    homes = [t.one_home, t.two_home, t.three_home, t.gu_a_home, t.down_b_home]
    homes += [t.gate_home, t.up_home, t.down]
    for move in [t.grad_input, t.activations, t.q_home, t.qb_home, t.out_home] + homes:
        move.finish()


def backward(given, dims, collective_id):
    S, F, R, seg, L, kb, rb, hb, ob = dims
    own = R * seg
    G = S // R
    C = G // HEADS
    qlen = L // C
    width = given["resid"].shape[1]
    per_head = S // HEADS
    hp = given["sum_up"].shape[2]
    lora = width + RANK
    one = 2 * HEAD + 3 * RANK
    two = 2 * HEAD + width
    low = functools.partial(jax.ShapeDtypeStruct, dtype=BF)
    full = functools.partial(jax.ShapeDtypeStruct, dtype=F32)

    def to_rows(at):
        return [(j, lax.rem(at, G) * R + j, at // G) for j in range(R)]

    def to_out(at):
        return [
            (j, lax.rem(at, G) // C * per_head + j, at // G * C + lax.rem(at, C)) for j in range(per_head)
        ]

    outs = dict(
        act_home=low((R, seg, width)),
        grad_home=full((R, seg, width)),
        o_q=low((S, kb, HEAD)),
        o_qb=low((S, rb, HEAD)),
        o_out=low((R * C, ob, lora)),
        o_gate=low((S, kb + rb, hp)),
        o_up=low((S, kb + rb, hp)),
        o_down=low((F, hb, lora)),
        o_one=low((F, kb, one)),
        o_two=low((F, rb, two)),
        o_three=low((F, kb, 128)),
        o_gu_a=low((F, kb, 2 * RANK)),
        o_down_b=low((F, rb, width)),
    )
    scratch = dict(
        d_resid=full((own, width)),
        d_attn_own=low((own, width)),
        d_attn=low((G, own, width)),
        da=low((qlen, lora)),
        d_mixed=low((qlen, HEAD)),
        d_scores=low((qlen, L)),
        probs_low=low((qlen, L)),
        d_pu=low((L, 3 * HEAD + 3 * RANK)),
        d_n1_sum=full((own, width)),
        grad_rows=full((R, seg, width)),
        act_rows=low((R, seg, width)),
        t_out=low((F, per_head, ob, lora)),
        t_q=low((F, S, kb, HEAD)),
        t_qb=low((F, S, rb, HEAD)),
        t_1=low((S, F, kb, one)),
        t_2=low((S, F, rb, two)),
        t_3=low((S, F, kb, 128)),
        r_out=low((F, per_head, ob, lora)),
        r_q=low((F, S, kb, HEAD)),
        r_qb=low((F, S, rb, HEAD)),
        s_out=low((per_head, ob, lora)),
        s_q=low((S, kb, HEAD)),
        s_qb=low((S, rb, HEAD)),
    )
    scratch.update(
        f_one=full((F, kb, one)),
        s_one=low((F, kb, one)),
        f_two=full((F, rb, two)),
        s_two=low((F, rb, two)),
        f_three=full((F, kb, 128)),
        s_three=low((F, kb, 128)),
        s_gu_a=low((F, kb, 2 * RANK)),
        s_down_b=low((F, rb, width)),
    )
    slots = named(given, outs, scratch)
    a = Bag(slots)

    def op(kind, src, dst, *more):
        return kind(src, *more), src, dst

    ops = dict(
        down=op(Direct, a.part_down, a.o_down, "fsdp", F),
        d_attn=op(Line, a.d_attn_own, a.d_attn, G),
        d_n1=op(LineSum, a.d_attn, a.d_n1_sum, G),
        out=op(Direct, a.t_out, a.r_out, "fsdp", F),
        q=op(Direct, a.t_q, a.r_q, "fsdp", F),
        qb=op(Direct, a.t_qb, a.r_qb, "fsdp", F),
        one=op(LineSum, a.t_1, a.f_one, S),
        two=op(LineSum, a.t_2, a.f_two, S),
        three=op(LineSum, a.t_3, a.f_three, S),
        grad_input=op(Post, a.grad_rows, a.grad_home, R, to_rows),
        activations=op(Post, a.act_rows, a.act_home, R, to_rows),
        q_home=op(Direct, a.s_q, a.o_q, "seq", S),
        qb_home=op(Direct, a.s_qb, a.o_qb, "seq", S),
        out_home=op(Post, a.s_out, a.o_out, R * C, to_out),
        gate_home=op(Direct, a.sum_gate, a.o_gate, "seq", S),
        up_home=op(Direct, a.sum_up, a.o_up, "seq", S),
    )
    ops.update(
        one_home=op(Direct, a.s_one, a.o_one, "fsdp", F),
        two_home=op(Direct, a.s_two, a.o_two, "fsdp", F),
        three_home=op(Direct, a.s_three, a.o_three, "fsdp", F),
        gu_a_home=op(Direct, a.s_gu_a, a.o_gu_a, "fsdp", F),
        down_b_home=op(Direct, a.s_down_b, a.o_down_b, "fsdp", F),
    )
    far = [id(x) for x in (a.part_down, a.sum_gate, a.sum_up)]
    vmem = pl.BlockSpec(memory_space=pltpu.VMEM)
    away = pl.BlockSpec(memory_space=pl.ANY)
    result = pl.pallas_call(
        functools.partial(back_kernel, dims, slots, ops),
        out_shape=list(outs.values()),
        in_specs=[away if id(slots[name]) in far else vmem for name in given],
        out_specs=[away] * len(outs),
        scratch_shapes=[pltpu.VMEM(a.shape, a.dtype) for a in scratch.values()]
        + [entry for kind, _, _ in ops.values() for entry in kind.scratch],
        compiler_params=pltpu.CompilerParams(
            collective_id=collective_id, has_side_effects=True, vmem_limit_bytes=62 << 20
        ),
    )(*given.values())
    return Bag(zip(outs, result))


def finish_kernel(dims, slots, *refs):
    S, F, R, kb, rb, hb, ob, hidden, hl, width = dims
    buffers, sem = refs[len(slots) : -1], refs[-1]
    copies = [pltpu.make_async_copy(refs[k], buffers[k], sem.at[k]) for k in range(len(buffers))]
    for copy in copies:
        copy.start()
    for copy in copies:
        copy.wait()
    v = Bag(zip(slots, buffers + refs[len(buffers) : len(slots)]))
    G = S // R
    C = G // HEADS
    v.activations[...] = v.act_home[...]
    v.grad_input[...] = v.grad_home[...]

    def of_head(ref, head):
        parts = [ref[row * G + head * C + c].astype(F32) for row in range(R) for c in range(C)]
        return sum(parts[1:], parts[0])

    for head in range(HEADS):
        cols = slice(head * HEAD, head * HEAD + HEAD)
        v.w_qkv[:, cols] = of_head(v.o_q, head)
        v.q_b[:, cols] = of_head(v.o_qb, head)
    out = over_fsdp(v.o_one, (), F)
    v.w_qkv[:, HEADS * HEAD :] = out[:, : 2 * HEAD]
    v.qkv_a[...] = out[:, 2 * HEAD :]
    out = over_fsdp(v.o_two, (), F)
    v.kv_b[0] = out[:, :HEAD]
    v.kv_b[1] = out[:, HEAD : 2 * HEAD]
    v.out_b[...] = out[:, 2 * HEAD :]
    v.gains[...] = over_fsdp(v.o_three, (), F)
    v.gu_a[...] = over_fsdp(v.o_gu_a, (), F)
    v.down_b[...] = over_fsdp(v.o_down_b, (), F)
    out = over_fsdp(v.o_down, (), F)
    v.w_down[...] = out[:, :width]
    v.down_a[...] = out[:, width:]
    out = over_fsdp(v.o_out, (), R * C)
    v.w_out[...] = out[:, :width]
    v.out_a[...] = out[:, width:]
    for half, ref in ((0, v.o_gate), (1, v.o_up)):
        for j in range(S):
            at = half * hidden + j * hl
            v.w_gu[:, at : at + hl] = ref[j, 0:kb, :hl].astype(F32)
            v.gu_b[half, :, j * hl : j * hl + hl] = ref[j, kb:, :hl].astype(F32)


def finish(got, dims):
    S, F, R, kb, rb, hb, ob, hidden, hl, width = dims
    full = functools.partial(jax.ShapeDtypeStruct, dtype=F32)
    given = vars(got)
    outs = dict(
        activations=got.act_home,
        grad_input=got.grad_home,
        w_qkv=full((kb, (HEADS + 2) * HEAD)),
        qkv_a=full((kb, 3 * RANK)),
        q_b=full((rb, HEADS * HEAD)),
        kv_b=full((2, rb, HEAD)),
        w_out=full((ob, width)),
        out_a=full((ob, RANK)),
        out_b=full((rb, width)),
        w_gu=full((kb, 2 * hidden)),
        gu_a=full((kb, 2 * RANK)),
        gu_b=full((2, rb, hidden)),
        w_down=full((hb, width)),
        down_a=full((hb, RANK)),
        down_b=full((rb, width)),
        gains=full((kb, 128)),
    )
    slots = named(given, outs)
    vmem = pl.BlockSpec(memory_space=pltpu.VMEM)
    result = pl.pallas_call(
        functools.partial(finish_kernel, dims, slots),
        out_shape=[jax.ShapeDtypeStruct(x.shape, x.dtype) for x in outs.values()],
        in_specs=[pl.BlockSpec(memory_space=pl.ANY)] * len(given),
        out_specs=[vmem] * len(outs),
        scratch_shapes=[pltpu.VMEM(x.shape, x.dtype) for x in given.values()]
        + [pltpu.SemaphoreType.DMA((len(given),))],
        compiler_params=pltpu.CompilerParams(vmem_limit_bytes=62 << 20),
    )(*given.values())
    return Bag(zip(outs, result))


def shards(
    S,
    F,
    layer_input,
    document_numbers,
    cotangent,
    w_qkv,
    qkv_a,
    q_b,
    kv_b,
    w_out,
    out_a,
    out_b,
    w_gu,
    gu_a,
    gu_b,
    w_down,
    down_a,
    down_b,
    gain_a,
    gain_f,
):
    R, seg, width = layer_input.shape
    L = seg * S
    own = R * seg
    G = S // R
    C = G // HEADS
    scale = HEAD**-0.5
    kb = w_qkv.shape[0]
    rb = q_b.shape[0]
    hb = w_down.shape[0]
    ob = w_out.shape[0]
    hidden = w_gu.shape[1] // 2
    hl = hidden // S
    hp = (hl + 127) // 128 * 128
    s = lax.axis_index("seq")
    r = s // G
    head = lax.rem(s, G) // C
    chunk = lax.rem(s, C)
    qlen = L // C

    on_seq = ("seq", S)
    h = forward(
        dict(
            x=layer_input,
            ids=document_numbers,
            cot=cotangent,
            w_qkv=w_qkv,
            qkv_a=qkv_a,
            gain_pair=jnp.pad(jnp.stack([gain_a, gain_f], axis=1), ((0, 0), (0, 126))),
            q_b=q_b,
            kv_b=kv_b,
            add_out_b=out_b,
            w_out=w_out,
            out_a=out_a,
            w_gu=w_gu,
            gu_b=gu_b,
            w_down=w_down,
            down_a=down_a,
            gu_a=gu_a,
            down_b=down_b,
        ),
        (S, F, R, seg, kb, rb, ob),
        0,
    )
    cot = h.cot_all

    dims = (S, F, R, seg, kb, rb, hb, hl, hp)
    apart = S * own > 1024
    ffn = feed_forward(
        dict(
            n2_own=h.n2_own,
            gw=h.gw_all,
            dw=h.dw_all,
            cot=cot,
            gu_a=h.gu_a_all,
            down_b=h.down_b_all.reshape(RANK, width),
        ),
        dims,
        apart,
        5,
    )
    if apart:
        ffn.ffn_sum, ffn.f_gu_a, ffn.f_down_b = transfer(
            [LineSum(x, S) for x in (ffn.ffn_part, ffn.g_gu_a, ffn.g_down_b)], [on_seq], 7
        )
    cot_own = lax.dynamic_slice_in_dim(cot, lax.rem(s, G) * R, R, 0)
    cot_own = lax.dynamic_index_in_dim(cot_own, r, 1, keepdims=False).reshape(own, width)

    got = backward(
        dict(
            d_n2=ffn.dn_sum,
            cot_own=cot_own,
            resid=h.resid,
            gains=h.gains,
            x_own=h.x_own,
            out_b=h.out_b,
            wo=h.wo,
            w1=h.w1,
            up_b=h.up_b,
            norm_one=h.norm_one,
            u=h.u,
            u_out=h.u_out,
            query=h.query,
            key=h.key,
            value=h.value,
            cosine=h.cosine,
            sine=h.sine,
            probs=h.probs,
            mixed=h.mixed,
            ffn_sum=ffn.ffn_sum,
            f_gu_a=ffn.f_gu_a,
            f_down_b=ffn.f_down_b,
            part_down=ffn.part_down,
            sum_gate=ffn.sum_gate,
            sum_up=ffn.sum_up,
        ),
        (S, F, R, seg, L, kb, rb, hb, ob),
        8,
    )

    done = finish(got, (S, F, R, kb, rb, hb, ob, hidden, hl, width))
    return (
        done.activations,
        done.grad_input,
        done.w_qkv,
        done.qkv_a,
        done.q_b,
        done.kv_b,
        done.w_out,
        done.out_a,
        done.out_b,
        done.w_gu,
        done.gu_a,
        done.gu_b,
        done.w_down,
        done.down_a,
        done.down_b,
        done.gains[:, 0],
        done.gains[:, 1],
    )


def solution(mesh):
    both = P(("seq", "fsdp"), None)
    second = P(None, ("seq", "fsdp"), None)
    tokens = P("fsdp", "seq", None)
    gain = P(("seq", "fsdp"))
    return jax.shard_map(
        functools.partial(shards, mesh.shape["seq"], mesh.shape["fsdp"]),
        mesh=mesh,
        in_specs=(tokens, P("fsdp", "seq"), tokens)
        + (both, both, both, second, both, both, both, both, both, second, both, both, both, gain, gain),
        out_specs=(tokens, tokens)
        + (both, both, both, second, both, both, both, both, both, second, both, both, both, gain, gain),
        check_vma=False,
    )
```

```python
import functools
import math

import jax
import jax.numpy as jnp
from jax import lax
from jax.experimental import pallas as pl
from jax.experimental.pallas import tpu as pltpu
from jax.sharding import PartitionSpec as P

HEADS = 4
HEAD = 256
RANK = 256
EPSILON = 1e-06
ROPE_BASE = 10000.0
MASKED = -1e30
FFN = "ffn"
ROWS = tuple("abcdefgh")
MESH = pl.DeviceIdType.MESH
BF = jnp.bfloat16
F32 = jnp.float32


def mm(left, right):
    return jnp.dot(left, right, preferred_element_type=F32)


def mm_tn(left, right):
    return lax.dot_general(left, right, (((0,), (0,)), ((), ())), preferred_element_type=F32)


def mm_nt(left, right):
    return lax.dot_general(left, right, (((1,), (1,)), ((), ())), preferred_element_type=F32)


def remote(src, dst, send, recv, peer):
    return pltpu.make_async_remote_copy(
        src_ref=src, dst_ref=dst, send_sem=send, recv_sem=recv, device_id=peer, device_id_type=MESH
    )


class Bag:
    def __init__(self, entries=()):
        self.__dict__.update(entries)


class Slot(jax.ShapeDtypeStruct):
    pass


def named(*groups):
    slots = {}
    for group in groups:
        for name, a in group.items():
            slots[name] = Slot(a.shape, a.dtype)
    return slots


def unpack(slots, ops, refs):
    refs = list(refs)
    where = {id(slot): ref for slot, ref in zip(slots.values(), refs)}
    v = Bag(zip(slots, refs))
    rest = refs[len(slots) :]
    bound = Bag()
    for name, (op, src, dst) in ops.items():
        take = len(op.scratch)
        src, dst = (
            where[id(x[0])].at[x[1]] if isinstance(x, tuple) else where[id(x)] for x in (src, dst)
        )
        op.bind(src, dst, *rest[:take])
        setattr(bound, name, op)
        rest = rest[take:]
    return v, bound


class Direct:
    steps = 0

    def relay(self):
        pass

    def __init__(self, x, axis, size, spread=False):
        self.x, self.axis, self.size, self.spread = x, axis, size, spread
        shape = ((size,) if spread else ()) + x.shape
        self.out = jax.ShapeDtypeStruct(shape, x.dtype)
        self.scratch = [
            pltpu.SemaphoreType.DMA,
            pltpu.SemaphoreType.DMA((size,)),
            pltpu.SemaphoreType.DMA((size,)),
        ]

    def bind(self, x_ref, o_ref, local, send, recv):
        me = lax.axis_index(self.axis)
        self.copies = []
        for k in range(1, self.size):
            peer = lax.rem(me + k, self.size)
            src = x_ref if self.spread else x_ref.at[peer]
            self.copies.append(remote(src, o_ref.at[me], send.at[k], recv.at[k], {self.axis: peer}))
        src = x_ref if self.spread else x_ref.at[me]
        self.copies.append(pltpu.make_async_copy(src, o_ref.at[me], local))

    def start(self):
        for copy in self.copies:
            copy.start()

    def finish(self):
        for copy in self.copies:
            copy.wait()


class Square:
    steps = 0

    def __init__(self, x, dim):
        self.x = x
        size = x.shape[dim]
        half = size // 2 if dim == 0 else size // 256 * 128
        first = (slice(None),) * dim
        self.cut = (first + (pl.ds(0, half),), first + (pl.ds(half, size - half),))
        self.out = jax.ShapeDtypeStruct((4,) + x.shape, x.dtype)
        self.scratch = [
            pltpu.SemaphoreType.DMA,
            pltpu.SemaphoreType.DMA((3, 2)),
            pltpu.SemaphoreType.DMA((3, 2)),
        ]

    def bind(self, x_ref, o_ref, local, send, recv):
        me = lax.axis_index("fsdp")
        near_x, near_y, far = me + 1 - 2 * lax.rem(me, 2), lax.rem(me + 2, 4), 3 - me
        cut = self.cut

        def move(src, owner, part, way, peer):
            dst = o_ref.at[owner].at[cut[part]]
            src = dst if src is None else src.at[cut[part]]
            return remote(src, dst, send.at[way, part], recv.at[way, part], {"fsdp": peer})

        self.to_x = [move(x_ref, me, part, 0, near_x) for part in range(2)]
        self.to_y = [move(x_ref, me, part, 1, near_y) for part in range(2)]
        self.from_x = [move(None, near_x, part, 0, near_x) for part in range(2)]
        self.from_y = [move(None, near_y, part, 1, near_y) for part in range(2)]
        self.on_y = move(None, near_x, 0, 2, near_y)
        self.on_x = move(None, near_y, 1, 2, near_x)
        self.from_far = [move(None, far, part, 2, near_x) for part in range(2)]
        self.own = pltpu.make_async_copy(x_ref, o_ref.at[me], local)

    def start(self):
        self.to_x[0].start()
        self.to_y[1].start()
        self.to_x[1].start()
        self.to_y[0].start()
        self.own.start()

    def relay(self):
        self.from_x[0].wait_recv()
        self.on_y.start()
        self.from_y[1].wait_recv()
        self.on_x.start()

    def finish(self):
        self.from_x[1].wait_recv()
        self.from_y[0].wait_recv()
        for part in range(2):
            self.from_far[part].wait_recv()
            self.to_x[part].wait_send()
            self.to_y[part].wait_send()
        self.on_y.wait_send()
        self.on_x.wait_send()
        self.own.wait()


class Post:
    steps = 0

    def __init__(self, x, slots, sends):
        self.slots, self.sends = slots, sends
        self.x = x
        count = len(sends(0))
        self.scratch = [
            pltpu.SemaphoreType.DMA((count,)),
            pltpu.SemaphoreType.DMA((count,)),
            pltpu.SemaphoreType.DMA((slots,)),
        ]

    def bind(self, x_ref, o_ref, local, send, recv):
        s = lax.axis_index("seq")
        self.s = s
        self.plan = []
        for k, (block, device, slot) in enumerate(self.sends(s)):
            src = x_ref if block is None else x_ref.at[block]
            away = remote(src, o_ref.at[slot], send.at[k], recv.at[slot], {"seq": device})
            here = pltpu.make_async_copy(src, o_ref.at[slot], recv.at[slot])
            self.plan.append((device, away, here))
        self.arrive = [
            pltpu.make_async_copy(o_ref.at[k], o_ref.at[k], recv.at[k]) for k in range(self.slots)
        ]

    def start(self):
        for device, away, here in self.plan:
            pl.when(device != self.s)(away.start)
            pl.when(device == self.s)(here.start)

    def finish(self):
        for copy in self.arrive:
            copy.wait()
        for device, away, here in self.plan:
            pl.when(device != self.s)(away.wait_send)


class Line:
    def __init__(self, x, line, span=None):
        self.x, self.line = x, line
        self.lo, self.hi = span or (0, line // 2)
        self.steps = line // 2 - 1
        self.out = jax.ShapeDtypeStruct((line,) + x.shape, x.dtype)
        self.scratch = [
            pltpu.SemaphoreType.DMA,
            pltpu.SemaphoreType.DMA((2 * line,)),
            pltpu.SemaphoreType.DMA((line,)),
        ]

    def bind(self, x_ref, o_ref, local, send, recv):
        self.x_ref, self.o_ref, self.send, self.recv = x_ref, o_ref, send, recv
        line = self.line
        s = lax.axis_index("seq")
        base = s // line * line
        self.n2 = line // 2
        self.i = s - base
        self.p, self.core = self.i // 2, lax.rem(self.i, 2)
        self.sib = s + 1 - 2 * self.core
        self.left = base + lax.rem(self.i + line - 2, line)
        self.right = base + lax.rem(self.i + 2, line)
        self.own = pltpu.make_async_copy(x_ref, o_ref.at[self.i], local)
        self.inside = (self.p >= self.lo) & (self.p < self.hi)

    def copy(self, blk, src, dst, k):
        return remote(src, self.o_ref.at[blk], self.send.at[k], self.recv.at[blk], {"seq": dst})

    def start(self):
        @pl.when(self.p + 1 < self.hi)
        def _():
            self.copy(self.i, self.x_ref, self.right, 0).start()

        @pl.when(self.p > self.lo)
        def _():
            self.copy(self.i, self.x_ref, self.left, 1).start()

        @pl.when(self.inside)
        def _():
            self.copy(self.i, self.x_ref, self.sib, 2).start()

        self.own.start()

    def step(self, d):
        p, n2, o = self.p, self.n2, self.o_ref

        @pl.when((p - d >= 0) & (p < self.hi))
        def _():
            blk = self.i - 2 * d
            self.copy(blk, o.at[blk], self.left, 0).wait_recv()

            @pl.when(p + 1 < self.hi)
            def _():
                self.copy(blk, o.at[blk], self.right, 4 * d).start()

            @pl.when(self.inside)
            def _():
                self.copy(blk, o.at[blk], self.sib, 4 * d + 1).start()

        @pl.when((p + d < n2) & (p >= self.lo))
        def _():
            blk = self.i + 2 * d
            self.copy(blk, o.at[blk], self.right, 0).wait_recv()

            @pl.when(p > self.lo)
            def _():
                self.copy(blk, o.at[blk], self.left, 4 * d + 2).start()

            @pl.when(self.inside)
            def _():
                self.copy(blk, o.at[blk], self.sib, 4 * d + 3).start()

    def from_core(self, q):
        blk = 2 * q + 1 - self.core
        self.copy(blk, self.o_ref.at[blk], self.sib, 0).wait_recv()

    def finish(self):
        @pl.when(self.inside)
        def _():
            for q in range(self.n2):
                self.from_core(q)

        self.settle()
        self.own.wait()

    def settle(self):
        p, n2 = self.p, self.n2

        def sent(k, sure):
            @pl.when(sure)
            def _():
                self.copy(self.i, self.x_ref, self.sib, k).wait_send()

        sent(0, p + 1 < self.hi)
        sent(1, p > self.lo)
        sent(2, self.inside)
        for d in range(1, n2):
            sent(4 * d, (p - d >= 0) & (p + 1 < self.hi))
            sent(4 * d + 1, (p - d >= 0) & self.inside)
            sent(4 * d + 2, (p + d < n2) & (p > self.lo))
            sent(4 * d + 3, (p + d < n2) & self.inside)


class Grid:
    def __init__(self, x, S, F):
        self.x, self.S, self.F = x, S, F
        self.n2 = n2 = S // 2
        self.steps = n2 - 1
        self.out = jax.ShapeDtypeStruct((S, F) + x.shape, x.dtype)
        self.scratch = [
            pltpu.SemaphoreType.DMA,
            pltpu.SemaphoreType.DMA((2, n2)),
            pltpu.SemaphoreType.DMA((n2, F)),
            pltpu.SemaphoreType.DMA((n2, F)),
            pltpu.SemaphoreType.DMA((S, F)),
        ]

    def bind(self, x_ref, o_ref, local, z_send, f_send, s_send, recv):
        self.x_ref, self.o_ref, self.recv = x_ref, o_ref, recv
        self.z_send, self.f_send, self.s_send = z_send, f_send, s_send
        s, self.f = lax.axis_index("seq"), lax.axis_index("fsdp")
        self.p, self.core = s // 2, lax.rem(s, 2)
        self.s = s
        self.sib = {"seq": s + 1 - 2 * self.core}
        self.left = {"seq": lax.rem(s + self.S - 2, self.S)}
        self.right = {"seq": lax.rem(s + 2, self.S)}
        self.own = pltpu.make_async_copy(x_ref, o_ref.at[s, self.f], local)
        self.square = self.F == 4
        self.near = (1, 2) if self.square else range(1, self.F)

    def place(self, k):
        f = self.f
        if self.square:
            return (f, f + 1 - 2 * lax.rem(f, 2), lax.rem(f + 2, 4), 3 - f)[k]
        return lax.rem(f + self.F - k, self.F)

    def peer(self, k):
        return {"fsdp": self.place(k) if self.square else lax.rem(self.f + k, self.F)}

    def copy(self, q, f, send, peer):
        blk = 2 * q + self.core
        dst = self.o_ref.at[blk, f]
        return remote(dst, dst, send, self.recv.at[blk, f], peer)

    def first(self, send, peer):
        return remote(self.x_ref, self.o_ref.at[self.s, self.f], send, self.recv.at[self.s, self.f], peer)

    def start(self):
        p, n2 = self.p, self.n2

        @pl.when(p < n2 - 1)
        def _():
            self.first(self.z_send.at[0, p], self.right).start()

        @pl.when(p > 0)
        def _():
            self.first(self.z_send.at[1, p], self.left).start()

        for k in self.near:
            self.first(self.f_send.at[p, k], self.peer(k)).start()
        self.first(self.s_send.at[p, 0], self.sib).start()
        self.own.start()

    def pass_on(self, q):
        for k in self.near:
            self.copy(q, self.f, self.f_send.at[q, k], self.peer(k)).start()
        self.copy(q, self.f, self.s_send.at[q, 0], self.sib).start()

    def arrived(self, q, f):
        self.copy(q, f, self.s_send.at[q, 0], self.sib).wait_recv()

    def step(self, d):
        p, n2 = self.p, self.n2

        @pl.when(p - d >= 0)
        def _():
            self.arrived(p - d, self.f)

            @pl.when(p < n2 - 1)
            def _():
                self.copy(p - d, self.f, self.z_send.at[0, p - d], self.right).start()

            self.pass_on(p - d)

        @pl.when(p + d < n2)
        def _():
            self.arrived(p + d, self.f)

            @pl.when(p > 0)
            def _():
                self.copy(p + d, self.f, self.z_send.at[1, p + d], self.left).start()

            self.pass_on(p + d)

    def relay(self, k):
        f = self.place(k)
        for q in range(self.n2):
            self.arrived(q, f)
            self.copy(q, f, self.s_send.at[q, k], self.sib).start()
            if self.square and ((k == 1 and q < self.n2 // 2) or (k == 2 and q >= self.n2 // 2)):
                self.copy(q, f, self.f_send.at[q, 3], self.peer(3 - k)).start()

    def finish(self):
        p, n2 = self.p, self.n2
        for q in range(n2):
            for k in range(self.F):
                f = self.place(k)
                blk = 2 * q + 1 - self.core
                dst = self.o_ref.at[blk, f]
                remote(dst, dst, self.s_send.at[q, k], self.recv.at[blk, f], self.sib).wait_recv()
        for q in range(n2):

            @pl.when((q <= p) & (p < n2 - 1))
            def _():
                self.first(self.z_send.at[0, q], self.right).wait_send()

            @pl.when((q >= p) & (p > 0))
            def _():
                self.first(self.z_send.at[1, q], self.left).wait_send()

            for k in range(self.F):
                self.first(self.s_send.at[q, k], self.sib).wait_send()
                if k:
                    self.first(self.f_send.at[q, k], self.sib).wait_send()
        self.own.wait()


class LineSum:
    vmem = True

    def __init__(self, x, line):
        self.x, self.line = x, line
        self.n2 = n2 = line // 2
        self.steps = n2 - 1
        blk = x.shape[1:]
        self.out = jax.ShapeDtypeStruct(blk, F32)
        self.scratch = [pltpu.VMEM((n2,) + blk, BF), pltpu.VMEM((n2 + 1,) + blk, BF)] + [
            pltpu.SemaphoreType.DMA((3 * n2,)),
            pltpu.SemaphoreType.DMA((3 * n2,)),
        ]

    def bind(self, x_ref, o_ref, mine, came, send, recv):
        self.x_ref, self.o_ref, self.mine, self.came = x_ref, o_ref, mine, came
        line, n2 = self.line, self.n2
        s = lax.axis_index("seq")
        base = s // line * line
        i = s - base
        self.p, self.core = i // 2, lax.rem(i, 2)
        sib = {"seq": s + 1 - 2 * self.core}
        left = {"seq": base + lax.rem(i + line - 2, line)}
        right = {"seq": base + lax.rem(i + 2, line)}
        core = self.core
        self.hand_over = lambda q: remote(
            x_ref.at[2 * q + 1 - core], mine.at[q], send.at[q], recv.at[q], sib
        )
        self.rightward = lambda q: remote(
            mine.at[q], came.at[q + 1], send.at[n2 + q], recv.at[n2 + q], right
        )
        self.leftward = lambda q: remote(
            mine.at[q], came.at[q], send.at[2 * n2 + q], recv.at[2 * n2 + q], left
        )
        order = []
        for k in range((n2 + 1) // 2):
            order += [n2 - 1 - k] + ([k] if k != n2 - 1 - k else [])
        self.order = order

    def start(self):
        for q in self.order:
            self.hand_over(q).start()

    def add(self, q, other):
        self.mine[q] = (self.mine[q].astype(F32) + self.came[other].astype(F32)).astype(BF)

    def step(self, d):
        p, n2 = self.p, self.n2
        if d == 1:
            for q in self.order:
                self.hand_over(q).wait_recv()
                own = self.x_ref[2 * q + self.core].astype(F32)
                self.mine[q] = (own + self.mine[q].astype(F32)).astype(BF)

                @pl.when((q > p) & (p == 0))
                def _():
                    self.rightward(q).start()

                @pl.when((q < p) & (p == n2 - 1))
                def _():
                    self.leftward(q).start()

        q_right = n2 - d

        @pl.when((p > 0) & (p < q_right))
        def _():
            self.rightward(q_right).wait_recv()
            self.add(q_right, q_right + 1)
            self.rightward(q_right).start()

        q_left = d - 1

        @pl.when((p < n2 - 1) & (p > q_left))
        def _():
            self.leftward(q_left).wait_recv()
            self.add(q_left, q_left)
            self.leftward(q_left).start()

    def finish(self):
        p, n2 = self.p, self.n2
        for q in range(n2):

            @pl.when(p == q)
            def _():
                total = self.mine[q].astype(F32)
                if q > 0:
                    self.rightward(q).wait_recv()
                    total += self.came[q + 1].astype(F32)
                if q < n2 - 1:
                    self.leftward(q).wait_recv()
                    total += self.came[q].astype(F32)
                self.o_ref[...] = total

        for q in range(n2):
            self.hand_over(q).wait_send()

            @pl.when(q > p)
            def _():
                self.rightward(q).wait_send()

            @pl.when(q < p)
            def _():
                self.leftward(q).wait_send()


def transfer_kernel(ops, axes, *refs):
    count = len(ops)
    rest = list(refs[2 * count :])
    for a, op in enumerate(ops):
        take = len(op.scratch)
        op.bind(refs[a], refs[count + a], *rest[:take])
        rest = rest[take:]
    barrier = pltpu.get_barrier_semaphore()
    for axis, size in axes:
        me = lax.axis_index(axis)
        for k in range(1, size):
            peer = {axis: lax.rem(me + k, size)}
            pl.semaphore_signal(barrier, inc=1, device_id=peer, device_id_type=MESH)
    pl.semaphore_wait(barrier, sum(size - 1 for _, size in axes))
    for op in ops:
        op.start()
    for d in range(1, 1 + max(op.steps for op in ops)):
        for op in ops:
            if d <= op.steps:
                op.step(d)
    for op in ops:
        op.finish()


def transfer(ops, axes, collective_id):
    spaces = [
        pl.BlockSpec(memory_space=pltpu.VMEM if hasattr(op, "vmem") else pl.ANY) for op in ops
    ]
    return pl.pallas_call(
        functools.partial(transfer_kernel, ops, axes),
        out_shape=[op.out for op in ops],
        in_specs=spaces,
        out_specs=spaces,
        scratch_shapes=[entry for op in ops for entry in op.scratch],
        compiler_params=pltpu.CompilerParams(
            collective_id=collective_id, has_side_effects=True, vmem_limit_bytes=48 << 20
        ),
    )(*[op.x for op in ops])


def meet(axes):
    barrier = pltpu.get_barrier_semaphore()
    for axis, size in axes:
        me = lax.axis_index(axis)
        for k in range(1, size):
            peer = {axis: lax.rem(me + k, size)}
            pl.semaphore_signal(barrier, inc=1, device_id=peer, device_id_type=MESH)
    pl.semaphore_wait(barrier, sum(size - 1 for _, size in axes))


def ffn_kernel(dims, slots, ops, *refs):
    S, F, R, seg, kb, rb, hb, hl, hp = dims
    v, t = unpack(slots, ops, refs[2:])
    stage_sem, cot_sem = refs[:2]
    own = R * seg
    width = v.n2_own.shape[1]
    tokens = S * own
    G = S // R
    gather, scatter = t.n2, t.d_n2
    early = [t.gu_a, t.down_b, t.ffn] if hasattr(t, FFN) else []
    n2, gw, gb, dw, cot_u, gu_a, down_b = v.n2, v.w, v.gb, v.w_down, v.cot_u, v.w_gu_a, v.down_b
    u_gu, act, d_gu, d_u_gu = v.u_gu, v.act, v.d_gu, v.d_u_gu
    meet([("seq", S), ("fsdp", F)])
    gather.start()

    def fetch(s):
        return pltpu.make_async_copy(v.gw.at[:, s], v.stage.at[s % 2], stage_sem.at[s % 2])

    fetch(0).start()
    moves = []
    for j in range(S):
        row, i = j // G, j % G
        for e in range(R):
            at = j * own + e * seg
            src = v.cot.at[i * R + e, row]
            dst = cot_u.at[pl.ds(at, seg), pl.ds(0, width)]
            moves.append(pltpu.make_async_copy(src, dst, cot_sem.at[len(moves)]))
            moves[-1].start()

    for s in range(S):
        if s + 1 < S:
            fetch(s + 1).start()
        fetch(s).wait()
        for f in range(F):
            b = s * F + f
            gw[b * kb : b * kb + kb, :] = v.stage[s % 2, f, 0:kb, :]
            gb[b * rb : b * rb + rb, :] = v.stage[s % 2, f, kb : kb + rb, :]
            gu_a[b * kb : b * kb + kb, :] = v.gu_a[s, f]
        if s == S // 2 and gather.steps >= 1:
            gather.step(1)
    for move in moves:
        move.wait()
    v.cot_own[...] = cot_u[pl.ds(pl.multiple_of(lax.axis_index("seq") * own, own), own), :width]
    tile = 2 * own
    tiles = tokens // tile

    @pl.loop(0, tiles)
    def _(k):
        rows = pl.ds(pl.multiple_of(k * tile, tile), tile)
        cot_u[rows, width:] = mm_nt(cot_u[rows, :width], down_b[...]).astype(BF)

    for f in range(F):
        dw[f * hb : f * hb + hb, :] = v.dw[f]
    if hp > hl:
        dw[hl:hp, :] = jnp.zeros((hp - hl, dw.shape[1]), BF)
    gather.own.wait()
    if gather.steps >= 2:
        gather.step(2)
    inner = math.sqrt(2.0 / math.pi)
    per_tile = 2

    def one_chip(k):
        rows = pl.ds(pl.multiple_of(k * tile, tile), tile)
        n = n2[pl.ds(k * per_tile, per_tile)].reshape(tile, width)
        u = mm(n, gu_a[...]).astype(BF)
        u_gu[rows, :] = u
        d_act = mm_nt(cot_u[rows, :], dw[...])
        gate = mm(n, gw[:, :hp]) + mm(u[:, :RANK], gb[:, :hp])
        up = mm(n, gw[:, hp:]) + mm(u[:, RANK:], gb[:, hp:])
        square = gate * gate
        th = jnp.tanh(inner * gate * (1.0 + 0.044715 * square))
        half = 0.5 * (1.0 + th)
        gelu = gate * half
        act[rows, :] = (gelu * up).astype(BF)
        slope = half + 0.5 * gate * (1.0 - th * th) * (inner * (1.0 + 3 * 0.044715 * square))
        d_gate = (d_act * up * slope).astype(BF)
        d_up = (d_act * gelu).astype(BF)
        d_gu[rows, :hp] = d_gate
        d_gu[rows, hp:] = d_up
        d_u_gu[rows, :RANK] = mm_nt(d_gate, gb[:, :hp]).astype(BF)
        d_u_gu[rows, RANK:] = mm_nt(d_up, gb[:, hp:]).astype(BF)
        out = mm_nt(d_gu[rows, :], gw[...]) + mm_nt(d_u_gu[rows, :], gu_a[...])
        v.dn[pl.ds(k * per_tile, per_tile)] = out.astype(BF).reshape(per_tile, own, width)

    @pl.loop(0, 2 * tiles - 1)
    def _(turn):
        for d in range(3, gather.steps + 1):

            @pl.when(turn == 2 * d - 3)
            def _():
                gather.step(d)

        away = (turn + 1) // 2
        k = jnp.where(lax.rem(turn, 2) == 1, gather.p - away, gather.p + away)

        @pl.when((k >= 0) & (k < tiles))
        def _():
            gather.from_core(k)
            one_chip(k)

    gather.settle()
    scatter.start()

    def gate_or_up(half, part, move):
        base = half * hp
        out = mm_tn(u_gu[:, half * RANK : half * RANK + RANK], d_gu[:, base : base + hp]).astype(BF)
        for b in range(S * F):
            part[b % F, b // F, kb : kb + rb, :] = out[b * rb : b * rb + rb, :]

        def columns(src, dst):
            out = mm_tn(n2[...].reshape(tokens, width), d_gu[:, src]).astype(BF)
            for b in range(S * F):
                part[b % F, b // F, 0:kb, dst] = out[b * kb : b * kb + kb, :]

        @pl.loop(0, hp // 256)
        def _(k):
            at = pl.multiple_of(k * 256, 128)
            columns(pl.ds(pl.multiple_of(base + at, 128), 256), pl.ds(at, 256))

        left = hp % 256
        if left:
            columns(slice(base + hp - left, base + hp), slice(hp - left, hp))
        move.start()

    gate_or_up(0, v.part_gate, t.gate)
    scatter.step(1)
    gate_or_up(1, v.part_up, t.up)
    if scatter.steps >= 2:
        scatter.step(2)

    @pl.loop(0, tiles)
    def _(k):
        rows = pl.ds(pl.multiple_of(k * tile, tile), tile)
        out = mm(act[rows, :], dw[...])
        low = out[:, width:].astype(BF)
        v.u_down[rows, :] = low
        out = out[:, :width] + mm(low, down_b[...])
        v.ffn_part[pl.ds(k * per_tile, per_tile)] = out.astype(BF).reshape(per_tile, own, width)

    for d in range(3, scatter.steps + 1):
        scatter.step(d)
    for op in early[2:]:
        op.start()
    scatter.finish()
    out = mm_tn(v.u_down[...], cot_u[:, :width]).astype(BF)
    for b in range(S * F):
        v.g_down_b[b // F, b % F] = out[b * rb : b * rb + rb, :]
    out = mm_tn(n2[...].reshape(tokens, width), d_u_gu[...]).astype(BF)
    for b in range(S * F):
        v.g_gu_a[b // F, b % F] = out[b * kb : b * kb + kb, :]
    for op in early[:2]:
        op.start()
    for op in early:
        op.step(1)
    step = 128

    @pl.loop(0, cot_u.shape[1] // step)
    def _(k):
        cols = pl.ds(pl.multiple_of(k * step, step), step)
        out = mm_tn(act[...], cot_u[:, cols]).astype(BF)
        for f in range(F):
            v.part_down[f, :, cols] = out[f * hb : f * hb + hb, :]

    def sum_up(move, came, put):
        def load(s):
            place = v.stage.at[s % 2].at[:, :, pl.ds(s // 2 % 2 * hp, hp)]
            return pltpu.make_async_copy(came.at[:, s], place, stage_sem.at[s % 4])

        move.finish()
        for s in range(3):
            load(s).start()
        for s in range(S):
            if s + 3 < S:
                load(s + 3).start()
            load(s).wait()
            cols = slice(s // 2 % 2 * hp, s // 2 % 2 * hp + hp)
            total = v.stage[s % 2, 0, :, cols].astype(F32)
            for f in range(1, F):
                total += v.stage[s % 2, f, :, cols].astype(F32)
            put[s] = total.astype(BF)

    for d in range(2, scatter.steps + 1):
        for op in early:
            op.step(d)
        if d == 2:
            sum_up(t.gate, v.came_gate, v.sum_gate)
    for op in early:
        op.finish()
    sum_up(t.up, v.came_up, v.sum_up)


def over_fsdp(ref, at, F):
    out = ref[(0,) + at].astype(F32)
    for f in range(1, F):
        out += ref[(f,) + at].astype(F32)
    return out


def feed_forward(given, dims, apart, collective_id):
    S, F, R, seg, kb, rb, hb, hl, hp = dims
    g = Bag(given)
    own, width = g.n2_own.shape
    tokens = S * own
    low = functools.partial(jax.ShapeDtypeStruct, dtype=BF)
    full = functools.partial(jax.ShapeDtypeStruct, dtype=F32)
    lora = width + RANK
    outs = dict(
        dn_sum=full((own, width)),
        cot_own=low((own, width)),
        part_down=low((F, hb, lora)),
        sum_gate=low((S, kb + rb, hp)),
        sum_up=low((S, kb + rb, hp)),
        came_gate=low((F, S, kb + rb, hp)),
        came_up=low((F, S, kb + rb, hp)),
    )
    scratch = dict(
        n2=low((S, own, width)),
        w=low((width, 2 * hp)),
        gb=low((RANK, 2 * hp)),
        w_down=low((hp, lora)),
        cot_u=low((tokens, lora)),
        w_gu_a=low((width, 2 * RANK)),
        u_gu=low((tokens, 2 * RANK)),
        act=low((tokens, hp)),
        d_gu=low((tokens, 2 * hp)),
        d_u_gu=low((tokens, 2 * RANK)),
        u_down=low((tokens, RANK)),
        dn=low((S, own, width)),
        stage=low((2, F, kb + rb, 2 * hp)),
        part_gate=low((F, S, kb + rb, hp)),
        part_up=low((F, S, kb + rb, hp)),
    )
    parts = dict(
        ffn_part=low((S, own, width)),
        g_gu_a=low((S, F, kb, 2 * RANK)),
        g_down_b=low((S, F, rb, width)),
    )
    if apart:
        outs.update(parts)
    else:
        scratch.update(parts)
        outs.update(
            ffn_sum=full((own, width)),
            f_gu_a=full((F, kb, 2 * RANK)),
            f_down_b=full((F, rb, width)),
        )
    slots = named(given, outs, scratch)
    a = Bag(slots)

    def op(kind, src, dst, *more):
        return kind(src, *more), src, dst

    ops = dict(
        n2=op(Line, a.n2_own, a.n2, S),
        d_n2=op(LineSum, a.dn, a.dn_sum, S),
        gate=op(Direct, a.part_gate, a.came_gate, "fsdp", F),
        up=op(Direct, a.part_up, a.came_up, "fsdp", F),
    )
    if not apart:
        ops.update(
            ffn=op(LineSum, a.ffn_part, a.ffn_sum, S),
            gu_a=op(LineSum, a.g_gu_a, a.f_gu_a, S),
            down_b=op(LineSum, a.g_down_b, a.f_down_b, S),
        )
    vmem = pl.BlockSpec(memory_space=pltpu.VMEM)
    away = pl.BlockSpec(memory_space=pl.ANY)
    far = [id(x) for x in (a.gw, a.cot, a.came_gate, a.came_up)]

    def kernel(*refs):
        count = len(slots)
        ffn_kernel(dims, slots, ops, *refs[count : count + 2], *refs[:count], *refs[count + 2 :])

    result = pl.pallas_call(
        kernel,
        out_shape=list(outs.values()),
        in_specs=[away if id(slots[name]) in far else vmem for name in given],
        out_specs=[away if id(slots[name]) in far else vmem for name in outs],
        scratch_shapes=[pltpu.VMEM(x.shape, x.dtype) for x in scratch.values()]
        + [pltpu.SemaphoreType.DMA((4,)), pltpu.SemaphoreType.DMA((S * R,))]
        + [entry for kind, _, _ in ops.values() for entry in kind.scratch],
        compiler_params=pltpu.CompilerParams(
            collective_id=collective_id, has_side_effects=True, vmem_limit_bytes=62 << 20
        ),
    )(*given.values())
    return Bag(zip(outs, result))


def front_kernel(dims, slots, ops, *refs):
    S, F, R, seg, kb, rb, ob = dims
    v, t = unpack(slots, ops, refs)
    own = R * seg
    L = S * seg
    G = S // R
    C = G // HEADS
    qlen = L // C
    width = v.x.shape[2]
    scale = HEAD**-0.5
    s = lax.axis_index("seq")
    r = s // G
    head = lax.rem(s, G) // C
    chunk = lax.rem(s, C)
    meet([("seq", S), ("fsdp", F)])

    n_qkv, n_a, n_q = v.w_qkv.shape[1], v.qkv_a.shape[1], v.q_b.shape[1]
    v.p1[:, :n_qkv] = v.w_qkv[...]
    v.p1[:, n_qkv : n_qkv + n_a] = v.qkv_a[...]
    v.p1[:, n_qkv + n_a :] = v.gain_pair[...]
    t.one.start()
    v.p2[:, :n_q] = v.q_b[...]
    v.p2[:, n_q : n_q + HEAD] = v.kv_b[0]
    v.p2[:, n_q + HEAD : n_q + 2 * HEAD] = v.kv_b[1]
    v.p2[:, n_q + 2 * HEAD :] = v.add_out_b[...]
    t.two.start()
    rows_in = [getattr(t, ROWS[j]) for j in range(R)]
    for op in rows_in:
        op.start()
    t.ids.start()
    first = [t.one, t.two, t.ids] + rows_in
    v.p3[:, :width] = v.w_out[...]
    v.p3[:, width:] = v.out_a[...]
    t.three.start()
    hidden = v.w_gu.shape[1] // 2
    hl = hidden // S
    hp = v.gws.shape[2] // 2
    for half in range(2):
        for j in range(S):
            at = half * hidden + j * hl
            v.gws[j, 0:kb, half * hp : half * hp + hl] = v.w_gu[:, at : at + hl]
            v.gws[j, kb:, half * hp : half * hp + hl] = v.gu_b[half, :, j * hl : j * hl + hl]
            if hp > hl:
                v.gws[j, :, half * hp + hl : half * hp + hp] = jnp.zeros((kb + rb, hp - hl), BF)
    t.gw.start()
    v.dws[:, :width] = v.w_down[...]
    v.dws[:, width:] = v.down_a[...]
    t.dw.start()
    later = [t.gu_a, t.down_b]
    for op in later:
        op.start()
    for d in range(1, t.one.steps + 1):
        for op in first:
            op.step(d)
    t.cot.start()
    t.three.finish()
    t.wo.start()
    t.ids.finish()

    for j in range(S):
        ids = jnp.where(r == 0, v.ids_all[j, 0:1, :], v.ids_all[j, 1:2, :])
        for row in range(2, R):
            ids = jnp.where(r == row, v.ids_all[j, row : row + 1, :], ids)
        v.id_row[:, j * seg : j * seg + seg] = ids.astype(F32)
    id_row = v.id_row[...]
    v.id_cols[...] = jnp.transpose(jnp.broadcast_to(id_row, (128, L)))
    lane = lax.broadcasted_iota(jnp.int32, (128, HEAD // 2), 1).astype(F32)
    spacing = jnp.exp(lane * (-2.0 / HEAD * math.log(ROPE_BASE)))
    places = lax.broadcasted_iota(jnp.int32, (128, L), 1)
    steps = lax.broadcasted_iota(jnp.int32, (128, L), 0)

    @pl.loop(0, L // 128)
    def _(i):
        rows = pl.ds(pl.multiple_of(i * 128, 128), 128)
        before = (v.id_cols[rows, 0:1] == id_row) & (places < steps + i * 128)
        position = jnp.sum(jnp.where(before, 1.0, 0.0), axis=1, keepdims=True)
        angle = position * spacing
        v.cosine[rows, :] = jnp.cos(angle)
        v.sine[rows, :] = jnp.sin(angle)

    for k in range(1, F):
        for op in (t.one, t.two):
            op.relay(k)
    for d in range(1, t.gu_a.steps + 1):
        for op in later:
            op.step(d)
    for op in (t.one, t.two):
        op.finish()
    for op in rows_in:
        op.finish()

    q_cols = pl.ds(pl.multiple_of(head * HEAD, HEAD), HEAD)
    rest_of = HEADS * HEAD
    wide = 2 * HEAD + 3 * RANK
    for j in range(S):
        for f in range(F):
            at = (j * F + f) * kb
            v.w1[at : at + kb, :HEAD] = v.p1_all[j, f, :, q_cols]
            v.w1[at : at + kb, HEAD:] = v.p1_all[j, f, :, rest_of : rest_of + wide]
            v.gain_cols[at : at + kb, :] = v.p1_all[j, f, :, rest_of + wide :].astype(F32)
            at = (j * F + f) * rb
            v.up_b[0, at : at + rb, :] = v.p2_all[j, f, :, q_cols]
            v.up_b[1, at : at + rb, :] = v.p2_all[j, f, :, rest_of : rest_of + HEAD]
            v.up_b[2, at : at + rb, :] = v.p2_all[j, f, :, rest_of + HEAD : rest_of + 2 * HEAD]
            v.out_b[at : at + rb, :] = v.p2_all[j, f, :, rest_of + 2 * HEAD :]
    v.gains[...] = jnp.transpose(v.gain_cols[...])[0:8, :]

    def norm(h, g):
        return (h * lax.rsqrt(jnp.mean(h * h, axis=-1, keepdims=True) + EPSILON) * g).astype(BF)

    for j in range(S):
        v.norm_one[j * seg : j * seg + seg, :] = norm(v.x_all[r, j].astype(F32), v.gains[0:1, :])
    mine = lax.rem(s, G) * R
    for e in range(R):
        v.x_own[e * seg : e * seg + seg, :] = v.x_all[r, mine + e]

    for k in range(1, F):
        for op in later:
            op.relay(k)
    half = HEAD // 2

    @pl.loop(0, L // 256)
    def _(i):
        rows = pl.ds(pl.multiple_of(i * 256, 256), 256)
        pu = mm(v.norm_one[rows, :], v.w1[...])
        u = pu[:, 3 * HEAD :].astype(BF)
        v.u[rows, :] = u
        cosine, sine = v.cosine[rows, :], v.sine[rows, :]
        for k, ref in ((0, v.q_all), (1, v.key)):
            out = pu[:, k * HEAD : (k + 1) * HEAD] + mm(u[:, k * RANK : (k + 1) * RANK], v.up_b[k])
            a, b = out[:, :half], out[:, half:]
            ref[rows, :half] = (a * cosine - b * sine).astype(BF)
            ref[rows, half:] = (b * cosine + a * sine).astype(BF)
        out = pu[:, 2 * HEAD : 3 * HEAD] + mm(u[:, 2 * RANK :], v.up_b[2])
        v.value[rows, :] = out.astype(BF)

    t.gw.finish()
    t.gw_all.start()
    t.cot.step(1)
    t.wo.finish()
    for j in range(S // HEADS):
        for f in range(F):
            at = (j * F + f) * ob
            v.wo[at : at + ob, :] = v.wo_in[j, f]
    from_row = pl.multiple_of(chunk * qlen, own)
    v.query[...] = v.q_all[pl.ds(from_row, qlen), :]
    if C > 1:
        v.part[...] = jnp.zeros(v.part.shape, BF)

    @pl.loop(0, qlen // 128)
    def _(i):
        rows = pl.ds(pl.multiple_of(i * 128, 128), 128)
        here = pl.multiple_of(from_row + i * 128, own)
        allowed = (v.id_cols[pl.ds(here, 128), 0:1] == id_row) & (places <= steps + here)
        scores = jnp.where(allowed, mm_nt(v.query[rows, :], v.key[...]) * scale, MASKED)
        top = jnp.max(scores, axis=-1, keepdims=True)
        lse = top + jnp.log(jnp.sum(jnp.exp(scores - top), axis=-1, keepdims=True))
        probs = jnp.where(allowed, jnp.exp(scores - lse), 0.0)
        v.probs[rows, :] = probs
        mixed = mm(probs.astype(BF), v.value[...]).astype(BF)
        v.mixed[rows, :] = mixed
        out = mm(mixed, v.wo[...]).astype(BF)
        v.part[pl.ds(here // own, 128 // own)] = out.reshape(128 // own, own, out.shape[1])

    t.attn.start()
    t.gw_all.relay()
    for d in range(1, t.attn.steps + 1):
        t.attn.step(d)
    t.attn.finish()
    u_out = v.attn[:, width:].astype(BF)
    v.u_out[...] = u_out
    resid = v.x_own[...].astype(F32) + v.attn[:, :width] + mm(u_out, v.out_b[...])
    v.resid[...] = resid
    v.n2_own[...] = norm(resid, v.gains[1:2, :])

    for d in range(2, t.cot.steps + 1):
        t.cot.step(d)
    for op in later + [t.cot, t.gw_all, t.dw]:
        op.finish()


def forward(given, dims, collective_id):
    S, F, R, seg, kb, rb, ob = dims
    own = R * seg
    L = S * seg
    G = S // R
    C = G // HEADS
    qlen = L // C
    width = given["x"].shape[2]
    per_head = S // HEADS
    lora = width + RANK
    low = functools.partial(jax.ShapeDtypeStruct, dtype=BF)
    full = functools.partial(jax.ShapeDtypeStruct, dtype=F32)

    g = Bag(given)
    wide = g.w_qkv.shape[1] + g.qkv_a.shape[1] + 128
    thin = g.q_b.shape[1] + 2 * HEAD + width
    hb = g.w_down.shape[0]
    hp = (g.w_gu.shape[1] // 2 // S + 127) // 128 * 128

    def like(array, *lead):
        return jax.ShapeDtypeStruct(lead + array.shape, array.dtype)

    outs = dict(
        w1=low((width, 3 * HEAD + 3 * RANK)),
        norm_one=low((L, width)),
        u=low((L, 3 * RANK)),
        query=low((qlen, HEAD)),
        key=low((L, HEAD)),
        value=low((L, HEAD)),
        cosine=full((L, HEAD // 2)),
        sine=full((L, HEAD // 2)),
        probs=full((qlen, L)),
        mixed=low((qlen, HEAD)),
        u_out=low((own, RANK)),
        resid=full((own, width)),
        n2_own=low((own, width)),
        x_own=low((own, width)),
        gains=full((8, width)),
        out_b=low((RANK, width)),
        wo=low((HEAD, lora)),
        up_b=low((3, RANK, HEAD)),
        gw_all=low((F, S, kb + rb, 2 * hp)),
        dw_all=low((F, hb, lora)),
        cot_all=like(g.cot, S),
        gu_a_all=like(g.gu_a, S, F),
        down_b_all=like(g.down_b, S, F),
        gw_mid=low((S, kb + rb, 2 * hp)),
    )
    scratch = dict(
        p1=low((kb, wide)),
        p2=low((rb, thin)),
        p3=low((ob, lora)),
        gws=low((S, kb + rb, 2 * hp)),
        dws=low((hb, lora)),
        p1_all=low((S, F, kb, wide)),
        p2_all=low((S, F, rb, thin)),
        x_all=low((R, S, seg, width)),
        ids_all=like(g.ids, S),
        p3_all=low((F, ob, lora)),
        wo_in=low((per_head, F, ob, lora)),
        id_row=full((1, L)),
        id_cols=full((L, 128)),
        gain_cols=full((width, 128)),
        q_all=low((L, HEAD)),
        part=low((G, own, lora)),
        attn=full((own, lora)),
    )
    slots = named(given, outs, scratch)
    a = Bag(slots)

    far = [id(x) for x in (a.gw_all, a.dw_all, a.cot_all, a.gu_a_all, a.down_b_all, a.gw_mid)]
    far += [id(x) for x in (a.x, a.ids, a.cot, a.gu_a, a.down_b)]

    def to_head(at):
        return [
            (None, row * G + at // per_head * C + c, lax.rem(at, per_head))
            for row in range(R)
            for c in range(C)
        ]

    def op(kind, src, dst, *more):
        return kind(src, *more), src, dst

    ops = dict(
        one=op(Grid, a.p1, a.p1_all, S, F),
        two=op(Grid, a.p2, a.p2_all, S, F),
        ids=op(Line, a.ids, a.ids_all, S),
        three=op(Direct, a.p3, a.p3_all, "fsdp", F, True),
        wo=op(Post, a.p3_all, a.wo_in, per_head, to_head),
        gw=op(Direct, a.gws, a.gw_mid, "seq", S),
        dw=op(Direct, a.dws, a.dw_all, "fsdp", F, True),
        gw_all=op(Square, a.gw_mid, a.gw_all, 0) if F == 4 else op(Direct, a.gw_mid, a.gw_all, "fsdp", F, True),
        cot=op(Line, a.cot, a.cot_all, S),
        gu_a=op(Grid, a.gu_a, a.gu_a_all, S, F),
        down_b=op(Grid, a.down_b, a.down_b_all, S, F),
        attn=op(LineSum, a.part, a.attn, G),
    )
    for j in range(R):
        span = (j * G // 2, (j + 1) * G // 2)
        ops[ROWS[j]] = Line(jax.ShapeDtypeStruct((seg, width), BF), S, span), (a.x, j), (a.x_all, j)
    vmem = pl.BlockSpec(memory_space=pltpu.VMEM)
    away = pl.BlockSpec(memory_space=pl.ANY)
    result = pl.pallas_call(
        functools.partial(front_kernel, dims, slots, ops),
        out_shape=list(outs.values()),
        in_specs=[away if id(slots[name]) in far else vmem for name in given],
        out_specs=[away if id(slots[name]) in far else vmem for name in outs],
        scratch_shapes=[pltpu.VMEM(a.shape, a.dtype) for a in scratch.values()]
        + [entry for kind, _, _ in ops.values() for entry in kind.scratch],
        compiler_params=pltpu.CompilerParams(
            collective_id=collective_id, has_side_effects=True, vmem_limit_bytes=62 << 20
        ),
    )(*given.values())
    return Bag(zip(outs, result))


def norm_back(G_in, h, g):
    q = lax.rsqrt(jnp.mean(h * h, axis=-1, keepdims=True) + EPSILON)
    gg = G_in * g
    d_gain = jnp.sum(G_in * (h * q), axis=0, keepdims=True)
    return d_gain, q * gg - h * (q * q * q) * jnp.mean(gg * h, axis=-1, keepdims=True)


def back_kernel(dims, slots, ops, *refs):
    S, F, R, seg, L, kb, rb, hb, ob = dims
    v, t = unpack(slots, ops, refs)
    own = R * seg
    G = S // R
    C = G // HEADS
    qlen = L // C
    width = v.resid.shape[1]
    scale = HEAD**-0.5
    s = lax.axis_index("seq")
    chunk = lax.rem(s, C)
    meet([("seq", S), ("fsdp", F)])
    t.down.start()

    gain_two, back = norm_back(v.d_n2[...], v.resid[...], v.gains[1:2, :])
    d_resid = v.cot_own[...].astype(F32) + back
    v.d_resid[...] = d_resid
    v.d_attn_own[...] = d_resid.astype(BF)
    t.d_attn.start()
    activations = (v.resid[...] + v.ffn_sum[...]).astype(BF)
    for j in range(R):
        v.act_rows[j] = activations[j * seg : j * seg + seg, :]
    t.activations.start()
    for put, got, home in ((v.s_gu_a, v.f_gu_a, t.gu_a_home), (v.s_down_b, v.f_down_b, t.down_b_home)):
        put[...] = got[...].astype(BF)
        home.start()
    t.gate_home.start()
    t.up_home.start()
    for d in range(1, t.d_attn.steps + 1):
        t.d_attn.step(d)
    t.d_attn.finish()

    blocks = qlen // own
    first = chunk * blocks
    v.da[:, :width] = v.d_attn[pl.ds(first, blocks)].reshape(qlen, width)
    v.da[:, width:] = mm_nt(v.da[:, :width], v.out_b[...]).astype(BF)
    v.d_mixed[...] = mm_nt(v.da[...], v.wo[...]).astype(BF)

    @pl.loop(0, qlen // 128)
    def _(i):
        rows = pl.ds(pl.multiple_of(i * 128, 128), 128)
        p = v.probs[rows, :]
        d_probs = mm_nt(v.d_mixed[rows, :], v.value[...])
        delta = jnp.sum(p * d_probs, axis=-1, keepdims=True)
        v.d_scores[rows, :] = (p * (d_probs - delta)).astype(BF)
        v.probs_low[rows, :] = p.astype(BF)

    def unrot(g, rows):
        half = HEAD // 2
        cosine, sine = v.cosine[rows, :], v.sine[rows, :]
        a, b = g[:, :half], g[:, half:]
        return (a * cosine + b * sine).astype(BF), (b * cosine - a * sine).astype(BF)

    half = HEAD // 2
    mine = pl.ds(pl.multiple_of(chunk * qlen, own), qlen)
    if C > 1:
        v.d_pu[:, :HEAD] = jnp.zeros((L, HEAD), BF)
    v.d_pu[mine, :half], v.d_pu[mine, half:HEAD] = unrot(mm(v.d_scores[...], v.key[...]) * scale, mine)
    every = pl.ds(0, L)
    v.d_pu[:, HEAD : HEAD + half], v.d_pu[:, HEAD + half : 2 * HEAD] = unrot(
        mm_tn(v.d_scores[...], v.query[...]) * scale, every
    )
    v.d_pu[:, 2 * HEAD : 3 * HEAD] = mm_tn(v.probs_low[...], v.d_mixed[...]).astype(BF)
    for k in range(3):
        v.d_pu[:, 3 * HEAD + k * RANK : 3 * HEAD + (k + 1) * RANK] = mm_nt(
            v.d_pu[:, k * HEAD : (k + 1) * HEAD], v.up_b[k]
        ).astype(BF)

    @pl.loop(0, L // 256)
    def _(i):
        rows = pl.ds(pl.multiple_of(i * 256, 256), 256)
        out = mm_nt(v.d_pu[rows, :], v.w1[...]).astype(BF)
        v.d_attn[pl.ds(i * (256 // own), 256 // own)] = out.reshape(256 // own, own, width)

    t.d_n1.start()

    out = mm_tn(v.mixed[...], v.da[...]).astype(BF)
    for j in range(HEAD // ob):
        v.t_out[j % F, j // F] = out[j * ob : j * ob + ob, :]
    t.out.start()
    out = mm_tn(v.norm_one[...], v.d_pu[:, :HEAD]).astype(BF)
    for b in range(S * F):
        v.t_q[b % F, b // F] = out[b * kb : b * kb + kb, :]
    t.q.start()
    out = mm_tn(v.u[:, :RANK], v.d_pu[:, :HEAD]).astype(BF)
    for b in range(S * F):
        v.t_qb[b % F, b // F] = out[b * rb : b * rb + rb, :]
    t.qb.start()
    t.d_n1.step(1)

    @pl.loop(0, v.t_1.shape[3] // 256)
    def _(i):
        cols = pl.ds(pl.multiple_of(i * 256, 256), 256)
        src = pl.ds(pl.multiple_of(i * 256 + 256, 256), 256)
        out = mm_tn(v.norm_one[...], v.d_pu[:, src]).astype(BF)
        for b in range(S * F):
            v.t_1[b // F, b % F, :, cols] = out[b * kb : b * kb + kb, :]

    t.one.start()
    for d in range(2, t.d_n1.steps + 1):
        t.d_n1.step(d)
    for k in range(2):
        out = mm_tn(
            v.u[:, (k + 1) * RANK : (k + 2) * RANK], v.d_pu[:, (k + 1) * HEAD : (k + 2) * HEAD]
        ).astype(BF)
        for b in range(S * F):
            v.t_2[b // F, b % F, :, k * HEAD : (k + 1) * HEAD] = out[b * rb : b * rb + rb, :]
    out = mm_tn(v.u_out[...], v.d_attn_own[...]).astype(BF)
    for b in range(S * F):
        v.t_2[b // F, b % F, :, 2 * HEAD :] = out[b * rb : b * rb + rb, :]
    t.two.start()

    t.d_n1.finish()
    gain_one, back = norm_back(v.d_n1_sum[...], v.x_own[...].astype(F32), v.gains[0:1, :])
    grad_input = v.d_resid[...] + back
    for j in range(R):
        v.grad_rows[j] = grad_input[j * seg : j * seg + seg, :]
    t.grad_input.start()
    both = jnp.concatenate([gain_one, gain_two, jnp.zeros((126, width), F32)], axis=0)
    both = jnp.transpose(both)
    for b in range(S * F):
        v.t_3[b // F, b % F] = both[b * kb : b * kb + kb, :].astype(BF)
    t.three.start()
    late = [t.one, t.two, t.three]
    for op in late:
        op.step(1)
    for move, got, put, home in (
        (t.q, v.r_q, v.s_q, t.q_home),
        (t.qb, v.r_qb, v.s_qb, t.qb_home),
        (t.out, v.r_out, v.s_out, t.out_home),
    ):
        move.finish()
        for k in range(put.shape[0]):
            put[k] = over_fsdp(got, (k,), F).astype(BF)
        home.start()
    for d in range(2, t.one.steps + 1):
        for op in late:
            op.step(d)
    for op in late:
        op.finish()
    for put, got, home in (
        (v.s_one, v.f_one, t.one_home),
        (v.s_two, v.f_two, t.two_home),
        (v.s_three, v.f_three, t.three_home),
    ):
        put[...] = got[...].astype(BF)
        home.start()
    homes = [t.one_home, t.two_home, t.three_home, t.gu_a_home, t.down_b_home]
    homes += [t.gate_home, t.up_home, t.down]
    for move in [t.grad_input, t.activations, t.q_home, t.qb_home, t.out_home] + homes:
        move.finish()


def backward(given, dims, collective_id):
    S, F, R, seg, L, kb, rb, hb, ob = dims
    own = R * seg
    G = S // R
    C = G // HEADS
    qlen = L // C
    width = given["resid"].shape[1]
    per_head = S // HEADS
    hp = given["sum_up"].shape[2]
    lora = width + RANK
    one = 2 * HEAD + 3 * RANK
    two = 2 * HEAD + width
    low = functools.partial(jax.ShapeDtypeStruct, dtype=BF)
    full = functools.partial(jax.ShapeDtypeStruct, dtype=F32)

    def to_rows(at):
        return [(j, lax.rem(at, G) * R + j, at // G) for j in range(R)]

    def to_out(at):
        return [
            (j, lax.rem(at, G) // C * per_head + j, at // G * C + lax.rem(at, C)) for j in range(per_head)
        ]

    outs = dict(
        act_home=low((R, seg, width)),
        grad_home=full((R, seg, width)),
        o_q=low((S, kb, HEAD)),
        o_qb=low((S, rb, HEAD)),
        o_out=low((R * C, ob, lora)),
        o_gate=low((S, kb + rb, hp)),
        o_up=low((S, kb + rb, hp)),
        o_down=low((F, hb, lora)),
        o_one=low((F, kb, one)),
        o_two=low((F, rb, two)),
        o_three=low((F, kb, 128)),
        o_gu_a=low((F, kb, 2 * RANK)),
        o_down_b=low((F, rb, width)),
    )
    scratch = dict(
        d_resid=full((own, width)),
        d_attn_own=low((own, width)),
        d_attn=low((G, own, width)),
        da=low((qlen, lora)),
        d_mixed=low((qlen, HEAD)),
        d_scores=low((qlen, L)),
        probs_low=low((qlen, L)),
        d_pu=low((L, 3 * HEAD + 3 * RANK)),
        d_n1_sum=full((own, width)),
        grad_rows=full((R, seg, width)),
        act_rows=low((R, seg, width)),
        t_out=low((F, per_head, ob, lora)),
        t_q=low((F, S, kb, HEAD)),
        t_qb=low((F, S, rb, HEAD)),
        t_1=low((S, F, kb, one)),
        t_2=low((S, F, rb, two)),
        t_3=low((S, F, kb, 128)),
        r_out=low((F, per_head, ob, lora)),
        r_q=low((F, S, kb, HEAD)),
        r_qb=low((F, S, rb, HEAD)),
        s_out=low((per_head, ob, lora)),
        s_q=low((S, kb, HEAD)),
        s_qb=low((S, rb, HEAD)),
    )
    scratch.update(
        f_one=full((F, kb, one)),
        s_one=low((F, kb, one)),
        f_two=full((F, rb, two)),
        s_two=low((F, rb, two)),
        f_three=full((F, kb, 128)),
        s_three=low((F, kb, 128)),
        s_gu_a=low((F, kb, 2 * RANK)),
        s_down_b=low((F, rb, width)),
    )
    slots = named(given, outs, scratch)
    a = Bag(slots)

    def op(kind, src, dst, *more):
        return kind(src, *more), src, dst

    ops = dict(
        down=op(Direct, a.part_down, a.o_down, "fsdp", F),
        d_attn=op(Line, a.d_attn_own, a.d_attn, G),
        d_n1=op(LineSum, a.d_attn, a.d_n1_sum, G),
        out=op(Direct, a.t_out, a.r_out, "fsdp", F),
        q=op(Direct, a.t_q, a.r_q, "fsdp", F),
        qb=op(Direct, a.t_qb, a.r_qb, "fsdp", F),
        one=op(LineSum, a.t_1, a.f_one, S),
        two=op(LineSum, a.t_2, a.f_two, S),
        three=op(LineSum, a.t_3, a.f_three, S),
        grad_input=op(Post, a.grad_rows, a.grad_home, R, to_rows),
        activations=op(Post, a.act_rows, a.act_home, R, to_rows),
        q_home=op(Direct, a.s_q, a.o_q, "seq", S),
        qb_home=op(Direct, a.s_qb, a.o_qb, "seq", S),
        out_home=op(Post, a.s_out, a.o_out, R * C, to_out),
        gate_home=op(Direct, a.sum_gate, a.o_gate, "seq", S),
        up_home=op(Direct, a.sum_up, a.o_up, "seq", S),
    )
    ops.update(
        one_home=op(Direct, a.s_one, a.o_one, "fsdp", F),
        two_home=op(Direct, a.s_two, a.o_two, "fsdp", F),
        three_home=op(Direct, a.s_three, a.o_three, "fsdp", F),
        gu_a_home=op(Direct, a.s_gu_a, a.o_gu_a, "fsdp", F),
        down_b_home=op(Direct, a.s_down_b, a.o_down_b, "fsdp", F),
    )
    far = [id(x) for x in (a.part_down, a.sum_gate, a.sum_up)]
    vmem = pl.BlockSpec(memory_space=pltpu.VMEM)
    away = pl.BlockSpec(memory_space=pl.ANY)
    result = pl.pallas_call(
        functools.partial(back_kernel, dims, slots, ops),
        out_shape=list(outs.values()),
        in_specs=[away if id(slots[name]) in far else vmem for name in given],
        out_specs=[away] * len(outs),
        scratch_shapes=[pltpu.VMEM(a.shape, a.dtype) for a in scratch.values()]
        + [entry for kind, _, _ in ops.values() for entry in kind.scratch],
        compiler_params=pltpu.CompilerParams(
            collective_id=collective_id, has_side_effects=True, vmem_limit_bytes=62 << 20
        ),
    )(*given.values())
    return Bag(zip(outs, result))


def finish_kernel(dims, slots, *refs):
    S, F, R, kb, rb, hb, ob, hidden, hl, width = dims
    buffers, sem = refs[len(slots) : -1], refs[-1]
    copies = [pltpu.make_async_copy(refs[k], buffers[k], sem.at[k]) for k in range(len(buffers))]
    for copy in copies:
        copy.start()
    for copy in copies:
        copy.wait()
    v = Bag(zip(slots, buffers + refs[len(buffers) : len(slots)]))
    G = S // R
    C = G // HEADS
    v.activations[...] = v.act_home[...]
    v.grad_input[...] = v.grad_home[...]

    def of_head(ref, head):
        parts = [ref[row * G + head * C + c].astype(F32) for row in range(R) for c in range(C)]
        return sum(parts[1:], parts[0])

    for head in range(HEADS):
        cols = slice(head * HEAD, head * HEAD + HEAD)
        v.w_qkv[:, cols] = of_head(v.o_q, head)
        v.q_b[:, cols] = of_head(v.o_qb, head)
    out = over_fsdp(v.o_one, (), F)
    v.w_qkv[:, HEADS * HEAD :] = out[:, : 2 * HEAD]
    v.qkv_a[...] = out[:, 2 * HEAD :]
    out = over_fsdp(v.o_two, (), F)
    v.kv_b[0] = out[:, :HEAD]
    v.kv_b[1] = out[:, HEAD : 2 * HEAD]
    v.out_b[...] = out[:, 2 * HEAD :]
    v.gains[...] = over_fsdp(v.o_three, (), F)
    v.gu_a[...] = over_fsdp(v.o_gu_a, (), F)
    v.down_b[...] = over_fsdp(v.o_down_b, (), F)
    out = over_fsdp(v.o_down, (), F)
    v.w_down[...] = out[:, :width]
    v.down_a[...] = out[:, width:]
    out = over_fsdp(v.o_out, (), R * C)
    v.w_out[...] = out[:, :width]
    v.out_a[...] = out[:, width:]
    for half, ref in ((0, v.o_gate), (1, v.o_up)):
        for j in range(S):
            at = half * hidden + j * hl
            v.w_gu[:, at : at + hl] = ref[j, 0:kb, :hl].astype(F32)
            v.gu_b[half, :, j * hl : j * hl + hl] = ref[j, kb:, :hl].astype(F32)


def finish(got, dims):
    S, F, R, kb, rb, hb, ob, hidden, hl, width = dims
    full = functools.partial(jax.ShapeDtypeStruct, dtype=F32)
    given = vars(got)
    outs = dict(
        activations=got.act_home,
        grad_input=got.grad_home,
        w_qkv=full((kb, (HEADS + 2) * HEAD)),
        qkv_a=full((kb, 3 * RANK)),
        q_b=full((rb, HEADS * HEAD)),
        kv_b=full((2, rb, HEAD)),
        w_out=full((ob, width)),
        out_a=full((ob, RANK)),
        out_b=full((rb, width)),
        w_gu=full((kb, 2 * hidden)),
        gu_a=full((kb, 2 * RANK)),
        gu_b=full((2, rb, hidden)),
        w_down=full((hb, width)),
        down_a=full((hb, RANK)),
        down_b=full((rb, width)),
        gains=full((kb, 128)),
    )
    slots = named(given, outs)
    vmem = pl.BlockSpec(memory_space=pltpu.VMEM)
    result = pl.pallas_call(
        functools.partial(finish_kernel, dims, slots),
        out_shape=[jax.ShapeDtypeStruct(x.shape, x.dtype) for x in outs.values()],
        in_specs=[pl.BlockSpec(memory_space=pl.ANY)] * len(given),
        out_specs=[vmem] * len(outs),
        scratch_shapes=[pltpu.VMEM(x.shape, x.dtype) for x in given.values()]
        + [pltpu.SemaphoreType.DMA((len(given),))],
        compiler_params=pltpu.CompilerParams(vmem_limit_bytes=62 << 20),
    )(*given.values())
    return Bag(zip(outs, result))


def shards(
    S,
    F,
    layer_input,
    document_numbers,
    cotangent,
    w_qkv,
    qkv_a,
    q_b,
    kv_b,
    w_out,
    out_a,
    out_b,
    w_gu,
    gu_a,
    gu_b,
    w_down,
    down_a,
    down_b,
    gain_a,
    gain_f,
):
    R, seg, width = layer_input.shape
    L = seg * S
    own = R * seg
    G = S // R
    C = G // HEADS
    scale = HEAD**-0.5
    kb = w_qkv.shape[0]
    rb = q_b.shape[0]
    hb = w_down.shape[0]
    ob = w_out.shape[0]
    hidden = w_gu.shape[1] // 2
    hl = hidden // S
    hp = (hl + 127) // 128 * 128
    s = lax.axis_index("seq")
    r = s // G
    head = lax.rem(s, G) // C
    chunk = lax.rem(s, C)
    qlen = L // C

    on_seq = ("seq", S)
    h = forward(
        dict(
            x=layer_input,
            ids=document_numbers,
            cot=cotangent,
            w_qkv=w_qkv,
            qkv_a=qkv_a,
            gain_pair=jnp.pad(jnp.stack([gain_a, gain_f], axis=1), ((0, 0), (0, 126))),
            q_b=q_b,
            kv_b=kv_b,
            add_out_b=out_b,
            w_out=w_out,
            out_a=out_a,
            w_gu=w_gu,
            gu_b=gu_b,
            w_down=w_down,
            down_a=down_a,
            gu_a=gu_a,
            down_b=down_b,
        ),
        (S, F, R, seg, kb, rb, ob),
        0,
    )
    cot = h.cot_all

    dims = (S, F, R, seg, kb, rb, hb, hl, hp)
    apart = S * own > 1024
    ffn = feed_forward(
        dict(
            n2_own=h.n2_own,
            gw=h.gw_all,
            dw=h.dw_all,
            cot=cot,
            gu_a=h.gu_a_all,
            down_b=h.down_b_all.reshape(RANK, width),
        ),
        dims,
        apart,
        5,
    )
    if apart:
        ffn.ffn_sum, ffn.f_gu_a, ffn.f_down_b = transfer(
            [LineSum(x, S) for x in (ffn.ffn_part, ffn.g_gu_a, ffn.g_down_b)], [on_seq], 7
        )
    got = backward(
        dict(
            d_n2=ffn.dn_sum,
            cot_own=ffn.cot_own,
            resid=h.resid,
            gains=h.gains,
            x_own=h.x_own,
            out_b=h.out_b,
            wo=h.wo,
            w1=h.w1,
            up_b=h.up_b,
            norm_one=h.norm_one,
            u=h.u,
            u_out=h.u_out,
            query=h.query,
            key=h.key,
            value=h.value,
            cosine=h.cosine,
            sine=h.sine,
            probs=h.probs,
            mixed=h.mixed,
            ffn_sum=ffn.ffn_sum,
            f_gu_a=ffn.f_gu_a,
            f_down_b=ffn.f_down_b,
            part_down=ffn.part_down,
            sum_gate=ffn.sum_gate,
            sum_up=ffn.sum_up,
        ),
        (S, F, R, seg, L, kb, rb, hb, ob),
        8,
    )

    done = finish(got, (S, F, R, kb, rb, hb, ob, hidden, hl, width))
    return (
        done.activations,
        done.grad_input,
        done.w_qkv,
        done.qkv_a,
        done.q_b,
        done.kv_b,
        done.w_out,
        done.out_a,
        done.out_b,
        done.w_gu,
        done.gu_a,
        done.gu_b,
        done.w_down,
        done.down_a,
        done.down_b,
        done.gains[:, 0],
        done.gains[:, 1],
    )


def solution(mesh):
    both = P(("seq", "fsdp"), None)
    second = P(None, ("seq", "fsdp"), None)
    tokens = P("fsdp", "seq", None)
    gain = P(("seq", "fsdp"))
    return jax.shard_map(
        functools.partial(shards, mesh.shape["seq"], mesh.shape["fsdp"]),
        mesh=mesh,
        in_specs=(tokens, P("fsdp", "seq"), tokens)
        + (both, both, both, second, both, both, both, both, both, second, both, both, both, gain, gain),
        out_specs=(tokens, tokens)
        + (both, both, both, second, both, both, both, both, both, second, both, both, both, gain, gain),
        check_vma=False,
    )
```
